256 devices in a mesh: cam: 32 (over z, y), pt: 8 (over x, core).
Axes of the slice: x: 4, y: 4, z: 8, core: 2. Of those that a mesh axis runs over, the one named last changes fastest.
Arguments:
- jacobian_cam: float32 [4, 18, 131072], P(None, None, ('cam', 'pt')), may hold values from -2 to 2
- jacobian_pt: float32 [4, 6, 131072], P(None, None, ('cam', 'pt'))
- residuals: float32 [4, 2, 131072], P(None, None, ('cam', 'pt')), may hold values from -8 to 8
- point_inverse: float32 [9, 131072], P(None, ('cam', 'pt')), as said below
- obs_camera: int32 [4, 131072], P(None, ('cam', 'pt')), may hold values from 0 to 32767, as said below
- pair_slot: int32 [4, 4, 131072], P(None, None, ('cam', 'pt')), may hold values from 0 to 12, as said below
- observation_used: int32 [4, 131072], P(None, ('cam', 'pt')), may hold values from 0 to 1, as said below
- pattern: int32 [12, 32768], P(None, ('cam', 'pt')), may hold values from 0 to 32767, as said below
Outputs:
- camera_step: float32 [9, 32768], P(None, ('cam', 'pt'))
- cam_residual: float32 [9, 32768], P(None, ('cam', 'pt'))
- point_step: float32 [3, 131072], P(None, ('cam', 'pt'))
The draws below stay inside these ranges and needn't reach their ends.
Inputs may be any that keep to these rules, and one draw needn't show every extreme that they name: `obs_camera`: the 4 cameras of a point are distinct and lie within 12 places of one another in the order behind pattern. `pair_slot`: entry [a, b, j] is the place k with pattern[k, obs_camera[a, j]] = obs_camera[b, j], and 12 where a equals b. `observation_used`: among the live observations of the points of one device, at most 16 name cameras of one device's share; some pair of devices reaches it. `pattern`: column i lists 12 distinct cameras other than i; camera i is coupled to j exactly when j is coupled to i. `point_inverse`: the inverse of the identity plus the sum over the point's live observations of Jp^T Jp.
All inputs are finite; a program needn't handle non-finite values.
Results may differ from the reference program's by a relative error of at most 0.0003.
Values sent between devices are 32-bit elements; how exact they have to be, the bound alone decides.
No kernel may reach another device: no remote copies, remote signals or barrier semaphores. Data moves between devices by JAX's collectives and lax.ppermute only.
A program may use at most 128 MiB of HBM per device.

```python
import jax
import jax.numpy as jnp
from jax import lax

CP = 9
TRACK = 4
HALF = 6
NBR = 12
ITERS = 4
CAM_DEV = 128
PTS_DEV = 512
CAMS = 32768
POINTS = 131072
OBS_CAP = 16
DEVICES = 256


def camera_visibility(key):
    key = jax.random.fold_in(key, 101)
    key_perm, key_hot, key_home, key_free, key_steps = jax.random.split(key, 5)
    order_cams = jax.random.permutation(key_perm, CAMS).astype(jnp.int32)
    place = jnp.zeros((CAMS,), jnp.int32).at[order_cams].set(jnp.arange(CAMS, dtype=jnp.int32))
    hot_device = jax.random.randint(key_hot, (DEVICES, 1), 0, DEVICES)
    forced_cam = hot_device * CAM_DEV + jax.random.randint(key_home, (DEVICES, PTS_DEV), 0, CAM_DEV)
    free_cam = jax.random.randint(key_free, (DEVICES, PTS_DEV), 0, CAMS)
    anchor_cam = jnp.where(jnp.arange(PTS_DEV)[None, :] < OBS_CAP, forced_cam, free_cam).astype(jnp.int32)
    strides = jax.random.randint(key_steps, (TRACK - 1, DEVICES, PTS_DEV), 1, HALF // (TRACK - 1) + 1)
    offsets = jnp.concatenate([jnp.zeros((1, DEVICES, PTS_DEV), jnp.int32), jnp.cumsum(strides, axis=0).astype(jnp.int32)], axis=0)
    cameras = order_cams[(place[anchor_cam][None, :, :] + offsets) % CAMS]
    shifts = jnp.arange(NBR, dtype=jnp.int32)
    shifts = jnp.where(shifts < HALF, shifts - HALF, shifts - HALF + 1)
    neighbors = order_cams[(place[:, None] + shifts[None, :]) % CAMS].T
    gaps = offsets[None, :, :, :] - offsets[:, None, :, :]
    slots = jnp.where(gaps < 0, gaps + HALF, jnp.where(gaps > 0, gaps + HALF - 1, NBR)).astype(jnp.int32)
    owners = cameras // CAM_DEV
    flat = jnp.transpose(owners, (1, 0, 2)).reshape(DEVICES, TRACK * PTS_DEV)
    total = TRACK * PTS_DEV

    def ranks(keyed):
        order = jnp.argsort(keyed * total + jnp.arange(total, dtype=jnp.int32))
        sorted_keys = keyed[order]
        starts = jnp.searchsorted(sorted_keys, sorted_keys, side='left').astype(jnp.int32)
        return jnp.zeros((total,), jnp.int32).at[order].set(jnp.arange(total, dtype=jnp.int32) - starts)
    rank = jnp.transpose(jax.vmap(ranks)(flat).reshape(DEVICES, TRACK, PTS_DEV), (1, 0, 2))
    live = (rank < OBS_CAP).astype(jnp.int32)
    return (cameras.reshape(TRACK, POINTS), slots.reshape(TRACK, TRACK, POINTS), live.reshape(TRACK, POINTS), neighbors)


def point_jacobian(key):
    return jax.random.normal(jax.random.fold_in(key, 202), (TRACK, 6, POINTS), jnp.float32)


def draw_obs_camera(key, part):
    return camera_visibility(key)[0]


def draw_pair_slot(key, part):
    return camera_visibility(key)[1]


def draw_observation_used(key, part):
    return camera_visibility(key)[2]


def draw_pattern(key, part):
    return camera_visibility(key)[3]


def draw_jacobian_pt(key, part):
    return point_jacobian(key)


def draw_point_inverse(key, part):
    values = point_jacobian(key).reshape(TRACK, 2, 3, POINTS)
    observation_active = camera_visibility(key)[2].astype(jnp.float32)
    gram_matrix = jnp.sum(values[:, :, :, None, :] * values[:, :, None, :, :], axis=1)
    gram_matrix = jnp.sum(gram_matrix * observation_active[:, None, None, :], axis=0) + jnp.eye(3, dtype=jnp.float32)[:, :, None]
    aval, bval, cval = (gram_matrix[0, 0], gram_matrix[0, 1], gram_matrix[0, 2])
    dval, eval_, fval = (gram_matrix[1, 1], gram_matrix[1, 2], gram_matrix[2, 2])
    first_minor = dval * fval - eval_ * eval_
    second_minor = cval * eval_ - bval * fval
    third_minor = bval * eval_ - cval * dval
    determinant = aval * first_minor + bval * second_minor + cval * third_minor
    mid_one = aval * fval - cval * cval
    mid_two = bval * cval - aval * eval_
    last_one = aval * dval - bval * bval
    stacked = jnp.stack([first_minor, second_minor, third_minor, second_minor, mid_one, mid_two, third_minor, mid_two, last_one])
    return stacked / determinant[None, :]


def level_of(stream_key, extent, pieces, smallest, largest):
    gain = 1.0
    for position, parts in pieces:
        draws = jax.random.uniform(jax.random.fold_in(jax.random.fold_in(stream_key, 6), position), (parts,), jnp.float32, smallest / len(pieces), largest / len(pieces))
        gain = gain * jnp.repeat(jnp.exp(draws), extent[position] // parts).reshape((-1,) + (1,) * (len(extent) - 1 - position))
    return gain


def scatter_about(key, dims, spread, limit, shards=(), held_as=jnp.bfloat16):
    loudness = level_of(key, dims, shards, -0.22, 0.18) if shards else 1.0
    values = jax.random.normal(key, dims, jnp.float32) * spread * loudness
    return jnp.minimum(jnp.maximum(values, -limit), limit).astype(held_as)


def setup_inputs(seed: int = 0) -> dict:
    seeds = jax.random.split(jax.random.key(seed), 9)
    jacobian_cam = scatter_about(seeds[0], (TRACK, 2 * CP, POINTS), 0.25, 2.0, ((2, 256),), jnp.float32)
    jacobian_pt = draw_jacobian_pt(jax.random.fold_in(seeds[8], 71), 0)
    residuals = scatter_about(seeds[2], (TRACK, 2, POINTS), 1.0, 8.0, ((2, 256),), jnp.float32)
    point_inverse = draw_point_inverse(jax.random.fold_in(seeds[8], 71), 0)
    obs_camera = draw_obs_camera(jax.random.fold_in(seeds[8], 71), 0)
    pair_slot = draw_pair_slot(jax.random.fold_in(seeds[8], 71), 0)
    observation_used = draw_observation_used(jax.random.fold_in(seeds[8], 71), 0)
    pattern = draw_pattern(jax.random.fold_in(seeds[8], 71), 0)
    return {"jacobian_cam": jacobian_cam, "jacobian_pt": jacobian_pt, "residuals": residuals, "point_inverse": point_inverse, "obs_camera": obs_camera, "pair_slot": pair_slot, "observation_used": observation_used, "pattern": pattern}


DAMPING = 1.0

def point_terms(jacobian_cam, jacobian_pt, residuals, point_inverse, observation_used):
    npts = jacobian_cam.shape[-1]
    observation_active = observation_used.astype(jnp.float32)
    camera_jacobian_rows = jacobian_cam.reshape(TRACK, 2, 9, npts)
    point_jacobian_rows = jacobian_pt.reshape(TRACK, 2, 3, npts)
    inverse_blocks = point_inverse.reshape(3, 3, npts)
    camera_point_coupling = lax.optimization_barrier(jnp.sum(camera_jacobian_rows[:, :, :, None, :] * point_jacobian_rows[:, :, None, :, :], axis=1)) * observation_active[:, None, None, :]
    points_removed = lax.optimization_barrier(jnp.sum(camera_point_coupling[:, :, :, None, :] * inverse_blocks[None, None, :, :, :], axis=2))
    point_gradient = -lax.optimization_barrier(jnp.sum(observation_active[:, None, :] * lax.optimization_barrier(jnp.sum(point_jacobian_rows * residuals[:, :, None, :], axis=1)), axis=0))
    camera_gradient = -observation_active[:, None, :] * lax.optimization_barrier(jnp.sum(camera_jacobian_rows * residuals[:, :, None, :], axis=1))
    return (camera_jacobian_rows, camera_point_coupling, points_removed, point_gradient, camera_gradient, observation_active, inverse_blocks)

def pair_block(square_root, partner, normal_terms):
    camera_jacobian_rows, camera_point_coupling, points_removed, point_gradient, camera_gradient, observation_active, inverse_blocks = normal_terms
    npts = camera_jacobian_rows.shape[-1]
    cross = -lax.optimization_barrier(jnp.sum(points_removed[square_root][:, None, :, :] * camera_point_coupling[partner][None, :, :, :], axis=2))
    if square_root == partner:
        gram_matrix = lax.optimization_barrier(jnp.sum(camera_jacobian_rows[square_root][:, :, None, :] * camera_jacobian_rows[square_root][:, None, :, :], axis=0)) * observation_active[square_root]
        block = gram_matrix + cross
        right = camera_gradient[square_root] - lax.optimization_barrier(jnp.sum(points_removed[square_root] * point_gradient[None, :, :], axis=1))
    else:
        block = cross
        right = jnp.zeros((9, npts), jnp.float32)
    return jnp.concatenate([block.reshape(81, npts), right], axis=0)

def factor_blocks(matrix):
    lower = {}
    for row_idx in range(9):
        for col_idx in range(row_idx + 1):
            accum = matrix[row_idx, col_idx]
            for inner_idx in range(col_idx):
                accum = accum - lower[row_idx, inner_idx] * lower[col_idx, inner_idx]
            if row_idx == col_idx:
                lower[row_idx, row_idx] = jnp.sqrt(accum)
            else:
                lower[row_idx, col_idx] = accum / lower[col_idx, col_idx]
    return lower

def solve_blocks(lower, vector):
    forward = []
    for row_idx in range(9):
        accum = vector[row_idx]
        for inner_idx in range(row_idx):
            accum = accum - lower[row_idx, inner_idx] * forward[inner_idx]
        forward.append(accum / lower[row_idx, row_idx])
    backward = [None] * 9
    for row_idx in reversed(range(9)):
        accum = forward[row_idx]
        for inner_idx in range(row_idx + 1, 9):
            accum = accum - lower[inner_idx, row_idx] * backward[inner_idx]
        backward[row_idx] = accum / lower[row_idx, row_idx]
    return jnp.stack(backward)

def apply_schur(blocks, neighbors, direction_full, direction_own):
    count = direction_own.shape[1]
    taken = direction_full[:, neighbors]
    stacked = jnp.concatenate([taken, direction_own[:, None, :]], axis=1)
    return jnp.einsum('rckn,ckn->rn', blocks.reshape(9, 9, NBR + 1, count), stacked, precision=lax.Precision.HIGHEST)

def reference(jacobian_cam, jacobian_pt, residuals, point_inverse, obs_camera, pair_slot, observation_used, pattern):
    normal_terms = point_terms(jacobian_cam, jacobian_pt, residuals, point_inverse, observation_used)
    cells = jnp.zeros((90, NBR + 1, CAMS), jnp.float32)
    for square_root in range(TRACK):
        for partner in range(TRACK):
            values = pair_block(square_root, partner, normal_terms)
            cells = cells.at[:, pair_slot[square_root, partner], obs_camera[square_root]].add(values)
    identity = jnp.eye(9, dtype=jnp.float32).reshape(81)
    blocks = cells[:81].at[:, NBR, :].add(DAMPING * identity[:, None])
    gradient = cells[81:, NBR, :]
    lower = factor_blocks(blocks[:, NBR, :].reshape(9, 9, CAMS))
    solution = jnp.zeros_like(gradient)
    remainder = gradient
    precond = solve_blocks(lower, remainder)
    direction = precond
    energy_now = jnp.sum(remainder * precond)
    for step_idx in range(ITERS):
        image = apply_schur(blocks, pattern, direction, direction)
        alpha = energy_now / jnp.sum(direction * image)
        solution = solution + alpha * direction
        remainder = remainder - alpha * image
        precond = solve_blocks(lower, remainder)
        energy_next = jnp.sum(remainder * precond)
        direction = precond + energy_next / energy_now * direction
        energy_now = energy_next
    camera_jacobian_rows, camera_point_coupling, points_removed, point_gradient, camera_gradient, observation_active, inverse_blocks = normal_terms
    reduced = point_gradient
    for square_root in range(TRACK):
        seen = solution[:, obs_camera[square_root]]
        reduced = reduced - lax.optimization_barrier(jnp.sum(camera_point_coupling[square_root] * seen[:, None, :], axis=0))
    point_step = lax.optimization_barrier(jnp.sum(inverse_blocks * reduced[None, :, :], axis=1))
    return (solution, remainder, point_step)
```

```python
import functools

import jax
import jax.numpy as jnp
from jax import lax
from jax.experimental import pallas as pl
from jax.experimental.pallas import tpu as pltpu
from jax.sharding import PartitionSpec as P

TRACK = 4
NBR = 12
ITERS = 4
OBS_CAP = 16
DAMPING = 1.0
BOTH = ("cam", "pt")

GROUP = 14
PAIRS = 7
ROWS = 2
PAIR_ROWS = 3
CELL = 96
F32 = jnp.float32
BF16 = jnp.bfloat16
PARAMS = pltpu.CompilerParams(vmem_limit_bytes=48 * 1024 * 1024)


def iota(shape, dim):
    return lax.broadcasted_iota(jnp.int32, shape, dim)


def quotient(values, divisor):
    return jnp.floor((values.astype(F32) + 0.5) * (1.0 / divisor))


def pieces(values):
    high = values.astype(BF16)
    rest = values - high.astype(F32)
    middle = rest.astype(BF16)
    low = (rest - middle.astype(F32)).astype(BF16)
    return high, middle, low


def dot_nn(left, right):
    return lax.dot_general(left, right, (((1,), (0,)), ((), ())), preferred_element_type=F32)


def dot_nt(left, right):
    return lax.dot_general(left, right, (((1,), (1,)), ((), ())), preferred_element_type=F32)


def one_hot(condition):
    return jnp.where(condition, 1.0, 0.0).astype(BF16)


def before(size):
    return one_hot(iota((size, size), 0) < iota((size, size), 1))


def pack_kernel(
    devices, shift, jc_ref, jp_ref, rs_ref, vi_ref, cam_ref, slot_ref, used_ref, pattern_ref,
    out_ref, place_ref, rank_ref, feat_ref,
):
    npts = cam_ref.shape[1]
    cam_dev = pattern_ref.shape[1]
    found = jnp.zeros((devices, cam_dev), F32)
    for k in range(NBR):
        target = lax.shift_right_logical(pattern_ref[k : k + 1, :], shift)
        found = jnp.where(iota((devices, cam_dev), 0) == target, 1.0, found)
    rank = dot_nn(found.astype(BF16), before(cam_dev))
    rank_ref[...] = jnp.where(found > 0, rank, -1.0e6)

    live = [used_ref[a : a + 1, :].astype(F32) for a in range(TRACK)]
    carry = jnp.zeros((devices, 1), F32)
    triangle = before(npts)
    hits = []
    withins = []
    for a in range(TRACK):
        owner = lax.shift_right_logical(cam_ref[a : a + 1, :], shift)
        hit = jnp.where(
            jnp.logical_and(iota((devices, npts), 0) == owner, live[a] > 0), 1.0, 0.0
        )
        hits.append(hit.astype(BF16))
        count = dot_nn(hits[a], triangle) + carry
        within = jnp.sum(hit * count, axis=0, keepdims=True)
        carry = carry + jnp.sum(hit, axis=1, keepdims=True)
        withins.append(within)
        part = quotient(within, PAIRS)
        place_ref[a : a + 1, :] = jnp.where(live[a] > 0, owner.astype(F32) * PAIR_ROWS + part, -1.0)
        place_ref[TRACK + a : TRACK + a + 1, :] = within - part * PAIRS

    vi = [[vi_ref[3 * x + y : 3 * x + y + 1, :] for y in range(3)] for x in range(3)]
    jp = [
        [[jp_ref[a, 3 * u + x : 3 * u + x + 1, :] for x in range(3)] for u in range(2)]
        for a in range(TRACK)
    ]
    res = [[rs_ref[a, u : u + 1, :] for u in range(2)] for a in range(TRACK)]
    grad = []
    for x in range(3):
        total = jnp.zeros((1, npts), F32)
        for a in range(TRACK):
            total = total - live[a] * (jp[a][0][x] * res[a][0] + jp[a][1][x] * res[a][1])
        grad.append(total)
    for a in range(TRACK):
        at = slice(a * npts, (a + 1) * npts)
        for u in range(2):
            feat_ref[8 * u : 8 * u + 8, at] = jc_ref[a, 9 * u : 9 * u + 8, :]
            feat_ref[64 + u : 65 + u, at] = jc_ref[a, 9 * u + 8 : 9 * u + 9, :]
        removed = [
            [live[a] * sum(jp[a][u][x] * vi[x][y] for x in range(3)) for y in range(3)]
            for u in range(2)
        ]

        def middle(b, u, v):
            return -live[b] * sum(removed[u][y] * jp[b][v][y] for y in range(3))

        partners = [b for b in range(TRACK) if b != a]
        for m, b in enumerate(partners):
            first = [jc_ref[b, 9 * v : 9 * v + 8, :] for v in range(2)]
            ninth = [jc_ref[b, 9 * v + 8 : 9 * v + 9, :] for v in range(2)]
            for u in range(2):
                row = 2 + 2 * m + u
                one, two = middle(b, u, 0), middle(b, u, 1)
                feat_ref[8 * row : 8 * row + 8, at] = one * first[0] + two * first[1]
                feat_ref[64 + row : 65 + row, at] = one * ninth[0] + two * ninth[1]
        feat_ref[72:73, at] = live[a] + middle(a, 0, 0)
        feat_ref[73:74, at] = middle(a, 0, 1)
        feat_ref[74:75, at] = live[a] + middle(a, 1, 1)
        for u in range(2):
            right = -(live[a] * res[a][u] + sum(removed[u][y] * grad[y] for y in range(3)))
            feat_ref[75 + u : 76 + u, at] = right
        own = cam_ref[a : a + 1, :] & (cam_dev - 1)
        for m, b in enumerate(partners):
            label = slot_ref[a, b : b + 1, :] * cam_dev + own
            feat_ref[77 + m : 78 + m, at] = label.astype(F32)

    owners = jnp.concatenate(hits, axis=1)
    place = jnp.concatenate(withins, axis=1)
    split = pieces(feat_ref[...])
    masks = [
        one_hot(jnp.broadcast_to(place, (16, TRACK * npts)) == float(s)) for s in range(OBS_CAP)
    ]
    for g in range(5):
        for h in range(2):
            right = jnp.concatenate(
                [part[16 * g : 16 * g + 16] * masks[8 * h + c] for part in split for c in range(8)], axis=0
            )
            sums = dot_nt(owners, right)
            out_ref[pl.ds(2 * g + h, devices, stride=10), :] = (
                sums[:, :128] + sums[:, 128:256] + sums[:, 256:]
            )


def place_kernel(devices, shift, pattern_ref, source_ref, rank_ref):
    cam_dev = pattern_ref.shape[1]
    count = jnp.zeros((devices, cam_dev), F32)
    sources = []
    withins = []
    for k in range(NBR):
        camera = pattern_ref[k : k + 1, :]
        source = lax.shift_right_logical(camera, shift)
        within = camera & (cam_dev - 1)
        sources.append(iota((devices, cam_dev), 0) == source)
        withins.append(iota((cam_dev, cam_dev), 0) == within)
        count = count + dot_nt(one_hot(sources[k]), one_hot(withins[k]))
        source_ref[:, k * cam_dev : (k + 1) * cam_dev] = source.astype(F32)
    rank = dot_nn(one_hot(count > 0), before(cam_dev))
    turned = rank.T.astype(BF16)
    for k in range(NBR):
        column = dot_nn(turned, one_hot(sources[k]))
        rank_ref[:, k * cam_dev : (k + 1) * cam_dev] = jnp.sum(
            jnp.where(withins[k], column, 0.0), axis=0, keepdims=True
        )


def schur_kernel(got_ref, out_ref, wanted_ref, text_ref):
    devices = got_ref.shape[0] // 10
    cam_dev = out_ref.shape[2]
    chunk = 2 * devices
    out_ref[...] = jnp.zeros_like(out_ref)
    for h in range(2):
        for g in range(5):
            turned = got_ref[pl.ds(2 * g + h, devices, stride=10), :].T
            for c in range(8):
                text_ref[4 * h + c // 2, 16 * g : 16 * g + 16, (c % 2) * devices : (c % 2 + 1) * devices] = (
                    turned[16 * c : 16 * c + 16]
                )
    lines = []
    for s in range(OBS_CAP):
        label = text_ref[s // 2, 77:78, (s % 2) * devices : (s % 2 + 1) * devices]
        lines.append(label - cam_dev * quotient(label, cam_dev))
    lines.append(jnp.zeros((128 - OBS_CAP, devices), F32))
    wanted_ref[...] = jnp.concatenate(lines, axis=0).T

    def outer(left, right, extra):
        blocks = []
        for r in range(8):
            blocks.append(left[0][0][r : r + 1] * right[0][0] + left[1][0][r : r + 1] * right[1][0])
        blocks.append(left[0][1] * right[0][0] + left[1][1] * right[1][0])
        blocks.append(left[0][0] * right[0][1] + left[1][0] * right[1][1])
        corner = left[0][1] * right[0][1] + left[1][1] * right[1][1]
        if extra is None:
            blocks.append(jnp.concatenate([corner, jnp.zeros((7, chunk), F32)], axis=0))
            blocks.append(jnp.zeros((8, chunk), F32))
        else:
            last = left[0][1] * extra[0] + left[1][1] * extra[1]
            blocks.append(jnp.concatenate([corner, last, jnp.zeros((6, chunk), F32)], axis=0))
            blocks.append(left[0][0] * extra[0] + left[1][0] * extra[1])
        return jnp.concatenate(blocks, axis=0)

    def step(index, _):
        text = text_ref[index]
        vectors = [(text[8 * v : 8 * v + 8], text[64 + v : 65 + v]) for v in range(8)]
        own = vectors[0:2]
        cells = [quotient(text[77 + m : 78 + m], cam_dev) for m in range(3)]
        within = text[77:78] - cells[0] * cam_dev
        hit = one_hot(iota((cam_dev, chunk), 0).astype(F32) == within)
        corner = [[text[72:73], text[73:74]], [text[73:74], text[74:75]]]
        weighted = [
            tuple(corner[u][0] * own[0][i] + corner[u][1] * own[1][i] for i in range(2)) for u in range(2)
        ]
        terms = [outer(own, weighted, [text[75:76], text[76:77]])]
        for m in range(3):
            terms.append(outer(own, vectors[2 + 2 * m : 4 + 2 * m], None))
        terms = [jnp.concatenate(pieces(term), axis=0) for term in terms]
        for k in range(NBR + 1):
            if k < NBR:
                part = None
                for m in range(3):
                    piece = terms[1 + m] * one_hot(cells[m] == float(k))
                    part = piece if part is None else part + piece
            else:
                part = terms[0]
            sums = dot_nt(part, hit)
            out_ref[k] = out_ref[k] + (sums[:CELL] + sums[CELL : 2 * CELL] + sums[2 * CELL :])
        return 0

    lax.fori_loop(0, OBS_CAP // 2, step, 0)
    unit = iota((CELL, cam_dev), 0)
    unit = jnp.logical_and(unit <= 63, unit == 9 * lax.shift_right_logical(unit, 3)) | (unit == 80)
    out_ref[NBR] = out_ref[NBR] + jnp.where(unit, DAMPING, 0.0)


def cholesky(cells_ref, lower_ref):
    cam_dev = cells_ref.shape[2]
    zero = jnp.zeros((7, cam_dev), F32)
    block = cells_ref[NBR]
    columns = [
        jnp.concatenate([block[8 * r : 8 * r + 8], block[64 + r : 65 + r], zero], axis=0) for r in range(8)
    ]
    columns.append(jnp.concatenate([block[64:72], block[80:81], zero], axis=0))
    row = iota((16, cam_dev), 0)
    for c in range(9):
        pivot = columns[c][c : c + 1]
        root = jnp.sqrt(pivot)
        inverse = 1.0 / root
        column = jnp.where(row > c, columns[c] * inverse, 0.0)
        for r in range(c + 1, 9):
            columns[r] = columns[r] - column * column[r : r + 1]
        lower_ref[c] = jnp.where(row == 9, inverse, jnp.where(row < 9, column, 0.0))


def solve(lower_ref, vector):
    row = iota(vector.shape, 0)
    rest = vector
    copies = vector.shape[1] // lower_ref.shape[2]
    columns = [jnp.concatenate([lower_ref[c]] * copies, axis=1) for c in range(9)]
    for c in range(9):
        column = columns[c]
        value = rest[c : c + 1] * column[9:10]
        rest = jnp.where(row == c, value, rest - jnp.where(row < 9, column, 0.0) * value)
    for c in reversed(range(9)):
        column = columns[c]
        if c < 8:
            dotted = jnp.sum(
                jnp.where(jnp.logical_and(row > c, row < 9), column * rest, 0.0), axis=0, keepdims=True
            )
        else:
            dotted = jnp.zeros((1, vector.shape[1]), F32)
        value = (rest[c : c + 1] - dotted) * column[9:10]
        rest = jnp.where(row == c, value, rest)
    return rest


def multiply(cells_ref, taken, own):
    cam_dev = own.shape[1]
    sums = [jnp.zeros((8, cam_dev), F32) for _ in range(9)]
    side = jnp.zeros((8, cam_dev), F32)
    corner = jnp.zeros((1, cam_dev), F32)
    for k in range(NBR + 1):
        vector = own if k == NBR else taken[:, k * cam_dev : (k + 1) * cam_dev]
        first, last = vector[0:8], vector[8:9]
        for r in range(9):
            sums[r] = sums[r] + cells_ref[k, 8 * r : 8 * r + 8, :] * first
        side = side + cells_ref[k, 72:80, :] * last
        corner = corner + cells_ref[k, 80:81, :] * last
    lines = [jnp.sum(part, axis=0, keepdims=True) for part in sums]
    top = jnp.concatenate(lines[:8], axis=0) + side
    return jnp.concatenate([top, lines[8] + corner, jnp.zeros((7, cam_dev), F32)], axis=0)


def total_of(values):
    return jnp.sum(jnp.sum(values, axis=1, keepdims=True), axis=0, keepdims=True)


def spread(vector, row_of):
    cam_dev = vector.shape[1]
    choose = one_hot(iota((128, vector.shape[0]), 1).astype(F32) == row_of)
    copies = dot_nn(choose, jnp.concatenate(pieces(vector), axis=1))
    return [copies[:, p * cam_dev : (p + 1) * cam_dev] for p in range(3)]


def lane_groups(count):
    size = 126 // count
    lane = iota((128, 1), 0)
    group = quotient(lane, size)
    return group, lane.astype(F32) - group * size


def value_rows(count, values):
    if count == PAIRS:
        return jnp.where(values < 9, values, values + 7)
    return values


def send_rows(send_ref, vector, count, hits_of, rows, scalars):
    devices = send_ref.shape[0] // rows
    group, value = lane_groups(count)
    copies = spread(vector, value_rows(count, value))
    right = jnp.concatenate(
        [
            jnp.concatenate([jnp.where(group == float(g), part, 0.0) for g in range(count)], axis=1)
            for part in copies
        ],
        axis=0,
    ).astype(BF16)
    lane = iota((devices, 128), 1)
    for h in range(rows):
        hits = [hits_of(count * h + g) for g in range(count)]
        sums = dot_nt(jnp.concatenate(hits, axis=1), right)
        text = sums[:, :128] + sums[:, 128:256] + sums[:, 256:]
        for index, scalar in enumerate(scalars[2 * h : 2 * h + 2]):
            text = jnp.where(lane == 126 + index, scalar, text)
        send_ref[pl.ds(h, devices, stride=rows), :] = text


def send_coupled(send_ref, vector, count, rank_ref, rows, scalars):
    rank = rank_ref[...]
    send_rows(send_ref, vector, count, lambda slot: one_hot(rank == float(slot)), rows, scalars)


def read_rows(got, rows, count, places, groups, height, scalars):
    turned = got.T
    total = turned.shape[1]
    group, _ = lane_groups(count)
    mark = one_hot(iota((total, places.shape[1]), 0).astype(F32) == places)
    taken = dot_nn(jnp.concatenate(pieces(turned), axis=0), mark)
    wide = jnp.concatenate([group] * 3, axis=0)
    kept = jnp.where(wide == groups, taken, 0.0).astype(BF16)
    lane = iota((height, 128), 1)
    size = 126 // count
    value = value_rows(count, lane.astype(F32) - quotient(lane, size) * size)
    fold = one_hot(jnp.logical_and(iota((height, 128), 0).astype(F32) == value, lane < 126))
    vectors = dot_nn(jnp.concatenate([fold] * 3, axis=1), kept)
    column = iota((1, total), 1)
    inner = column.astype(F32) - quotient(column, rows) * rows
    sums = []
    for index in range(scalars):
        line = turned[126 + index % 2 : 127 + index % 2]
        sums.append(
            jnp.sum(jnp.where(inner == float(index // 2), line, 0.0), axis=1, keepdims=True)
        )
    return vectors, sums


def read_coupled(got_ref, rows, count, source_ref, rank_ref, height, scalars):
    part = quotient(rank_ref[...], count)
    places = source_ref[...] * rows + part
    return read_rows(got_ref[...], rows, count, places, rank_ref[...] - part * count, height, scalars)


def wide(index):
    return index >= 2


def layout(index):
    return (2 * ROWS, PAIRS) if wide(index) else (ROWS, GROUP)


def start_kernel(cells_ref, rank_ref, lower_ref, state_ref, send_ref):
    cam_dev = cells_ref.shape[2]
    cholesky(cells_ref, lower_ref)
    block = cells_ref[NBR]
    right = jnp.concatenate([block[88:96], block[81:82], jnp.zeros((7, cam_dev), F32)], axis=0)
    scaled = solve(lower_ref, right)
    zero = jnp.zeros_like(right)
    state_ref[0] = zero
    state_ref[1] = right
    state_ref[2] = scaled
    state_ref[3] = scaled
    state_ref[4] = zero
    state_ref[5] = zero
    state_ref[6] = zero
    most = jnp.max(jnp.max(rank_ref[...], axis=1, keepdims=True), axis=0, keepdims=True)
    crowded = jnp.where(most >= float(GROUP * ROWS), 1.0, 0.0)
    send_coupled(send_ref, scaled, GROUP, rank_ref, ROWS, [crowded])


def step_kernel(
    index, got_ref, source_ref, place_ref, rank_ref, cells_ref, lower_ref, state_ref, far_ref,
    state_out, far_out, send_ref,
):
    rows, count = layout(index)
    arrived, sums = read_coupled(
        got_ref, rows, count, source_ref, place_ref, 32 if wide(index) else 16, 4 if index else 1
    )
    cam_dev = cells_ref.shape[2]
    step, rest, scaled, direction = (state_ref[i] for i in range(4))
    if index:
        image, image_scaled = state_ref[4], state_ref[5]
        energy, cross, square, old = sums
        alpha = old / energy
        beta = (old - 2.0 * alpha * cross + alpha * alpha * square) / old
        step = step + alpha * direction
        rest = rest - alpha * image
        direction = (scaled - alpha * image_scaled) + beta * direction
        far_before = arrived[16:] if wide(index) else far_ref[...]
        far = (far_before - alpha * arrived[:16]) + beta * far_ref[...]
    else:
        far = arrived
    image = multiply(cells_ref, far, direction)
    energy = total_of(direction * image)
    state_out[0] = step
    state_out[1] = rest
    state_out[3] = direction
    state_out[4] = image
    state_out[6] = state_ref[6] if index else jnp.zeros_like(step) + sums[0]
    far_out[...] = far
    if index == ITERS - 1:
        scaled = solve(lower_ref, rest)
        state_out[2] = scaled
        state_out[5] = jnp.zeros_like(image)
        lane = iota((rank_ref.shape[0], cam_dev), 1).astype(F32)

        def wanted(slot):
            if slot < OBS_CAP:
                return one_hot(rank_ref[:, slot : slot + 1] == lane)
            return jnp.zeros(lane.shape, BF16)

        both = jnp.concatenate([step, direction], axis=0)
        send_rows(send_ref, both, PAIRS, wanted, PAIR_ROWS, [energy, total_of(rest * scaled)])
        return
    solved = solve(lower_ref, jnp.concatenate([rest, image], axis=1))
    scaled, image_scaled = solved[:, :cam_dev], solved[:, cam_dev:]
    state_out[2] = scaled
    state_out[5] = image_scaled
    scalars = [
        energy, total_of(scaled * image), total_of(image * image_scaled), total_of(rest * scaled)
    ]
    rows, count = layout(index + 1)
    vector = jnp.concatenate([image_scaled, scaled], axis=0) if wide(index + 1) else image_scaled
    send_coupled(send_ref, vector, count, rank_ref, rows, scalars)


def finish_kernel(
    got_ref, place_ref, state_ref, jc_ref, jp_ref, rs_ref, vi_ref, used_ref, step_ref, rest_ref, point_ref
):
    npts = used_ref.shape[1]
    places = jnp.concatenate([place_ref[a : a + 1, :] for a in range(TRACK)], axis=1)
    groups = jnp.concatenate([place_ref[TRACK + a : TRACK + a + 1, :] for a in range(TRACK)], axis=1)
    seen, sums = read_rows(got_ref[...], PAIR_ROWS, PAIRS, places, groups, 32, 2)
    alpha = sums[1] / sums[0]
    step_ref[...] = (state_ref[0] + alpha * state_ref[3])[:9]
    rest_ref[...] = (state_ref[1] - alpha * state_ref[4])[:9]
    moved = seen[:16] + alpha * seen[16:]
    reduced = [jnp.zeros((1, npts), F32) for _ in range(3)]
    for a in range(TRACK):
        live = used_ref[a : a + 1, :].astype(F32)
        there = moved[:9, a * npts : (a + 1) * npts]
        for u in range(2):
            change = jnp.sum(jc_ref[a, 9 * u : 9 * u + 9, :] * there, axis=0, keepdims=True)
            change = live * (change + rs_ref[a, u : u + 1, :])
            for x in range(3):
                reduced[x] = reduced[x] - jp_ref[a, 3 * u + x : 3 * u + x + 1, :] * change
    for x in range(3):
        point_ref[x : x + 1, :] = sum(
            vi_ref[3 * x + y : 3 * x + y + 1, :] * reduced[y] for y in range(3)
        )


def factor_blocks(matrix):
    lower = {}
    for row_idx in range(9):
        for col_idx in range(row_idx + 1):
            accum = matrix[row_idx, col_idx]
            for inner_idx in range(col_idx):
                accum = accum - lower[row_idx, inner_idx] * lower[col_idx, inner_idx]
            if row_idx == col_idx:
                lower[row_idx, row_idx] = jnp.sqrt(accum)
            else:
                lower[row_idx, col_idx] = accum / lower[col_idx, col_idx]
    return lower


def solve_blocks(lower, vector):
    forward = []
    for row_idx in range(9):
        accum = vector[row_idx]
        for inner_idx in range(row_idx):
            accum = accum - lower[row_idx, inner_idx] * forward[inner_idx]
        forward.append(accum / lower[row_idx, row_idx])
    backward = [None] * 9
    for row_idx in reversed(range(9)):
        accum = forward[row_idx]
        for inner_idx in range(row_idx + 1, 9):
            accum = accum - lower[inner_idx, row_idx] * backward[inner_idx]
        backward[row_idx] = accum / lower[row_idx, row_idx]
    return jnp.stack(backward)


def whole_exchange(cells, pattern, jacobian_cam, jacobian_pt, residuals, point_inverse, obs_camera, used):
    cam_dev = pattern.shape[1]
    main = cells[:, :64].reshape(NBR + 1, 8, 8, cam_dev)
    side = cells[:, 72:80].reshape(NBR + 1, 8, 1, cam_dev)
    foot = jnp.concatenate([cells[:, 64:72], cells[:, 80:81]], axis=1)[:, None]
    blocks = jnp.concatenate([jnp.concatenate([main, side], axis=2), foot], axis=1)
    gradient = jnp.concatenate([cells[NBR, 88:96], cells[NBR, 81:82]], axis=0)
    lower = factor_blocks(blocks[NBR])

    def gathered(vector):
        return lax.all_gather(vector, BOTH, axis=1, tiled=True)

    def summed(values):
        return lax.psum(jnp.sum(values), BOTH)

    step = jnp.zeros_like(gradient)
    rest = gradient
    scaled = solve_blocks(lower, rest)
    direction = scaled
    energy_now = summed(rest * scaled)
    for _ in range(ITERS):
        taken = jnp.concatenate([gathered(direction)[:, pattern], direction[:, None, :]], axis=1)
        image = jnp.sum(blocks * jnp.swapaxes(taken, 0, 1)[:, None], axis=(0, 2))
        alpha = energy_now / summed(direction * image)
        step = step + alpha * direction
        rest = rest - alpha * image
        scaled = solve_blocks(lower, rest)
        energy_next = summed(rest * scaled)
        direction = scaled + energy_next / energy_now * direction
        energy_now = energy_next
    whole = gathered(step)
    npts = obs_camera.shape[1]
    rows = jacobian_cam.reshape(TRACK, 2, 9, npts)
    seen = jnp.swapaxes(whole[:, obs_camera], 0, 1)
    change = jnp.sum(rows * seen[:, None], axis=2) + residuals
    change = change * used.astype(F32)[:, None]
    reduced = -jnp.sum(jacobian_pt.reshape(TRACK, 2, 3, npts) * change[:, :, None], axis=(0, 1))
    point_step = jnp.sum(point_inverse.reshape(3, 3, npts) * reduced[None], axis=1)
    return step, rest, point_step


def shape(*dims):
    return jax.ShapeDtypeStruct(dims, F32)


def call(kernel, outs, name, scratch=()):
    return pl.pallas_call(
        kernel, out_shape=outs, name=name, compiler_params=PARAMS, scratch_shapes=list(scratch)
    )


def exchange(message, devices):
    width = message.shape[0] // devices
    arrived = lax.all_to_all(
        message.reshape(devices, width, 1, 128), BOTH, split_axis=0, concat_axis=0, tiled=True
    )
    return arrived.reshape(devices * width, 128)


def per_device(
    jacobian_cam, jacobian_pt, residuals, point_inverse, obs_camera, pair_slot, observation_used, pattern,
):
    devices = lax.axis_size("cam") * lax.axis_size("pt")
    npts = obs_camera.shape[1]
    cam_dev = pattern.shape[1]
    shift = cam_dev.bit_length() - 1
    couplings = NBR * cam_dev

    packed, places, rank = call(
        functools.partial(pack_kernel, devices, shift),
        (shape(devices * 10, 128), shape(2 * TRACK, npts), shape(devices, cam_dev)),
        "pack",
        [pltpu.VMEM((80, TRACK * npts), F32)],
    )(jacobian_cam, jacobian_pt, residuals, point_inverse, obs_camera, pair_slot, observation_used, pattern)
    got = exchange(packed, devices)
    sources, far_rank = call(
        functools.partial(place_kernel, devices, shift),
        (shape(1, couplings), shape(1, couplings)),
        "place",
    )(pattern)
    cells, wanted = call(
        schur_kernel,
        (shape(NBR + 1, CELL, cam_dev), shape(devices, 128)),
        "schur",
        [pltpu.VMEM((OBS_CAP // 2, 80, 2 * devices), F32)],
    )(got)
    lower, state, message = call(
        start_kernel,
        (shape(9, 16, cam_dev), shape(7, 16, cam_dev), shape(devices * ROWS, 128)),
        "start",
    )(cells, rank)
    far = jnp.zeros((16, couplings), F32)
    crowded = None
    for index in range(ITERS):
        last = index == ITERS - 1
        rows = PAIR_ROWS if last else layout(index + 1)[0]
        arrived = exchange(message, devices)
        state, far, message = call(
            functools.partial(step_kernel, index),
            (shape(7, 16, cam_dev), shape(16, couplings), shape(devices * rows, 128)),
            "step",
        )(arrived, sources, far_rank, wanted if last else rank, cells, lower, state, far)
        if index == 0:
            crowded = state[6, 0, 0] > 0.0
    arrived = exchange(message, devices)
    found = call(
        finish_kernel, (shape(9, cam_dev), shape(9, cam_dev), shape(3, npts)), "finish"
    )(arrived, places, state, jacobian_cam, jacobian_pt, residuals, point_inverse, observation_used)

    def dense():
        return whole_exchange(
            cells, pattern, jacobian_cam, jacobian_pt, residuals, point_inverse, obs_camera, observation_used
        )

    return lax.cond(crowded, dense, lambda: tuple(found))


def solution(mesh):
    return jax.shard_map(
        per_device,
        mesh=mesh,
        in_specs=(
            P(None, None, BOTH),
            P(None, None, BOTH),
            P(None, None, BOTH),
            P(None, BOTH),
            P(None, BOTH),
            P(None, None, BOTH),
            P(None, BOTH),
            P(None, BOTH),
        ),
        out_specs=(P(None, BOTH), P(None, BOTH), P(None, BOTH)),
        check_vma=False,
    )
```

```python
import functools

import jax
import jax.numpy as jnp
from jax import lax
from jax.experimental import pallas as pl
from jax.experimental.pallas import tpu as pltpu
from jax.sharding import PartitionSpec as P

TRACK = 4
NBR = 12
ITERS = 4
OBS_CAP = 16
DAMPING = 1.0
BOTH = ("cam", "pt")

GROUP = 14
PAIRS = 7
ROWS = 2
PAIR_ROWS = 3
CELL = 96
F32 = jnp.float32
BF16 = jnp.bfloat16
PARAMS = pltpu.CompilerParams(vmem_limit_bytes=28 * 1024 * 1024)


def iota(shape, dim):
    return lax.broadcasted_iota(jnp.int32, shape, dim)


def quotient(values, divisor):
    return jnp.floor((values.astype(F32) + 0.5) * (1.0 / divisor))


def pieces(values):
    high = values.astype(BF16)
    rest = values - high.astype(F32)
    middle = rest.astype(BF16)
    low = (rest - middle.astype(F32)).astype(BF16)
    return high, middle, low


def dot_nn(left, right):
    return lax.dot_general(left, right, (((1,), (0,)), ((), ())), preferred_element_type=F32)


def dot_nt(left, right):
    return lax.dot_general(left, right, (((1,), (1,)), ((), ())), preferred_element_type=F32)


def one_hot(condition):
    return jnp.where(condition, 1.0, 0.0).astype(BF16)


def before(size):
    return one_hot(iota((size, size), 0) < iota((size, size), 1))


def pack_kernel(
    devices, shift, jc_ref, jp_ref, rs_ref, vi_ref, cam_ref, slot_ref, used_ref, pattern_ref,
    out_ref, place_ref, rank_ref, feat_ref,
):
    npts = cam_ref.shape[1]
    cam_dev = pattern_ref.shape[1]
    found = jnp.zeros((devices, cam_dev), F32)
    for k in range(NBR):
        target = lax.shift_right_logical(pattern_ref[k : k + 1, :], shift)
        found = jnp.where(iota((devices, cam_dev), 0) == target, 1.0, found)
    rank = dot_nn(found.astype(BF16), before(cam_dev))
    rank_ref[...] = jnp.where(found > 0, rank, -1.0e6)

    live = [used_ref[a : a + 1, :].astype(F32) for a in range(TRACK)]
    carry = jnp.zeros((devices, 1), F32)
    triangle = before(npts)
    hits = []
    withins = []
    for a in range(TRACK):
        owner = lax.shift_right_logical(cam_ref[a : a + 1, :], shift)
        hit = jnp.where(
            jnp.logical_and(iota((devices, npts), 0) == owner, live[a] > 0), 1.0, 0.0
        )
        hits.append(hit.astype(BF16))
        count = dot_nn(hits[a], triangle) + carry
        within = jnp.sum(hit * count, axis=0, keepdims=True)
        carry = carry + jnp.sum(hit, axis=1, keepdims=True)
        withins.append(within)
        part = quotient(within, PAIRS)
        place_ref[a : a + 1, :] = jnp.where(live[a] > 0, owner.astype(F32) * PAIR_ROWS + part, -1.0)
        place_ref[TRACK + a : TRACK + a + 1, :] = within - part * PAIRS

    vi = [[vi_ref[3 * x + y : 3 * x + y + 1, :] for y in range(3)] for x in range(3)]
    jp = [
        [[jp_ref[3 * u + x : 3 * u + x + 1, a, :] for x in range(3)] for u in range(2)]
        for a in range(TRACK)
    ]
    res = [[rs_ref[a, u : u + 1, :] for u in range(2)] for a in range(TRACK)]
    grad = []
    for x in range(3):
        total = jnp.zeros((1, npts), F32)
        for a in range(TRACK):
            total = total - live[a] * (jp[a][0][x] * res[a][0] + jp[a][1][x] * res[a][1])
        grad.append(total)
    for a in range(TRACK):
        at = slice(a * npts, (a + 1) * npts)
        for u in range(2):
            feat_ref[8 * u : 8 * u + 8, at] = jc_ref[9 * u : 9 * u + 8, a, :]
            feat_ref[64 + u : 65 + u, at] = jc_ref[9 * u + 8 : 9 * u + 9, a, :]
        removed = [
            [live[a] * sum(jp[a][u][x] * vi[x][y] for x in range(3)) for y in range(3)]
            for u in range(2)
        ]

        def middle(b, u, v):
            return -live[b] * sum(removed[u][y] * jp[b][v][y] for y in range(3))

        partners = [b for b in range(TRACK) if b != a]
        for m, b in enumerate(partners):
            first = [jc_ref[9 * v : 9 * v + 8, b, :] for v in range(2)]
            ninth = [jc_ref[9 * v + 8 : 9 * v + 9, b, :] for v in range(2)]
            for u in range(2):
                row = 2 + 2 * m + u
                one, two = middle(b, u, 0), middle(b, u, 1)
                feat_ref[8 * row : 8 * row + 8, at] = one * first[0] + two * first[1]
                feat_ref[64 + row : 65 + row, at] = one * ninth[0] + two * ninth[1]
        feat_ref[72:73, at] = live[a] + middle(a, 0, 0)
        feat_ref[73:74, at] = middle(a, 0, 1)
        feat_ref[74:75, at] = live[a] + middle(a, 1, 1)
        for u in range(2):
            right = -(live[a] * res[a][u] + sum(removed[u][y] * grad[y] for y in range(3)))
            feat_ref[75 + u : 76 + u, at] = right
        own = cam_ref[a : a + 1, :] & (cam_dev - 1)
        for m, b in enumerate(partners):
            label = slot_ref[a, b : b + 1, :] * cam_dev + own
            feat_ref[77 + m : 78 + m, at] = label.astype(F32)

    owners = jnp.concatenate(hits, axis=1)
    place = jnp.concatenate(withins, axis=1)
    split = pieces(feat_ref[...])
    masks = [
        one_hot(jnp.broadcast_to(place, (16, TRACK * npts)) == float(s)) for s in range(OBS_CAP)
    ]
    for g in range(5):
        for h in range(2):
            right = jnp.concatenate(
                [part[16 * g : 16 * g + 16] * masks[8 * h + c] for part in split for c in range(8)], axis=0
            )
            sums = dot_nt(owners, right)
            out_ref[pl.ds(2 * g + h, devices, stride=10), :] = (
                sums[:, :128] + sums[:, 128:256] + sums[:, 256:]
            )


def place_kernel(devices, shift, pattern_ref, source_ref, far_ref):
    cam_dev = pattern_ref.shape[1]
    count = jnp.zeros((devices, cam_dev), F32)
    sources = []
    withins = []
    for k in range(NBR):
        camera = pattern_ref[k : k + 1, :]
        source = lax.shift_right_logical(camera, shift)
        within = camera & (cam_dev - 1)
        sources.append(iota((devices, cam_dev), 0) == source)
        withins.append(iota((cam_dev, cam_dev), 0) == within)
        count = count + dot_nt(one_hot(sources[k]), one_hot(withins[k]))
        source_ref[:, k * cam_dev : (k + 1) * cam_dev] = source.astype(F32)
    rank = dot_nn(one_hot(count > 0), before(cam_dev))
    turned = rank.T.astype(BF16)
    for k in range(NBR):
        column = dot_nn(turned, one_hot(sources[k]))
        mine = jnp.sum(jnp.where(withins[k], column, 0.0), axis=0, keepdims=True)
        far_ref[:, k * cam_dev : (k + 1) * cam_dev] = mine


def outer(left, right, extra):
    blocks = []
    for r in range(8):
        blocks.append(left[0][0][r : r + 1] * right[0][0] + left[1][0][r : r + 1] * right[1][0])
    blocks.append(left[0][1] * right[0][0] + left[1][1] * right[1][0])
    blocks.append(left[0][0] * right[0][1] + left[1][0] * right[1][1])
    corner = left[0][1] * right[0][1] + left[1][1] * right[1][1]
    chunk = corner.shape[1]
    if extra is None:
        blocks.append(jnp.concatenate([corner, jnp.zeros((7, chunk), F32)], axis=0))
        blocks.append(jnp.zeros((8, chunk), F32))
    else:
        last = left[0][1] * extra[0] + left[1][1] * extra[1]
        blocks.append(jnp.concatenate([corner, last, jnp.zeros((6, chunk), F32)], axis=0))
        blocks.append(left[0][0] * extra[0] + left[1][0] * extra[1])
    return jnp.concatenate(blocks, axis=0)


def observation(text, cam_dev):
    vectors = [(text[8 * v : 8 * v + 8], text[64 + v : 65 + v]) for v in range(8)]
    cells = [quotient(text[77 + m : 78 + m], cam_dev) for m in range(3)]
    within = text[77:78] - cells[0] * cam_dev
    hit = one_hot(iota((cam_dev, text.shape[1]), 0).astype(F32) == within)
    return vectors, cells, within, hit


def folded(sums):
    return sums[:CELL] + sums[CELL : 2 * CELL] + sums[2 * CELL :]


def diagonal_kernel(
    got_ref, rank_ref, text_ref, out_ref, lower_ref, state_ref, send_ref
):
    devices = got_ref.shape[0] // 10
    cam_dev = out_ref.shape[1]
    for h in range(2):
        for g in range(5):
            turned = got_ref[pl.ds(2 * g + h, devices, stride=10), :].T
            for c in range(8):
                at = slice((c % 2) * devices, (c % 2 + 1) * devices)
                text_ref[4 * h + c // 2, 16 * g : 16 * g + 16, at] = turned[16 * c : 16 * c + 16]
    unit = iota((CELL, cam_dev), 0)
    unit = jnp.logical_and(unit <= 63, unit == 9 * lax.shift_right_logical(unit, 3)) | (unit == 80)
    total = jnp.where(unit, DAMPING, 0.0)
    for index in range(OBS_CAP // 2):
        text = text_ref[index]
        vectors, _, _, hit = observation(text, cam_dev)
        own = vectors[0:2]
        corner = [[text[72:73], text[73:74]], [text[73:74], text[74:75]]]
        weighted = [
            tuple(corner[u][0] * own[0][i] + corner[u][1] * own[1][i] for i in range(2)) for u in range(2)
        ]
        term = outer(own, weighted, [text[75:76], text[76:77]])
        total = total + folded(dot_nt(jnp.concatenate(pieces(term), axis=0), hit))
    out_ref[...] = total
    cholesky(out_ref, lower_ref)
    right = jnp.concatenate([total[88:96], total[81:82], jnp.zeros((7, cam_dev), F32)], axis=0)
    scaled = solve(lower_ref, right)
    zero = jnp.zeros_like(right)
    state_ref[0] = zero
    state_ref[1] = right
    state_ref[2] = scaled
    state_ref[3] = scaled
    for index in range(4, 7):
        state_ref[index] = zero
    most = jnp.max(jnp.max(rank_ref[...], axis=1, keepdims=True), axis=0, keepdims=True)
    crowded = jnp.where(most >= float(GROUP * ROWS), 1.0, 0.0)
    send_rows(send_ref, scaled, GROUP, ranked(rank_ref), ROWS, [crowded])


def coupling_kernel(text_ref, out_ref, wanted_ref):
    cam_dev = out_ref.shape[2]
    devices = wanted_ref.shape[0]
    out_ref[...] = jnp.zeros_like(out_ref)

    def step(index, _):
        vectors, cells, _, hit = observation(text_ref[index], cam_dev)
        terms = [
            jnp.concatenate(pieces(outer(vectors[0:2], vectors[2 + 2 * m : 4 + 2 * m], None)), axis=0)
            for m in range(3)
        ]
        for k in range(NBR):
            part = None
            for m in range(3):
                piece = terms[m] * one_hot(cells[m] == float(k))
                part = piece if part is None else part + piece
            out_ref[k] = out_ref[k] + folded(dot_nt(part, hit))
        return 0

    lax.fori_loop(0, OBS_CAP // 2, step, 0)
    lines = []
    for s in range(OBS_CAP):
        label = text_ref[s // 2, 77:78, (s % 2) * devices : (s % 2 + 1) * devices]
        lines.append(label - cam_dev * quotient(label, cam_dev))
    lines.append(jnp.zeros((128 - OBS_CAP, devices), F32))
    wanted_ref[...] = jnp.concatenate(lines, axis=0).T


def cholesky(cells_ref, lower_ref):
    cam_dev = cells_ref.shape[1]
    zero = jnp.zeros((7, cam_dev), F32)
    block = cells_ref[...]
    columns = [
        jnp.concatenate([block[8 * r : 8 * r + 8], block[64 + r : 65 + r], zero], axis=0) for r in range(8)
    ]
    columns.append(jnp.concatenate([block[64:72], block[80:81], zero], axis=0))
    row = iota((16, cam_dev), 0)
    for c in range(9):
        pivot = columns[c][c : c + 1]
        root = jnp.sqrt(pivot)
        inverse = 1.0 / root
        column = jnp.where(row > c, columns[c] * inverse, 0.0)
        for r in range(c + 1, 9):
            columns[r] = columns[r] - column * column[r : r + 1]
        lower_ref[c] = jnp.where(row == 9, inverse, jnp.where(row < 9, column, 0.0))


def solve(lower_ref, vector):
    row = iota(vector.shape, 0)
    rest = vector
    copies = vector.shape[1] // lower_ref.shape[2]
    columns = [jnp.concatenate([lower_ref[c]] * copies, axis=1) for c in range(9)]
    for c in range(9):
        column = columns[c]
        value = rest[c : c + 1] * column[9:10]
        rest = jnp.where(row == c, value, rest - jnp.where(row < 9, column, 0.0) * value)
    for c in reversed(range(9)):
        column = columns[c]
        if c < 8:
            dotted = jnp.sum(
                jnp.where(jnp.logical_and(row > c, row < 9), column * rest, 0.0), axis=0, keepdims=True
            )
        else:
            dotted = jnp.zeros((1, vector.shape[1]), F32)
        value = (rest[c : c + 1] - dotted) * column[9:10]
        rest = jnp.where(row == c, value, rest)
    return rest


def multiply(cells_ref, diagonal_ref, taken, own):
    cam_dev = own.shape[1]
    sums = [jnp.zeros((8, cam_dev), F32) for _ in range(9)]
    side = jnp.zeros((8, cam_dev), F32)
    corner = jnp.zeros((1, cam_dev), F32)
    for k in range(NBR + 1):
        vector = own if k == NBR else taken[:, k * cam_dev : (k + 1) * cam_dev]
        first, last = vector[0:8], vector[8:9]
        cell_ref = diagonal_ref if k == NBR else cells_ref.at[k]
        for r in range(9):
            sums[r] = sums[r] + cell_ref[8 * r : 8 * r + 8, :] * first
        side = side + cell_ref[72:80, :] * last
        corner = corner + cell_ref[80:81, :] * last
    lines = [jnp.sum(part, axis=0, keepdims=True) for part in sums]
    top = jnp.concatenate(lines[:8], axis=0) + side
    return jnp.concatenate([top, lines[8] + corner, jnp.zeros((7, cam_dev), F32)], axis=0)


def total_of(values):
    return jnp.sum(jnp.sum(values, axis=1, keepdims=True), axis=0, keepdims=True)


def spread(vector, row_of):
    cam_dev = vector.shape[1]
    choose = one_hot(iota((128, vector.shape[0]), 1).astype(F32) == row_of)
    copies = dot_nn(choose, jnp.concatenate(pieces(vector), axis=1))
    return [copies[:, p * cam_dev : (p + 1) * cam_dev] for p in range(3)]


def lane_groups(count):
    size = 126 // count
    lane = iota((128, 1), 0)
    group = quotient(lane, size)
    return group, lane.astype(F32) - group * size


def value_rows(count, values):
    if count == PAIRS:
        return jnp.where(values < 9, values, values + 7)
    return values


def ranked(rank_ref):
    rank = rank_ref[...]
    return lambda slot: one_hot(rank == float(slot))


def send_rows(send_ref, vector, count, hits_of, rows, scalars):
    devices = send_ref.shape[0] // rows
    group, value = lane_groups(count)
    copies = spread(vector, value_rows(count, value))
    right = jnp.concatenate(
        [
            jnp.concatenate([jnp.where(group == float(g), part, 0.0) for g in range(count)], axis=1)
            for part in copies
        ],
        axis=0,
    ).astype(BF16)
    lane = iota((devices, 128), 1)
    for h in range(rows):
        hits = [hits_of(count * h + g) for g in range(count)]
        sums = dot_nt(jnp.concatenate(hits, axis=1), right)
        text = sums[:, :128] + sums[:, 128:256] + sums[:, 256:]
        for index, scalar in enumerate(scalars[2 * h : 2 * h + 2]):
            text = jnp.where(lane == 126 + index, scalar, text)
        send_ref[pl.ds(h, devices, stride=rows), :] = text


def read_rows(got, rows, count, places, groups, height, scalars):
    turned = got.T
    total = turned.shape[1]
    group, _ = lane_groups(count)
    mark = one_hot(iota((total, places.shape[1]), 0).astype(F32) == places)
    taken = dot_nn(jnp.concatenate(pieces(turned), axis=0), mark)
    group = jnp.concatenate([group] * 3, axis=0)
    kept = jnp.where(group == groups, taken, 0.0).astype(BF16)
    lane = iota((height, 128), 1)
    size = 126 // count
    value = value_rows(count, lane.astype(F32) - quotient(lane, size) * size)
    fold = one_hot(jnp.logical_and(iota((height, 128), 0).astype(F32) == value, lane < 126))
    vectors = dot_nn(jnp.concatenate([fold] * 3, axis=1), kept)
    column = iota((1, total), 1)
    inner = column.astype(F32) - quotient(column, rows) * rows
    sums = []
    for index in range(scalars):
        line = turned[126 + index % 2 : 127 + index % 2]
        sums.append(
            jnp.sum(jnp.where(inner == float(index // 2), line, 0.0), axis=1, keepdims=True)
        )
    return vectors, sums


def wide(index):
    return index >= 2


def layout(index):
    return (2 * ROWS, PAIRS) if wide(index) else (ROWS, GROUP)


def step_kernel(
    index, got_ref, source_ref, place_ref, rank_ref, cells_ref, diagonal_ref, lower_ref, state_ref, far_ref,
    state_out, far_out, send_ref,
):
    rows, count = layout(index)
    part = quotient(place_ref[...], count)
    places, groups = source_ref[...] * rows + part, place_ref[...] - part * count
    arrived, sums = read_rows(
        got_ref[...], rows, count, places, groups, 32 if wide(index) else 16, 4 if index else 1
    )
    cam_dev = cells_ref.shape[2]
    step, rest, scaled, direction = (state_ref[i] for i in range(4))
    if index:
        image, image_scaled = state_ref[4], state_ref[5]
        energy, cross, square, old = sums
        alpha = old / energy
        beta = (old - 2.0 * alpha * cross + alpha * alpha * square) / old
        step = step + alpha * direction
        rest = rest - alpha * image
        direction = (scaled - alpha * image_scaled) + beta * direction
        far_before = arrived[16:] if wide(index) else far_ref[...]
        far = (far_before - alpha * arrived[:16]) + beta * far_ref[...]
    else:
        far = arrived
    image = multiply(cells_ref, diagonal_ref, far, direction)
    energy = total_of(direction * image)
    state_out[0] = step
    state_out[1] = rest
    state_out[3] = direction
    state_out[4] = image
    state_out[6] = state_ref[6] if index else jnp.zeros_like(step) + sums[0]
    far_out[...] = far
    if index == ITERS - 1:
        scaled = solve(lower_ref, rest)
        state_out[2] = scaled
        state_out[5] = jnp.zeros_like(image)
        lane = iota((rank_ref.shape[0], cam_dev), 1).astype(F32)

        def wanted(slot):
            if slot < OBS_CAP:
                return one_hot(rank_ref[:, slot : slot + 1] == lane)
            return jnp.zeros(lane.shape, BF16)

        both = jnp.concatenate([step, direction], axis=0)
        send_rows(send_ref, both, PAIRS, wanted, PAIR_ROWS, [energy, total_of(rest * scaled)])
        return
    solved = solve(lower_ref, jnp.concatenate([rest, image], axis=1))
    scaled, image_scaled = solved[:, :cam_dev], solved[:, cam_dev:]
    state_out[2] = scaled
    state_out[5] = image_scaled
    scalars = [
        energy, total_of(scaled * image), total_of(image * image_scaled), total_of(rest * scaled)
    ]
    rows, count = layout(index + 1)
    vector = jnp.concatenate([image_scaled, scaled], axis=0) if wide(index + 1) else image_scaled
    send_rows(send_ref, vector, count, ranked(rank_ref), rows, scalars)


def finish_kernel(
    got_ref, place_ref, state_ref, jc_ref, jp_ref, rs_ref, vi_ref, used_ref, step_ref, rest_ref, point_ref
):
    npts = used_ref.shape[1]
    places = jnp.concatenate([place_ref[a : a + 1, :] for a in range(TRACK)], axis=1)
    groups = jnp.concatenate([place_ref[TRACK + a : TRACK + a + 1, :] for a in range(TRACK)], axis=1)
    seen, sums = read_rows(got_ref[...], PAIR_ROWS, PAIRS, places, groups, 32, 2)
    alpha = sums[1] / sums[0]
    step_ref[...] = (state_ref[0] + alpha * state_ref[3])[:9]
    rest_ref[...] = (state_ref[1] - alpha * state_ref[4])[:9]
    moved = seen[:16] + alpha * seen[16:]
    reduced = [jnp.zeros((1, npts), F32) for _ in range(3)]
    for a in range(TRACK):
        live = used_ref[a : a + 1, :].astype(F32)
        there = moved[:9, a * npts : (a + 1) * npts]
        for u in range(2):
            change = jnp.sum(jc_ref[9 * u : 9 * u + 9, a, :] * there, axis=0, keepdims=True)
            change = live * (change + rs_ref[a, u : u + 1, :])
            for x in range(3):
                reduced[x] = reduced[x] - jp_ref[3 * u + x : 3 * u + x + 1, a, :] * change
    for x in range(3):
        point_ref[x : x + 1, :] = sum(
            vi_ref[3 * x + y : 3 * x + y + 1, :] * reduced[y] for y in range(3)
        )


def factor_blocks(matrix):
    lower = {}
    for row_idx in range(9):
        for col_idx in range(row_idx + 1):
            accum = matrix[row_idx, col_idx]
            for inner_idx in range(col_idx):
                accum = accum - lower[row_idx, inner_idx] * lower[col_idx, inner_idx]
            if row_idx == col_idx:
                lower[row_idx, row_idx] = jnp.sqrt(accum)
            else:
                lower[row_idx, col_idx] = accum / lower[col_idx, col_idx]
    return lower


def solve_blocks(lower, vector):
    forward = []
    for row_idx in range(9):
        accum = vector[row_idx]
        for inner_idx in range(row_idx):
            accum = accum - lower[row_idx, inner_idx] * forward[inner_idx]
        forward.append(accum / lower[row_idx, row_idx])
    backward = [None] * 9
    for row_idx in reversed(range(9)):
        accum = forward[row_idx]
        for inner_idx in range(row_idx + 1, 9):
            accum = accum - lower[inner_idx, row_idx] * backward[inner_idx]
        backward[row_idx] = accum / lower[row_idx, row_idx]
    return jnp.stack(backward)


def whole_exchange(cells, diagonal, pattern, jacobian_cam, jacobian_pt, residuals, point_inverse, obs_camera, used):
    cam_dev = pattern.shape[1]
    cells = jnp.concatenate([cells, diagonal[None]], axis=0)
    main = cells[:, :64].reshape(NBR + 1, 8, 8, cam_dev)
    side = cells[:, 72:80].reshape(NBR + 1, 8, 1, cam_dev)
    foot = jnp.concatenate([cells[:, 64:72], cells[:, 80:81]], axis=1)[:, None]
    blocks = jnp.concatenate([jnp.concatenate([main, side], axis=2), foot], axis=1)
    gradient = jnp.concatenate([cells[NBR, 88:96], cells[NBR, 81:82]], axis=0)
    lower = factor_blocks(blocks[NBR])

    def gathered(vector):
        return lax.all_gather(vector, BOTH, axis=1, tiled=True)

    def summed(values):
        return lax.psum(jnp.sum(values), BOTH)

    step = jnp.zeros_like(gradient)
    rest = gradient
    scaled = solve_blocks(lower, rest)
    direction = scaled
    energy_now = summed(rest * scaled)
    for _ in range(ITERS):
        taken = jnp.concatenate([gathered(direction)[:, pattern], direction[:, None, :]], axis=1)
        image = jnp.sum(blocks * jnp.swapaxes(taken, 0, 1)[:, None], axis=(0, 2))
        alpha = energy_now / summed(direction * image)
        step = step + alpha * direction
        rest = rest - alpha * image
        scaled = solve_blocks(lower, rest)
        energy_next = summed(rest * scaled)
        direction = scaled + energy_next / energy_now * direction
        energy_now = energy_next
    whole = gathered(step)
    npts = obs_camera.shape[1]
    rows = jacobian_cam.reshape(TRACK, 2, 9, npts)
    seen = jnp.swapaxes(whole[:, obs_camera], 0, 1)
    change = jnp.sum(rows * seen[:, None], axis=2) + residuals
    change = change * used.astype(F32)[:, None]
    reduced = -jnp.sum(jacobian_pt.reshape(TRACK, 2, 3, npts) * change[:, :, None], axis=(0, 1))
    point_step = jnp.sum(point_inverse.reshape(3, 3, npts) * reduced[None], axis=1)
    return step, rest, point_step


def shape(*dims, dtype=F32):
    return jax.ShapeDtypeStruct(dims, dtype)


def call(kernel, outs, name, scratch=(), flops=0):
    cost = pl.CostEstimate(flops=flops, bytes_accessed=1 << 20, transcendentals=0) if flops else None
    return pl.pallas_call(
        kernel, out_shape=outs, name=name, compiler_params=PARAMS, scratch_shapes=list(scratch),
        cost_estimate=cost,
    )


def exchange(message, devices):
    width = message.shape[0] // devices
    arrived = lax.all_to_all(
        message.reshape(devices, width, 1, 128), BOTH, split_axis=0, concat_axis=0, tiled=True
    )
    return arrived.reshape(devices * width, 128)


def per_device(
    jacobian_cam, jacobian_pt, residuals, point_inverse, obs_camera, pair_slot, observation_used, pattern,
):
    devices = lax.axis_size("cam") * lax.axis_size("pt")
    npts = obs_camera.shape[1]
    cam_dev = pattern.shape[1]
    shift = cam_dev.bit_length() - 1
    couplings = NBR * cam_dev

    cameras = jnp.transpose(jacobian_cam, (1, 0, 2))
    points = jnp.transpose(jacobian_pt, (1, 0, 2))

    packed, places, rank = call(
        functools.partial(pack_kernel, devices, shift),
        (shape(devices * 10, 128), shape(2 * TRACK, npts), shape(devices, cam_dev)),
        "pack",
        [pltpu.VMEM((80, TRACK * npts), F32)],
    )(cameras, points, residuals, point_inverse, obs_camera, pair_slot, observation_used, pattern)
    got = exchange(packed, devices)
    sources, far_rank = call(
        functools.partial(place_kernel, devices, shift),
        (shape(1, couplings), shape(1, couplings)),
        "place",
        flops=4 * 10**9,
    )(pattern)
    text, diagonal, lower, state, message = call(
        diagonal_kernel,
        (
            shape(OBS_CAP // 2, 80, 2 * devices),
            shape(CELL, cam_dev),
            shape(9, 16, cam_dev),
            shape(7, 16, cam_dev),
            shape(devices * ROWS, 128),
        ),
        "diagonal",
    )(got, rank)
    cells, wanted = call(
        coupling_kernel,
        (shape(NBR, CELL, cam_dev), shape(devices, 128)),
        "coupling",
        flops=8 * 10**9,
    )(text)
    far = jnp.zeros((16, couplings), F32)
    crowded = None
    for index in range(ITERS):
        last = index == ITERS - 1
        rows = PAIR_ROWS if last else layout(index + 1)[0]
        arrived = exchange(message, devices)
        state, far, message = call(
            functools.partial(step_kernel, index),
            (shape(7, 16, cam_dev), shape(16, couplings), shape(devices * rows, 128)),
            "step",
        )(
            arrived, sources, far_rank, wanted if last else rank, cells, diagonal, lower, state, far
        )
        if index == 0:
            crowded = state[6, 0, 0] > 0.0
    arrived = exchange(message, devices)
    found = call(
        finish_kernel, (shape(9, cam_dev), shape(9, cam_dev), shape(3, npts)), "finish"
    )(arrived, places, state, cameras, points, residuals, point_inverse, observation_used)

    def dense():
        return whole_exchange(
            cells, diagonal, pattern, jacobian_cam, jacobian_pt, residuals, point_inverse, obs_camera, observation_used
        )

    return lax.cond(crowded, dense, lambda: tuple(found))


def solution(mesh):
    return jax.shard_map(
        per_device,
        mesh=mesh,
        in_specs=(
            P(None, None, BOTH),
            P(None, None, BOTH),
            P(None, None, BOTH),
            P(None, BOTH),
            P(None, BOTH),
            P(None, None, BOTH),
            P(None, BOTH),
            P(None, BOTH),
        ),
        out_specs=(P(None, BOTH), P(None, BOTH), P(None, BOTH)),
        check_vma=False,
    )
```

```python
import functools

import jax
import jax.numpy as jnp
from jax import lax
from jax.experimental import pallas as pl
from jax.experimental.pallas import tpu as pltpu
from jax.sharding import PartitionSpec as P

TRACK = 4
NBR = 12
ITERS = 4
OBS_CAP = 16
DAMPING = 1.0
BOTH = ("cam", "pt")

GROUP = 14
PAIRS = 7
ROWS = 2
SLOTS = GROUP * ROWS
CARRIED = 32
PAIR_ROWS = 3
CELL = 96
F32 = jnp.float32
BF16 = jnp.bfloat16
PARAMS = pltpu.CompilerParams(vmem_limit_bytes=28 * 1024 * 1024)


def iota(shape, dim):
    return lax.broadcasted_iota(jnp.int32, shape, dim)


def quotient(values, divisor):
    return jnp.floor((values.astype(F32) + 0.5) * (1.0 / divisor))


def pieces(values):
    high = values.astype(BF16)
    rest = values - high.astype(F32)
    middle = rest.astype(BF16)
    low = (rest - middle.astype(F32)).astype(BF16)
    return high, middle, low


def dot_nn(left, right):
    return lax.dot_general(left, right, (((1,), (0,)), ((), ())), preferred_element_type=F32)


def dot_nt(left, right):
    return lax.dot_general(left, right, (((1,), (1,)), ((), ())), preferred_element_type=F32)


def one_hot(condition):
    return jnp.where(condition, 1.0, 0.0).astype(BF16)


def before(size):
    return one_hot(iota((size, size), 0) < iota((size, size), 1))


def flat(array):
    tracks, rows, npts = array.shape
    tiles = jnp.transpose(array, (1, 0, 2)).reshape(rows, tracks, npts // 128, 128)
    return jnp.transpose(tiles, (0, 2, 1, 3)).reshape(-1, 128)


def lines(ref, a, first, count, npts):
    tiles = npts // 128
    step = TRACK * tiles
    return jnp.concatenate(
        [ref[pl.ds(step * first + TRACK * t + a, count, stride=step), :] for t in range(tiles)], axis=1
    )


def pack_kernel(
    devices, shift, jc_ref, jp_ref, rs_ref, vi_ref, cam_ref, slot_ref, used_ref, pattern_ref,
    out_ref, place_ref, rank_ref, back_ref, feat_ref,
):
    npts = cam_ref.shape[1]
    cam_dev = pattern_ref.shape[1]
    found = jnp.zeros((devices, cam_dev), F32)
    for k in range(NBR):
        target = lax.shift_right_logical(pattern_ref[k : k + 1, :], shift)
        found = jnp.where(iota((devices, cam_dev), 0) == target, 1.0, found)
    rank = dot_nn(found.astype(BF16), before(cam_dev))
    rank_ref[...] = jnp.where(found > 0, rank, -1.0e6)
    back = SLOTS - 1.0 - rank
    most = jnp.sum(found, axis=1, keepdims=True)
    back_ref[...] = jnp.where(jnp.logical_and(found > 0, back >= most), back, -1.0e6)

    live = [used_ref[a : a + 1, :].astype(F32) for a in range(TRACK)]
    carry = jnp.zeros((devices, 1), F32)
    triangle = before(npts)
    hits = []
    withins = []
    for a in range(TRACK):
        owner = lax.shift_right_logical(cam_ref[a : a + 1, :], shift)
        hit = jnp.where(
            jnp.logical_and(iota((devices, npts), 0) == owner, live[a] > 0), 1.0, 0.0
        )
        hits.append(hit.astype(BF16))
        count = dot_nn(hits[a], triangle) + carry
        within = jnp.sum(hit * count, axis=0, keepdims=True)
        carry = carry + jnp.sum(hit, axis=1, keepdims=True)
        withins.append(within)
        part = quotient(within, PAIRS)
        place_ref[a : a + 1, :] = jnp.where(live[a] > 0, owner.astype(F32) * PAIR_ROWS + part, -1.0)
        place_ref[TRACK + a : TRACK + a + 1, :] = within - part * PAIRS

    vi = [[vi_ref[3 * x + y : 3 * x + y + 1, :] for y in range(3)] for x in range(3)]
    jp = [
        [[gradient[3 * u + x : 3 * u + x + 1] for x in range(3)] for u in range(2)]
        for gradient in [lines(jp_ref, a, 0, 6, npts) for a in range(TRACK)]
    ]
    jc = [lines(jc_ref, a, 0, 18, npts) for a in range(TRACK)]
    res = [[rs_ref[a, u : u + 1, :] for u in range(2)] for a in range(TRACK)]
    grad = []
    for x in range(3):
        total = jnp.zeros((1, npts), F32)
        for a in range(TRACK):
            total = total - live[a] * (jp[a][0][x] * res[a][0] + jp[a][1][x] * res[a][1])
        grad.append(total)
    for a in range(TRACK):
        at = slice(a * npts, (a + 1) * npts)
        for u in range(2):
            feat_ref[8 * u : 8 * u + 8, at] = jc[a][9 * u : 9 * u + 8]
            feat_ref[64 + u : 65 + u, at] = jc[a][9 * u + 8 : 9 * u + 9]
        removed = [
            [live[a] * sum(jp[a][u][x] * vi[x][y] for x in range(3)) for y in range(3)]
            for u in range(2)
        ]

        def middle(b, u, v):
            return -live[b] * sum(removed[u][y] * jp[b][v][y] for y in range(3))

        partners = [b for b in range(TRACK) if b != a]
        for m, b in enumerate(partners):
            first = [jc[b][9 * v : 9 * v + 8] for v in range(2)]
            ninth = [jc[b][9 * v + 8 : 9 * v + 9] for v in range(2)]
            for u in range(2):
                row = 2 + 2 * m + u
                one, two = middle(b, u, 0), middle(b, u, 1)
                feat_ref[8 * row : 8 * row + 8, at] = one * first[0] + two * first[1]
                feat_ref[64 + row : 65 + row, at] = one * ninth[0] + two * ninth[1]
        feat_ref[72:73, at] = live[a] + middle(a, 0, 0)
        feat_ref[73:74, at] = middle(a, 0, 1)
        feat_ref[74:75, at] = live[a] + middle(a, 1, 1)
        for u in range(2):
            right = -(live[a] * res[a][u] + sum(removed[u][y] * grad[y] for y in range(3)))
            feat_ref[75 + u : 76 + u, at] = right
        own = cam_ref[a : a + 1, :] & (cam_dev - 1)
        for m, b in enumerate(partners):
            label = slot_ref[a, b : b + 1, :] * cam_dev + own
            feat_ref[77 + m : 78 + m, at] = label.astype(F32)

    owners = jnp.concatenate(hits, axis=1)
    place = jnp.concatenate(withins, axis=1)
    split = pieces(feat_ref[...])
    masks = [
        one_hot(jnp.broadcast_to(place, (16, TRACK * npts)) == float(s)) for s in range(OBS_CAP)
    ]
    for g in range(5):
        right = jnp.concatenate(
            [
                part[16 * g : 16 * g + 16] * masks[8 * h + c]
                for h in range(2) for part in split for c in range(8)
            ],
            axis=0,
        )
        sums = dot_nt(owners, right)
        for h in range(2):
            mine = sums[:, 384 * h : 384 * h + 384]
            out_ref[pl.ds(2 * g + h, devices, stride=10), :] = (
                mine[:, :128] + mine[:, 128:256] + mine[:, 256:]
            )


def place_kernel(devices, shift, pattern_ref, source_ref, far_ref, back_ref):
    cam_dev = pattern_ref.shape[1]
    count = jnp.zeros((devices, cam_dev), F32)
    sources = []
    withins = []
    for k in range(NBR):
        camera = pattern_ref[k : k + 1, :]
        source = lax.shift_right_logical(camera, shift)
        within = camera & (cam_dev - 1)
        sources.append(iota((devices, cam_dev), 0) == source)
        withins.append(iota((cam_dev, cam_dev), 0) == within)
        count = count + dot_nt(one_hot(sources[k]), one_hot(withins[k]))
        source_ref[:, k * cam_dev : (k + 1) * cam_dev] = source.astype(F32)
    found = one_hot(count > 0)
    rank = dot_nn(found, before(cam_dev))
    most = jnp.sum(found.astype(F32), axis=1, keepdims=True)
    turned = rank.T.astype(BF16)
    for k in range(NBR):
        column = dot_nn(turned, one_hot(sources[k]))
        mine = jnp.sum(jnp.where(withins[k], column, 0.0), axis=0, keepdims=True)
        far_ref[:, k * cam_dev : (k + 1) * cam_dev] = mine
        full = jnp.sum(jnp.where(sources[k], most, 0.0), axis=0, keepdims=True)
        back = SLOTS - 1.0 - mine
        back_ref[:, k * cam_dev : (k + 1) * cam_dev] = jnp.where(back >= full, back, -1.0)


def outer(left, right, extra):
    blocks = []
    for r in range(8):
        blocks.append(left[0][0][r : r + 1] * right[0][0] + left[1][0][r : r + 1] * right[1][0])
    blocks.append(left[0][1] * right[0][0] + left[1][1] * right[1][0])
    blocks.append(left[0][0] * right[0][1] + left[1][0] * right[1][1])
    corner = left[0][1] * right[0][1] + left[1][1] * right[1][1]
    chunk = corner.shape[1]
    if extra is None:
        blocks.append(jnp.concatenate([corner, jnp.zeros((7, chunk), F32)], axis=0))
        blocks.append(jnp.zeros((8, chunk), F32))
    else:
        last = left[0][1] * extra[0] + left[1][1] * extra[1]
        blocks.append(jnp.concatenate([corner, last, jnp.zeros((6, chunk), F32)], axis=0))
        blocks.append(left[0][0] * extra[0] + left[1][0] * extra[1])
    return jnp.concatenate(blocks, axis=0)


def observation(text, cam_dev):
    vectors = [(text[8 * v : 8 * v + 8], text[64 + v : 65 + v]) for v in range(8)]
    cells = [quotient(text[77 + m : 78 + m], cam_dev) for m in range(3)]
    within = text[77:78] - cells[0] * cam_dev
    hit = one_hot(iota((cam_dev, text.shape[1]), 0).astype(F32) == within)
    return vectors, cells, within, hit


def folded(sums):
    return sums[:CELL] + sums[CELL : 2 * CELL] + sums[2 * CELL :]


def diagonal_kernel(
    got_ref, rank_ref, back_ref, text_ref, out_ref, lower_ref, state_ref, send_ref
):
    devices = got_ref.shape[0] // 10
    cam_dev = out_ref.shape[1]
    for h in range(2):
        for g in range(5):
            turned = got_ref[pl.ds(2 * g + h, devices, stride=10), :].T
            for c in range(8):
                at = slice((c % 2) * devices, (c % 2 + 1) * devices)
                text_ref[4 * h + c // 2, 16 * g : 16 * g + 16, at] = turned[16 * c : 16 * c + 16]
    unit = iota((CELL, cam_dev), 0)
    unit = jnp.logical_and(unit <= 63, unit == 9 * lax.shift_right_logical(unit, 3)) | (unit == 80)
    total = jnp.where(unit, DAMPING, 0.0)
    for index in range(OBS_CAP // 2):
        text = text_ref[index]
        vectors, _, _, hit = observation(text, cam_dev)
        own = vectors[0:2]
        corner = [[text[72:73], text[73:74]], [text[73:74], text[74:75]]]
        weighted = [
            tuple(corner[u][0] * own[0][i] + corner[u][1] * own[1][i] for i in range(2)) for u in range(2)
        ]
        term = outer(own, weighted, [text[75:76], text[76:77]])
        total = total + folded(dot_nt(jnp.concatenate(pieces(term), axis=0), hit))
    out_ref[...] = total
    cholesky(out_ref, lower_ref)
    right = jnp.concatenate([total[88:96], total[81:82], jnp.zeros((7, cam_dev), F32)], axis=0)
    scaled = solve(lower_ref, right)
    zero = jnp.zeros_like(right)
    state_ref[0] = zero
    state_ref[1] = right
    state_ref[2] = scaled
    state_ref[3] = scaled
    for index in range(4, 7):
        state_ref[index] = zero
    most = jnp.max(jnp.max(rank_ref[...], axis=1, keepdims=True), axis=0, keepdims=True)
    single = jnp.logical_and(rank_ref[...] >= 0, back_ref[...] < 0)
    carried = total_of(jnp.where(single, 1.0, 0.0))
    crowded = jnp.where(jnp.logical_or(most >= float(SLOTS), carried > float(CARRIED)), 1.0, 0.0)
    send_rows(send_ref, [coupled(scaled, rank_ref)], ROWS, [crowded])


def coupling_kernel(text_ref, lower_ref, out_ref, wanted_ref, inverse_ref):
    cam_dev = out_ref.shape[2]
    devices = wanted_ref.shape[0]
    out_ref[...] = jnp.zeros_like(out_ref)

    def step(index, _):
        vectors, cells, _, hit = observation(text_ref[index], cam_dev)
        terms = [
            jnp.concatenate(pieces(outer(vectors[0:2], vectors[2 + 2 * m : 4 + 2 * m], None)), axis=0)
            for m in range(3)
        ]
        for k in range(NBR):
            part = None
            for m in range(3):
                piece = terms[m] * one_hot(cells[m] == float(k))
                part = piece if part is None else part + piece
            out_ref[k] = out_ref[k] + folded(dot_nt(part, hit))
        return 0

    lax.fori_loop(0, OBS_CAP // 2, step, 0)
    labels = []
    for s in range(OBS_CAP):
        label = text_ref[s // 2, 77:78, (s % 2) * devices : (s % 2 + 1) * devices]
        labels.append(label - cam_dev * quotient(label, cam_dev))
    labels.append(jnp.zeros((128 - OBS_CAP, devices), F32))
    wanted_ref[...] = jnp.concatenate(labels, axis=0).T
    row = iota((16, 9 * cam_dev), 0)
    unit = lax.shift_right_logical(iota((16, 9 * cam_dev), 1), cam_dev.bit_length() - 1) == row
    solved = solve(lower_ref, jnp.where(unit, 1.0, 0.0))
    columns = [solved[:, c * cam_dev : (c + 1) * cam_dev] for c in range(9)]
    inverse_ref[...] = jnp.concatenate(
        [column[:8] for column in columns] + [columns[8][:8], columns[8][8:], jnp.zeros((8, cam_dev), F32)],
        axis=0,
    )


def cholesky(cells_ref, lower_ref):
    cam_dev = cells_ref.shape[1]
    zero = jnp.zeros((7, cam_dev), F32)
    block = cells_ref[...]
    columns = [
        jnp.concatenate([block[8 * r : 8 * r + 8], block[64 + r : 65 + r], zero], axis=0) for r in range(8)
    ]
    columns.append(jnp.concatenate([block[64:72], block[80:81], zero], axis=0))
    row = iota((16, cam_dev), 0)
    for c in range(9):
        pivot = columns[c][c : c + 1]
        root = jnp.sqrt(pivot)
        inverse = 1.0 / root
        column = jnp.where(row > c, columns[c] * inverse, 0.0)
        for r in range(c + 1, 9):
            columns[r] = columns[r] - column * column[r : r + 1]
        lower_ref[c] = jnp.where(row == 9, inverse, jnp.where(row < 9, column, 0.0))


def solve(lower_ref, vector):
    row = iota(vector.shape, 0)
    rest = vector
    copies = vector.shape[1] // lower_ref.shape[2]
    columns = [jnp.concatenate([lower_ref[c]] * copies, axis=1) for c in range(9)]
    for c in range(9):
        column = columns[c]
        value = rest[c : c + 1] * column[9:10]
        rest = jnp.where(row == c, value, rest - jnp.where(row < 9, column, 0.0) * value)
    for c in reversed(range(9)):
        column = columns[c]
        if c < 8:
            dotted = jnp.sum(
                jnp.where(jnp.logical_and(row > c, row < 9), column * rest, 0.0), axis=0, keepdims=True
            )
        else:
            dotted = jnp.zeros((1, vector.shape[1]), F32)
        value = (rest[c : c + 1] - dotted) * column[9:10]
        rest = jnp.where(row == c, value, rest)
    return rest


def multiply(pairs):
    cam_dev = pairs[0][1].shape[1]
    sums = [jnp.zeros((8, cam_dev), F32) for _ in range(9)]
    side = jnp.zeros((8, cam_dev), F32)
    corner = jnp.zeros((1, cam_dev), F32)
    for cell_ref, vector in pairs:
        first, last = vector[0:8], vector[8:9]
        for r in range(9):
            sums[r] = sums[r] + cell_ref[8 * r : 8 * r + 8, :] * first
        side = side + cell_ref[72:80, :] * last
        corner = corner + cell_ref[80:81, :] * last
    sums = [jnp.sum(part, axis=0, keepdims=True) for part in sums]
    top = jnp.concatenate(sums[:8], axis=0) + side
    return jnp.concatenate([top, sums[8] + corner, jnp.zeros((7, cam_dev), F32)], axis=0)


def total_of(values):
    return jnp.sum(jnp.sum(values, axis=1, keepdims=True), axis=0, keepdims=True)


def lane_plan():
    lane = iota((128, 1), 0)
    group = jnp.where(lane < 112, lax.shift_right_logical(lane, 3), lane - 112)
    return group, jnp.where(lane < 112, lane & 7, 8)


def spread(vector):
    cam_dev = vector.shape[1]
    choose = one_hot(iota((128, 16), 1) == lane_plan()[1])
    copies = dot_nn(choose, jnp.concatenate(pieces(vector), axis=1))
    return [copies[:, p * cam_dev : (p + 1) * cam_dev] for p in range(3)]


def coupled(vector, rank_ref):
    group, _ = lane_plan()
    rank = rank_ref[...]
    copies = spread(vector)
    right = [
        jnp.concatenate([jnp.where(group == g, part, 0.0) for g in range(GROUP)], axis=1) for part in copies
    ]
    left = [[one_hot(rank == float(GROUP * h + g)) for g in range(GROUP)] for h in range(ROWS)]
    return left, right


def observed(first, second, wanted_ref):
    group, _ = lane_plan()
    lane = iota((wanted_ref.shape[0], first.shape[1]), 1).astype(F32)
    right = [
        jnp.concatenate(
            [
                jnp.where(group == 2 * g, one, jnp.where(group == 2 * g + 1, two, 0.0))
                for g in range(PAIRS)
            ],
            axis=1,
        )
        for one, two in zip(spread(first), spread(second))
    ]
    empty = jnp.zeros(lane.shape, BF16)
    left = [
        [
            one_hot(wanted_ref[:, slot : slot + 1] == lane) if slot < OBS_CAP else empty
            for slot in range(PAIRS * h, PAIRS * h + PAIRS)
        ]
        for h in range(PAIR_ROWS)
    ]
    return left, right


def send_rows(send_ref, parts, rows, scalars):
    devices = send_ref.shape[0] // rows
    left = jnp.concatenate(
        [jnp.concatenate([hit for part in parts for hit in part[0][h]], axis=1) for h in range(rows)], axis=0
    )
    right = jnp.concatenate(
        [jnp.concatenate([part[1][p] for part in parts], axis=1) for p in range(3)], axis=0
    ).astype(BF16)
    sums = dot_nt(left, right)
    lane = iota((devices, 128), 1)
    for h in range(rows):
        mine = sums[h * devices : (h + 1) * devices]
        text = mine[:, :128] + mine[:, 128:256] + mine[:, 256:]
        for index, scalar in enumerate(scalars[2 * h : 2 * h + 2]):
            text = jnp.where(lane == 126 + index, scalar, text)
        send_ref[pl.ds(h, devices, stride=rows), :] = text


def read_rows(turned, places):
    mark = one_hot(iota((turned.shape[1], places.shape[1]), 0).astype(F32) == places)
    taken = dot_nn(jnp.concatenate(pieces(turned), axis=0), mark)
    return taken[:128] + taken[128:256] + taken[256:]


def pick(taken, groups):
    top = jnp.zeros((8, taken.shape[1]), F32)
    for g in range(GROUP):
        top = jnp.where(groups == float(g), taken[8 * g : 8 * g + 8], top)
    ninth = jnp.where(iota((16, taken.shape[1]), 0).astype(F32) == groups, taken[112:128], 0.0)
    ninth = jnp.sum(ninth, axis=0, keepdims=True)
    return jnp.concatenate([top, ninth, jnp.zeros((7, taken.shape[1]), F32)], axis=0)


def read_scalars(turned, rows, count):
    column = iota((1, turned.shape[1]), 1)
    inner = column.astype(F32) - quotient(column, rows) * rows
    sums = []
    for index in range(count):
        line = turned[126 + index % 2 : 127 + index % 2]
        sums.append(
            jnp.sum(jnp.where(inner == float(index // 2), line, 0.0), axis=1, keepdims=True)
        )
    return sums


def step_kernel(
    index, got_ref, source_ref, place_ref, second_ref, rank_ref, back_ref, cells_ref, diagonal_ref, inverse_ref,
    state_ref, far_ref, state_out, far_out, send_ref,
):
    turned = got_ref[...].T
    sums = read_scalars(turned, ROWS, 4 if index else 1)
    source = source_ref[...]
    part = quotient(place_ref[...], GROUP)
    places, groups = source * ROWS + part, place_ref[...] - part * GROUP
    couplings = places.shape[1]
    if index >= 2:
        part = quotient(jnp.maximum(second_ref[...], 0.0), GROUP)
        room = second_ref[...] >= 0
        places = jnp.concatenate([places, jnp.where(room, source * ROWS + part, -1.0)], axis=1)
        groups = jnp.concatenate([groups, second_ref[...] - part * GROUP], axis=1)
    arrived = pick(read_rows(turned, places), groups)
    step, rest, scaled, direction = (state_ref[i] for i in range(4))
    if index:
        image, image_scaled = state_ref[4], state_ref[5]
        energy, cross, square, old = sums
        alpha = old / energy
        beta = (old - 2.0 * alpha * cross + alpha * alpha * square) / old
        step = step + alpha * direction
        rest = rest - alpha * image
        direction = (scaled - alpha * image_scaled) + beta * direction
        far_before = far_ref[1]
        if index >= 2:
            far_before = jnp.where(room, arrived[:, couplings:], far_before)
        far_scaled = far_before - alpha * arrived[:, :couplings]
        far = far_scaled + beta * far_ref[0]
    else:
        far_scaled = arrived
        far = arrived
    cam_dev = cells_ref.shape[2]
    image = multiply(
        [(diagonal_ref, direction)]
        + [(cells_ref.at[k], far[:, k * cam_dev : (k + 1) * cam_dev]) for k in range(NBR)]
    )
    energy = total_of(direction * image)
    scaled = multiply([(inverse_ref, rest)]) if index else scaled
    old = total_of(rest * scaled)
    state_out[0] = step
    state_out[1] = rest
    state_out[2] = scaled
    state_out[3] = direction
    state_out[4] = image
    state_out[6] = state_ref[6] if index else jnp.zeros_like(step) + sums[0]
    far_out[0] = far
    far_out[1] = far_scaled
    if index == ITERS - 1:
        state_out[5] = jnp.zeros_like(image)
        send_rows(send_ref, [observed(step, direction, rank_ref)], PAIR_ROWS, [energy, old])
        return
    image_scaled = multiply([(inverse_ref, image)])
    state_out[5] = image_scaled
    parts = [coupled(image_scaled, rank_ref)]
    if index + 1 >= 2:
        parts.append(coupled(scaled, back_ref))
    scalars = [energy, total_of(scaled * image), total_of(image * image_scaled), old]
    send_rows(send_ref, parts, ROWS, scalars)


def finish_kernel(
    got_ref, place_ref, state_ref, jc_ref, jp_ref, rs_ref, vi_ref, used_ref, step_ref, rest_ref, point_ref
):
    npts = used_ref.shape[1]
    places = jnp.concatenate([place_ref[a : a + 1, :] for a in range(TRACK)], axis=1)
    groups = jnp.concatenate([place_ref[TRACK + a : TRACK + a + 1, :] for a in range(TRACK)], axis=1)
    turned = got_ref[...].T
    energy, old = read_scalars(turned, PAIR_ROWS, 2)
    alpha = old / energy
    step_ref[...] = (state_ref[0] + alpha * state_ref[3])[:9]
    rest_ref[...] = (state_ref[1] - alpha * state_ref[4])[:9]
    taken = read_rows(turned, places)
    moved = pick(taken, 2.0 * groups) + alpha * pick(taken, 2.0 * groups + 1.0)
    reduced = [jnp.zeros((1, npts), F32) for _ in range(3)]
    for a in range(TRACK):
        live = used_ref[a : a + 1, :].astype(F32)
        there = moved[:9, a * npts : (a + 1) * npts]
        jacobian = lines(jc_ref, a, 0, 18, npts)
        gradient = lines(jp_ref, a, 0, 6, npts)
        for u in range(2):
            change = jnp.sum(jacobian[9 * u : 9 * u + 9] * there, axis=0, keepdims=True)
            change = live * (change + rs_ref[a, u : u + 1, :])
            for x in range(3):
                reduced[x] = reduced[x] - gradient[3 * u + x : 3 * u + x + 1] * change
    for x in range(3):
        point_ref[x : x + 1, :] = sum(
            vi_ref[3 * x + y : 3 * x + y + 1, :] * reduced[y] for y in range(3)
        )


def factor_blocks(matrix):
    lower = {}
    for row_idx in range(9):
        for col_idx in range(row_idx + 1):
            accum = matrix[row_idx, col_idx]
            for inner_idx in range(col_idx):
                accum = accum - lower[row_idx, inner_idx] * lower[col_idx, inner_idx]
            if row_idx == col_idx:
                lower[row_idx, row_idx] = jnp.sqrt(accum)
            else:
                lower[row_idx, col_idx] = accum / lower[col_idx, col_idx]
    return lower


def solve_blocks(lower, vector):
    forward = []
    for row_idx in range(9):
        accum = vector[row_idx]
        for inner_idx in range(row_idx):
            accum = accum - lower[row_idx, inner_idx] * forward[inner_idx]
        forward.append(accum / lower[row_idx, row_idx])
    backward = [None] * 9
    for row_idx in reversed(range(9)):
        accum = forward[row_idx]
        for inner_idx in range(row_idx + 1, 9):
            accum = accum - lower[inner_idx, row_idx] * backward[inner_idx]
        backward[row_idx] = accum / lower[row_idx, row_idx]
    return jnp.stack(backward)


def whole_exchange(cells, diagonal, pattern, jacobian_cam, jacobian_pt, residuals, point_inverse, obs_camera, used):
    cam_dev = pattern.shape[1]
    cells = jnp.concatenate([cells, diagonal[None]], axis=0)
    main = cells[:, :64].reshape(NBR + 1, 8, 8, cam_dev)
    side = cells[:, 72:80].reshape(NBR + 1, 8, 1, cam_dev)
    foot = jnp.concatenate([cells[:, 64:72], cells[:, 80:81]], axis=1)[:, None]
    blocks = jnp.concatenate([jnp.concatenate([main, side], axis=2), foot], axis=1)
    gradient = jnp.concatenate([cells[NBR, 88:96], cells[NBR, 81:82]], axis=0)
    lower = factor_blocks(blocks[NBR])

    def gathered(vector):
        return lax.all_gather(vector, BOTH, axis=1, tiled=True)

    def summed(values):
        return lax.psum(jnp.sum(values), BOTH)

    step = jnp.zeros_like(gradient)
    rest = gradient
    scaled = solve_blocks(lower, rest)
    direction = scaled
    energy_now = summed(rest * scaled)
    for _ in range(ITERS):
        taken = jnp.concatenate([gathered(direction)[:, pattern], direction[:, None, :]], axis=1)
        image = jnp.sum(blocks * jnp.swapaxes(taken, 0, 1)[:, None], axis=(0, 2))
        alpha = energy_now / summed(direction * image)
        step = step + alpha * direction
        rest = rest - alpha * image
        scaled = solve_blocks(lower, rest)
        energy_next = summed(rest * scaled)
        direction = scaled + energy_next / energy_now * direction
        energy_now = energy_next
    whole = gathered(step)
    npts = obs_camera.shape[1]
    rows = jacobian_cam.reshape(TRACK, 2, 9, npts)
    seen = jnp.swapaxes(whole[:, obs_camera], 0, 1)
    change = jnp.sum(rows * seen[:, None], axis=2) + residuals
    change = change * used.astype(F32)[:, None]
    reduced = -jnp.sum(jacobian_pt.reshape(TRACK, 2, 3, npts) * change[:, :, None], axis=(0, 1))
    point_step = jnp.sum(point_inverse.reshape(3, 3, npts) * reduced[None], axis=1)
    return step, rest, point_step


def shape(*dims, dtype=F32):
    return jax.ShapeDtypeStruct(dims, dtype)


def call(kernel, outs, name, scratch=(), flops=0):
    cost = pl.CostEstimate(flops=flops, bytes_accessed=1 << 20, transcendentals=0) if flops else None
    return pl.pallas_call(
        kernel, out_shape=outs, name=name, compiler_params=PARAMS, scratch_shapes=list(scratch),
        cost_estimate=cost,
    )


def exchange(message, devices):
    width = message.shape[0] // devices
    arrived = lax.all_to_all(
        message.reshape(devices, width, 1, 128), BOTH, split_axis=0, concat_axis=0, tiled=True
    )
    return arrived.reshape(devices * width, 128)


def per_device(
    jacobian_cam, jacobian_pt, residuals, point_inverse, obs_camera, pair_slot, observation_used, pattern,
):
    devices = lax.axis_size("cam") * lax.axis_size("pt")
    npts = obs_camera.shape[1]
    cam_dev = pattern.shape[1]
    shift = cam_dev.bit_length() - 1
    couplings = NBR * cam_dev

    cameras = flat(jacobian_cam)
    points = flat(jacobian_pt)

    packed, places, rank, back = call(
        functools.partial(pack_kernel, devices, shift),
        (
            shape(devices * 10, 128), shape(2 * TRACK, npts), shape(devices, cam_dev), shape(devices, cam_dev),
        ),
        "pack",
        [pltpu.VMEM((80, TRACK * npts), F32)],
    )(cameras, points, residuals, point_inverse, obs_camera, pair_slot, observation_used, pattern)
    got = exchange(packed, devices)
    sources, far_rank, far_back = call(
        functools.partial(place_kernel, devices, shift),
        (shape(1, couplings), shape(1, couplings), shape(1, couplings)),
        "place",
        flops=4 * 10**9,
    )(pattern)
    text, diagonal, lower, state, message = call(
        diagonal_kernel,
        (
            shape(OBS_CAP // 2, 80, 2 * devices),
            shape(CELL, cam_dev),
            shape(9, 16, cam_dev),
            shape(7, 16, cam_dev),
            shape(devices * ROWS, 128),
        ),
        "diagonal",
    )(got, rank, back)
    cells, wanted, inverse = call(
        coupling_kernel,
        (shape(NBR, CELL, cam_dev), shape(devices, 128), shape(CELL, cam_dev)),
        "coupling",
        flops=8 * 10**9,
    )(text, lower)
    far = jnp.zeros((2, 16, couplings), F32)
    crowded = None
    for index in range(ITERS):
        last = index == ITERS - 1
        rows = PAIR_ROWS if last else ROWS
        arrived = exchange(message, devices)
        state, far, message = call(
            functools.partial(step_kernel, index),
            (shape(7, 16, cam_dev), shape(2, 16, couplings), shape(devices * rows, 128)),
            "step",
        )(
            arrived, sources, far_rank, far_back, wanted if last else rank, back, cells, diagonal, inverse,
            state, far,
        )
        if index == 0:
            crowded = state[6, 0, 0] > 0.0
    arrived = exchange(message, devices)
    found = call(
        finish_kernel, (shape(9, cam_dev), shape(9, cam_dev), shape(3, npts)), "finish"
    )(arrived, places, state, cameras, points, residuals, point_inverse, observation_used)

    def dense():
        return whole_exchange(
            cells, diagonal, pattern, jacobian_cam, jacobian_pt, residuals, point_inverse, obs_camera, observation_used
        )

    return lax.cond(crowded, dense, lambda: tuple(found))


def solution(mesh):
    return jax.shard_map(
        per_device,
        mesh=mesh,
        in_specs=(
            P(None, None, BOTH),
            P(None, None, BOTH),
            P(None, None, BOTH),
            P(None, BOTH),
            P(None, BOTH),
            P(None, None, BOTH),
            P(None, BOTH),
            P(None, BOTH),
        ),
        out_specs=(P(None, BOTH), P(None, BOTH), P(None, BOTH)),
        check_vma=False,
    )
```

```python
import functools

import jax
import jax.numpy as jnp
from jax import lax
from jax.experimental import pallas as pl
from jax.experimental.pallas import tpu as pltpu
from jax.sharding import PartitionSpec as P

TRACK = 4
NBR = 12
ITERS = 4
OBS_CAP = 16
DAMPING = 1.0
BOTH = ("cam", "pt")

GROUP = 14
PAIRS = 7
ROWS = 2
SLOTS = GROUP * ROWS
CARRIED = 32
PAIR_ROWS = 3
CELL = 96
F32 = jnp.float32
BF16 = jnp.bfloat16
PARAMS = pltpu.CompilerParams(vmem_limit_bytes=28 * 1024 * 1024)


def iota(shape, dim):
    return lax.broadcasted_iota(jnp.int32, shape, dim)


def quotient(values, divisor):
    return jnp.floor((values.astype(F32) + 0.5) * (1.0 / divisor))


def pieces(values):
    high = values.astype(BF16)
    rest = values - high.astype(F32)
    middle = rest.astype(BF16)
    low = (rest - middle.astype(F32)).astype(BF16)
    return high, middle, low


def dot_nn(left, right):
    return lax.dot_general(left, right, (((1,), (0,)), ((), ())), preferred_element_type=F32)


def dot_nt(left, right):
    return lax.dot_general(left, right, (((1,), (1,)), ((), ())), preferred_element_type=F32)


def one_hot(condition):
    return jnp.where(condition, 1.0, 0.0).astype(BF16)


def before(size):
    return one_hot(iota((size, size), 0) < iota((size, size), 1))


def flat(array):
    tracks, rows, npts = array.shape
    tiles = jnp.transpose(array, (1, 0, 2)).reshape(rows, tracks, npts // 128, 128)
    return jnp.transpose(tiles, (0, 2, 1, 3)).reshape(-1, 128)


def lines(ref, a, first, count, npts):
    tiles = npts // 128
    step = TRACK * tiles
    return jnp.concatenate(
        [ref[pl.ds(step * first + TRACK * t + a, count, stride=step), :] for t in range(tiles)], axis=1
    )


def pack_kernel(
    devices, shift, jc_ref, jp_ref, rs_ref, vi_ref, cam_ref, slot_ref, used_ref, pattern_ref,
    out_ref, place_ref, rank_ref, back_ref, feat_ref,
):
    npts = cam_ref.shape[1]
    cam_dev = pattern_ref.shape[1]
    found = jnp.zeros((devices, cam_dev), F32)
    for k in range(NBR):
        target = lax.shift_right_logical(pattern_ref[k : k + 1, :], shift)
        found = jnp.where(iota((devices, cam_dev), 0) == target, 1.0, found)
    rank = dot_nn(found.astype(BF16), before(cam_dev))
    rank_ref[...] = jnp.where(found > 0, rank, -1.0e6)
    back = SLOTS - 1.0 - rank
    most = jnp.sum(found, axis=1, keepdims=True)
    back_ref[...] = jnp.where(jnp.logical_and(found > 0, back >= most), back, -1.0e6)

    live = [used_ref[a : a + 1, :].astype(F32) for a in range(TRACK)]
    carry = jnp.zeros((devices, 1), F32)
    triangle = before(npts)
    hits = []
    withins = []
    for a in range(TRACK):
        owner = lax.shift_right_logical(cam_ref[a : a + 1, :], shift)
        hit = jnp.where(
            jnp.logical_and(iota((devices, npts), 0) == owner, live[a] > 0), 1.0, 0.0
        )
        hits.append(hit.astype(BF16))
        count = dot_nn(hits[a], triangle) + carry
        within = jnp.sum(hit * count, axis=0, keepdims=True)
        carry = carry + jnp.sum(hit, axis=1, keepdims=True)
        withins.append(within)
        part = quotient(within, PAIRS)
        place_ref[a : a + 1, :] = jnp.where(live[a] > 0, owner.astype(F32) * PAIR_ROWS + part, -1.0)
        place_ref[TRACK + a : TRACK + a + 1, :] = within - part * PAIRS

    vi = [[vi_ref[3 * x + y : 3 * x + y + 1, :] for y in range(3)] for x in range(3)]
    jp = [
        [[gradient[3 * u + x : 3 * u + x + 1] for x in range(3)] for u in range(2)]
        for gradient in [lines(jp_ref, a, 0, 6, npts) for a in range(TRACK)]
    ]
    jc = [lines(jc_ref, a, 0, 18, npts) for a in range(TRACK)]
    res = [[rs_ref[a, u : u + 1, :] for u in range(2)] for a in range(TRACK)]
    grad = []
    for x in range(3):
        total = jnp.zeros((1, npts), F32)
        for a in range(TRACK):
            total = total - live[a] * (jp[a][0][x] * res[a][0] + jp[a][1][x] * res[a][1])
        grad.append(total)
    for a in range(TRACK):
        at = slice(a * npts, (a + 1) * npts)
        for u in range(2):
            feat_ref[8 * u : 8 * u + 8, at] = jc[a][9 * u : 9 * u + 8]
            feat_ref[64 + u : 65 + u, at] = jc[a][9 * u + 8 : 9 * u + 9]
        removed = [
            [live[a] * sum(jp[a][u][x] * vi[x][y] for x in range(3)) for y in range(3)]
            for u in range(2)
        ]

        def middle(b, u, v):
            return -live[b] * sum(removed[u][y] * jp[b][v][y] for y in range(3))

        partners = [b for b in range(TRACK) if b != a]
        for m, b in enumerate(partners):
            first = [jc[b][9 * v : 9 * v + 8] for v in range(2)]
            ninth = [jc[b][9 * v + 8 : 9 * v + 9] for v in range(2)]
            for u in range(2):
                row = 2 + 2 * m + u
                one, two = middle(b, u, 0), middle(b, u, 1)
                feat_ref[8 * row : 8 * row + 8, at] = one * first[0] + two * first[1]
                feat_ref[64 + row : 65 + row, at] = one * ninth[0] + two * ninth[1]
        feat_ref[72:73, at] = live[a] + middle(a, 0, 0)
        feat_ref[73:74, at] = middle(a, 0, 1)
        feat_ref[74:75, at] = live[a] + middle(a, 1, 1)
        for u in range(2):
            right = -(live[a] * res[a][u] + sum(removed[u][y] * grad[y] for y in range(3)))
            feat_ref[75 + u : 76 + u, at] = right
        own = cam_ref[a : a + 1, :] & (cam_dev - 1)
        for m, b in enumerate(partners):
            label = slot_ref[a, b : b + 1, :] * cam_dev + own
            feat_ref[77 + m : 78 + m, at] = label.astype(F32)

    owners = jnp.concatenate(hits, axis=1)
    place = jnp.concatenate(withins, axis=1)
    split = pieces(feat_ref[...])
    masks = [
        one_hot(jnp.broadcast_to(place, (16, TRACK * npts)) == float(s)) for s in range(OBS_CAP)
    ]
    for g in range(5):
        right = jnp.concatenate(
            [
                part[16 * g : 16 * g + 16] * masks[8 * h + c]
                for h in range(2) for part in split for c in range(8)
            ],
            axis=0,
        )
        sums = dot_nt(owners, right)
        for h in range(2):
            mine = sums[:, 384 * h : 384 * h + 384]
            out_ref[pl.ds(2 * g + h, devices, stride=10), :] = (
                mine[:, :128] + mine[:, 128:256] + mine[:, 256:]
            )


def place_kernel(devices, shift, pattern_ref, source_ref, far_ref, back_ref):
    cam_dev = pattern_ref.shape[1]
    count = jnp.zeros((devices, cam_dev), F32)
    sources = []
    withins = []
    for k in range(NBR):
        camera = pattern_ref[k : k + 1, :]
        source = lax.shift_right_logical(camera, shift)
        within = camera & (cam_dev - 1)
        sources.append(iota((devices, cam_dev), 0) == source)
        withins.append(iota((cam_dev, cam_dev), 0) == within)
        count = count + dot_nt(one_hot(sources[k]), one_hot(withins[k]))
        source_ref[:, k * cam_dev : (k + 1) * cam_dev] = source.astype(F32)
    found = one_hot(count > 0)
    rank = dot_nn(found, before(cam_dev))
    most = jnp.sum(found.astype(F32), axis=1, keepdims=True)
    turned = rank.T.astype(BF16)
    for k in range(NBR):
        column = dot_nn(turned, one_hot(sources[k]))
        mine = jnp.sum(jnp.where(withins[k], column, 0.0), axis=0, keepdims=True)
        far_ref[:, k * cam_dev : (k + 1) * cam_dev] = mine
        full = jnp.sum(jnp.where(sources[k], most, 0.0), axis=0, keepdims=True)
        back = SLOTS - 1.0 - mine
        back_ref[:, k * cam_dev : (k + 1) * cam_dev] = jnp.where(back >= full, back, -1.0)


def outer(left, right):
    blocks = []
    for r in range(8):
        blocks.append(left[0][0][r : r + 1] * right[0][0] + left[1][0][r : r + 1] * right[1][0])
    blocks.append(left[0][1] * right[0][0] + left[1][1] * right[1][0])
    blocks.append(left[0][0] * right[0][1] + left[1][0] * right[1][1])
    return blocks, left[0][1] * right[0][1] + left[1][1] * right[1][1]


def observation(text, cam_dev):
    vectors = [(text[8 * v : 8 * v + 8], text[64 + v : 65 + v]) for v in range(8)]
    cells = [quotient(text[77 + m : 78 + m], cam_dev) for m in range(3)]
    within = text[77:78] - cells[0] * cam_dev
    hit = one_hot(iota((cam_dev, text.shape[1]), 0).astype(F32) == within)
    return vectors, cells, within, hit


def folded(sums):
    size = sums.shape[0] // 3
    return sums[:size] + sums[size : 2 * size] + sums[2 * size :]


def diagonal_kernel(
    got_ref, rank_ref, back_ref, text_ref, out_ref, lower_ref, state_ref, send_ref
):
    devices = got_ref.shape[0] // 10
    cam_dev = out_ref.shape[1]
    for h in range(2):
        for g in range(5):
            turned = got_ref[pl.ds(2 * g + h, devices, stride=10), :].T
            for c in range(8):
                at = slice((c % 2) * devices, (c % 2 + 1) * devices)
                text_ref[4 * h + c // 2, 16 * g : 16 * g + 16, at] = turned[16 * c : 16 * c + 16]
    unit = iota((CELL, cam_dev), 0)
    unit = jnp.logical_and(unit <= 63, unit == 9 * lax.shift_right_logical(unit, 3)) | (unit == 80)
    total = jnp.where(unit, DAMPING, 0.0)
    for index in range(OBS_CAP // 2):
        text = text_ref[index]
        vectors, _, _, hit = observation(text, cam_dev)
        own = vectors[0:2]
        corner = [[text[72:73], text[73:74]], [text[73:74], text[74:75]]]
        weighted = [
            tuple(corner[u][0] * own[0][i] + corner[u][1] * own[1][i] for i in range(2)) for u in range(2)
        ]
        blocks, edge = outer(own, weighted)
        extra = [text[75:76], text[76:77]]
        ninth = own[0][1] * extra[0] + own[1][1] * extra[1]
        blocks.append(jnp.concatenate([edge, ninth, jnp.zeros((6, text.shape[1]), F32)], axis=0))
        blocks.append(own[0][0] * extra[0] + own[1][0] * extra[1])
        term = jnp.concatenate(blocks, axis=0)
        total = total + folded(dot_nt(jnp.concatenate(pieces(term), axis=0), hit))
    out_ref[...] = total
    cholesky(out_ref, lower_ref)
    right = jnp.concatenate([total[88:96], total[81:82], jnp.zeros((7, cam_dev), F32)], axis=0)
    scaled = solve(lower_ref, right)
    zero = jnp.zeros_like(right)
    state_ref[0] = zero
    state_ref[1] = right
    state_ref[2] = scaled
    state_ref[3] = scaled
    for index in range(4, 7):
        state_ref[index] = zero
    most = jnp.max(jnp.max(rank_ref[...], axis=1, keepdims=True), axis=0, keepdims=True)
    single = jnp.logical_and(rank_ref[...] >= 0, back_ref[...] < 0)
    carried = total_of(jnp.where(single, 1.0, 0.0))
    crowded = jnp.where(jnp.logical_or(most >= float(SLOTS), carried > float(CARRIED)), 1.0, 0.0)
    send_rows(send_ref, [coupled(scaled, rank_ref)], ROWS, [crowded])


def coupling_kernel(text_ref, lower_ref, out_ref, wanted_ref, inverse_ref, edge_ref):
    cam_dev = out_ref.shape[2]
    devices = wanted_ref.shape[0]
    out_ref[...] = jnp.zeros_like(out_ref)
    edge_ref[...] = jnp.zeros_like(edge_ref)

    def step(index, _):
        vectors, cells, _, hit = observation(text_ref[index], cam_dev)
        terms, edges = [], jnp.zeros((16, hit.shape[1]), F32)
        row = iota(edges.shape, 0).astype(F32)
        for m in range(3):
            blocks, edge = outer(vectors[0:2], vectors[2 + 2 * m : 4 + 2 * m])
            terms.append(jnp.concatenate(pieces(jnp.concatenate(blocks, axis=0)), axis=0))
            edges = jnp.where(row == cells[m], edge, edges)
        for k in range(NBR):
            part = None
            for m in range(3):
                piece = terms[m] * one_hot(cells[m] == float(k))
                part = piece if part is None else part + piece
            out_ref[k, :80] = out_ref[k, :80] + folded(dot_nt(part, hit))
        edge_ref[...] = edge_ref[...] + folded(dot_nt(jnp.concatenate(pieces(edges), axis=0), hit))
        return 0

    lax.fori_loop(0, OBS_CAP // 2, step, 0, unroll=True)
    for k in range(NBR):
        out_ref[k, 80:81] = edge_ref[k : k + 1]
    labels = []
    for s in range(OBS_CAP):
        label = text_ref[s // 2, 77:78, (s % 2) * devices : (s % 2 + 1) * devices]
        labels.append(label - cam_dev * quotient(label, cam_dev))
    labels.append(jnp.zeros((128 - OBS_CAP, devices), F32))
    wanted_ref[...] = jnp.concatenate(labels, axis=0).T
    row = iota((16, 9 * cam_dev), 0)
    unit = lax.shift_right_logical(iota((16, 9 * cam_dev), 1), cam_dev.bit_length() - 1) == row
    solved = solve(lower_ref, jnp.where(unit, 1.0, 0.0))
    columns = [solved[:, c * cam_dev : (c + 1) * cam_dev] for c in range(9)]
    inverse_ref[...] = jnp.concatenate(
        [column[:8] for column in columns] + [columns[8][:8], columns[8][8:], jnp.zeros((8, cam_dev), F32)],
        axis=0,
    )


def cholesky(cells_ref, lower_ref):
    cam_dev = cells_ref.shape[1]
    zero = jnp.zeros((7, cam_dev), F32)
    block = cells_ref[...]
    columns = [
        jnp.concatenate([block[8 * r : 8 * r + 8], block[64 + r : 65 + r], zero], axis=0) for r in range(8)
    ]
    columns.append(jnp.concatenate([block[64:72], block[80:81], zero], axis=0))
    row = iota((16, cam_dev), 0)
    for c in range(9):
        pivot = columns[c][c : c + 1]
        root = jnp.sqrt(pivot)
        inverse = 1.0 / root
        column = jnp.where(row > c, columns[c] * inverse, 0.0)
        for r in range(c + 1, 9):
            columns[r] = columns[r] - column * column[r : r + 1]
        lower_ref[c] = jnp.where(row == 9, inverse, jnp.where(row < 9, column, 0.0))


def solve(lower_ref, vector):
    row = iota(vector.shape, 0)
    rest = vector
    copies = vector.shape[1] // lower_ref.shape[2]
    columns = [jnp.concatenate([lower_ref[c]] * copies, axis=1) for c in range(9)]
    for c in range(9):
        column = columns[c]
        value = rest[c : c + 1] * column[9:10]
        rest = jnp.where(row == c, value, rest - jnp.where(row < 9, column, 0.0) * value)
    for c in reversed(range(9)):
        column = columns[c]
        if c < 8:
            dotted = jnp.sum(
                jnp.where(jnp.logical_and(row > c, row < 9), column * rest, 0.0), axis=0, keepdims=True
            )
        else:
            dotted = jnp.zeros((1, vector.shape[1]), F32)
        value = (rest[c : c + 1] - dotted) * column[9:10]
        rest = jnp.where(row == c, value, rest)
    return rest


def multiply(pairs):
    cam_dev = pairs[0][1].shape[1]
    sums = [jnp.zeros((8, cam_dev), F32) for _ in range(9)]
    side = jnp.zeros((8, cam_dev), F32)
    corner = jnp.zeros((1, cam_dev), F32)
    for cell_ref, vector in pairs:
        first, last = vector[0:8], vector[8:9]
        for r in range(9):
            sums[r] = sums[r] + cell_ref[8 * r : 8 * r + 8, :] * first
        side = side + cell_ref[72:80, :] * last
        corner = corner + cell_ref[80:81, :] * last
    sums = [jnp.sum(part, axis=0, keepdims=True) for part in sums]
    top = jnp.concatenate(sums[:8], axis=0) + side
    return jnp.concatenate([top, sums[8] + corner, jnp.zeros((7, cam_dev), F32)], axis=0)


def total_of(values):
    return jnp.sum(jnp.sum(values, axis=1, keepdims=True), axis=0, keepdims=True)


FIRST = 8
SPLIT = 9 * FIRST


def lane_plan():
    lane = iota((128, 1), 0)
    low = jnp.where(lane < 64, lax.shift_right_logical(lane, 3), lane - 64)
    high = FIRST + jnp.where(lane < 120, lax.shift_right_logical(lane - SPLIT, 3), lane - 120)
    ninth = jnp.logical_or(lane >= 120, jnp.logical_and(lane >= 64, lane < SPLIT))
    return jnp.where(lane < SPLIT, low, high), jnp.where(ninth, 8, lane & 7)


def spread(vector):
    cam_dev = vector.shape[1]
    choose = one_hot(iota((128, 16), 1) == lane_plan()[1])
    copies = dot_nn(choose, jnp.concatenate(pieces(vector), axis=1))
    return [copies[:, p * cam_dev : (p + 1) * cam_dev] for p in range(3)]


def coupled(vector, rank_ref):
    group, _ = lane_plan()
    rank = rank_ref[...].astype(BF16)
    one, zero = jnp.ones(rank.shape, BF16), jnp.zeros(rank.shape, BF16)
    copies = spread(vector)
    sides = []
    for lanes, groups in ((slice(0, SPLIT), range(FIRST)), (slice(SPLIT, 128), range(FIRST, GROUP))):
        left = [[jnp.where(rank == float(GROUP * h + g), one, zero) for g in groups] for h in range(ROWS)]
        right = [
            jnp.concatenate([jnp.where(group[lanes] == g, part[lanes], 0.0) for g in groups], axis=1)
            for part in copies
        ]
        sides.append((left, right))
    return sides


def observed(first, second, wanted_ref):
    group, _ = lane_plan()
    lane = iota((wanted_ref.shape[0], first.shape[1]), 1).astype(F32)
    empty = jnp.zeros(lane.shape, BF16)
    both = list(zip(spread(first), spread(second)))
    sides = []
    for lanes, pairs in ((slice(0, SPLIT), range(FIRST // 2)), (slice(SPLIT, 128), range(FIRST // 2, PAIRS))):
        left = [
            [
                one_hot(wanted_ref[:, slot : slot + 1] == lane) if slot < OBS_CAP else empty
                for slot in (PAIRS * h + g for g in pairs)
            ]
            for h in range(PAIR_ROWS)
        ]
        right = [
            jnp.concatenate(
                [
                    jnp.where(
                        group[lanes] == 2 * g, one[lanes], jnp.where(group[lanes] == 2 * g + 1, two[lanes], 0.0)
                    )
                    for g in pairs
                ],
                axis=1,
            )
            for one, two in both
        ]
        sides.append((left, right))
    return sides


def send_rows(send_ref, parts, rows, scalars):
    devices = send_ref.shape[0] // rows
    texts = []
    for side in range(2):
        here = [part[side] for part in parts]
        left = jnp.concatenate(
            [jnp.concatenate([hit for left, _ in here for hit in left[h]], axis=1) for h in range(rows)], axis=0
        )
        right = jnp.concatenate(
            [jnp.concatenate([right[p] for _, right in here], axis=1) for p in range(3)], axis=0
        )
        sums = dot_nt(left, right.astype(BF16))
        width = sums.shape[1] // 3
        texts.append(sums[:, :width] + sums[:, width : 2 * width] + sums[:, 2 * width :])
    texts = jnp.concatenate(texts, axis=1)
    lane = iota((devices, 128), 1)
    for h in range(rows):
        text = texts[h * devices : (h + 1) * devices]
        for index, scalar in enumerate(scalars[2 * h : 2 * h + 2]):
            text = jnp.where(lane == 126 + index, scalar, text)
        send_ref[pl.ds(h, devices, stride=rows), :] = text


def read_rows(turned, places):
    mark = one_hot(iota((turned.shape[1], places.shape[1]), 0).astype(F32) == places)
    taken = dot_nn(jnp.concatenate(pieces(turned), axis=0), mark)
    return taken[:128] + taken[128:256] + taken[256:]


def pick(taken, groups):
    top = jnp.zeros((8, taken.shape[1]), F32)
    for g in range(GROUP):
        at = 8 * g if g < FIRST else 8 * g + 8
        top = jnp.where(groups == float(g), taken[at : at + 8], top)
    row = iota((8, taken.shape[1]), 0).astype(F32)
    ninth = jnp.where(row == groups, taken[64:72], jnp.where(row + FIRST == groups, taken[120:128], 0.0))
    ninth = jnp.sum(ninth, axis=0, keepdims=True)
    return jnp.concatenate([top, ninth, jnp.zeros((7, taken.shape[1]), F32)], axis=0)


def read_scalars(turned, rows, count):
    column = iota((1, turned.shape[1]), 1)
    inner = column.astype(F32) - quotient(column, rows) * rows
    sums = []
    for index in range(count):
        line = turned[126 + index % 2 : 127 + index % 2]
        sums.append(
            jnp.sum(jnp.where(inner == float(index // 2), line, 0.0), axis=1, keepdims=True)
        )
    return sums


def step_kernel(
    index, got_ref, source_ref, place_ref, second_ref, rank_ref, back_ref, cells_ref, diagonal_ref, inverse_ref,
    state_ref, far_ref, state_out, far_out, send_ref,
):
    turned = got_ref[...].T
    sums = read_scalars(turned, ROWS, 4 if index else 1)
    source = source_ref[...]
    part = quotient(place_ref[...], GROUP)
    places, groups = source * ROWS + part, place_ref[...] - part * GROUP
    couplings = places.shape[1]
    if index >= 2:
        part = quotient(jnp.maximum(second_ref[...], 0.0), GROUP)
        room = second_ref[...] >= 0
        places = jnp.concatenate([places, jnp.where(room, source * ROWS + part, -1.0)], axis=1)
        groups = jnp.concatenate([groups, second_ref[...] - part * GROUP], axis=1)
    arrived = pick(read_rows(turned, places), groups)
    step, rest, scaled, direction = (state_ref[i] for i in range(4))
    if index:
        image, image_scaled = state_ref[4], state_ref[5]
        energy, cross, square, old = sums
        alpha = old / energy
        beta = (old - 2.0 * alpha * cross + alpha * alpha * square) / old
        step = step + alpha * direction
        rest = rest - alpha * image
        direction = (scaled - alpha * image_scaled) + beta * direction
        far_before = far_ref[1]
        if index >= 2:
            far_before = jnp.where(room, arrived[:, couplings:], far_before)
        far_scaled = far_before - alpha * arrived[:, :couplings]
        far = far_scaled + beta * far_ref[0]
    else:
        far_scaled = arrived
        far = arrived
    cam_dev = cells_ref.shape[2]
    image = multiply(
        [(diagonal_ref, direction)]
        + [(cells_ref.at[k], far[:, k * cam_dev : (k + 1) * cam_dev]) for k in range(NBR)]
    )
    energy = total_of(direction * image)
    scaled = multiply([(inverse_ref, rest)]) if index else scaled
    old = total_of(rest * scaled)
    state_out[0] = step
    state_out[1] = rest
    state_out[2] = scaled
    state_out[3] = direction
    state_out[4] = image
    state_out[6] = state_ref[6] if index else jnp.zeros_like(step) + sums[0]
    far_out[0] = far
    far_out[1] = far_scaled
    if index == ITERS - 1:
        state_out[5] = jnp.zeros_like(image)
        send_rows(send_ref, [observed(step, direction, rank_ref)], PAIR_ROWS, [energy, old])
        return
    image_scaled = multiply([(inverse_ref, image)])
    state_out[5] = image_scaled
    parts = [coupled(image_scaled, rank_ref)]
    if index + 1 >= 2:
        parts.append(coupled(scaled, back_ref))
    scalars = [energy, total_of(scaled * image), total_of(image * image_scaled), old]
    send_rows(send_ref, parts, ROWS, scalars)


def finish_kernel(
    got_ref, place_ref, state_ref, jc_ref, jp_ref, rs_ref, vi_ref, used_ref, step_ref, rest_ref, point_ref
):
    npts = used_ref.shape[1]
    places = jnp.concatenate([place_ref[a : a + 1, :] for a in range(TRACK)], axis=1)
    groups = jnp.concatenate([place_ref[TRACK + a : TRACK + a + 1, :] for a in range(TRACK)], axis=1)
    turned = got_ref[...].T
    energy, old = read_scalars(turned, PAIR_ROWS, 2)
    alpha = old / energy
    step_ref[...] = (state_ref[0] + alpha * state_ref[3])[:9]
    rest_ref[...] = (state_ref[1] - alpha * state_ref[4])[:9]
    taken = read_rows(turned, places)
    moved = pick(taken, 2.0 * groups) + alpha * pick(taken, 2.0 * groups + 1.0)
    reduced = [jnp.zeros((1, npts), F32) for _ in range(3)]
    for a in range(TRACK):
        live = used_ref[a : a + 1, :].astype(F32)
        there = moved[:9, a * npts : (a + 1) * npts]
        jacobian = lines(jc_ref, a, 0, 18, npts)
        gradient = lines(jp_ref, a, 0, 6, npts)
        for u in range(2):
            change = jnp.sum(jacobian[9 * u : 9 * u + 9] * there, axis=0, keepdims=True)
            change = live * (change + rs_ref[a, u : u + 1, :])
            for x in range(3):
                reduced[x] = reduced[x] - gradient[3 * u + x : 3 * u + x + 1] * change
    for x in range(3):
        point_ref[x : x + 1, :] = sum(
            vi_ref[3 * x + y : 3 * x + y + 1, :] * reduced[y] for y in range(3)
        )


def factor_blocks(matrix):
    lower = {}
    for row_idx in range(9):
        for col_idx in range(row_idx + 1):
            accum = matrix[row_idx, col_idx]
            for inner_idx in range(col_idx):
                accum = accum - lower[row_idx, inner_idx] * lower[col_idx, inner_idx]
            if row_idx == col_idx:
                lower[row_idx, row_idx] = jnp.sqrt(accum)
            else:
                lower[row_idx, col_idx] = accum / lower[col_idx, col_idx]
    return lower


def solve_blocks(lower, vector):
    forward = []
    for row_idx in range(9):
        accum = vector[row_idx]
        for inner_idx in range(row_idx):
            accum = accum - lower[row_idx, inner_idx] * forward[inner_idx]
        forward.append(accum / lower[row_idx, row_idx])
    backward = [None] * 9
    for row_idx in reversed(range(9)):
        accum = forward[row_idx]
        for inner_idx in range(row_idx + 1, 9):
            accum = accum - lower[inner_idx, row_idx] * backward[inner_idx]
        backward[row_idx] = accum / lower[row_idx, row_idx]
    return jnp.stack(backward)


def whole_exchange(cells, diagonal, pattern, jacobian_cam, jacobian_pt, residuals, point_inverse, obs_camera, used):
    cam_dev = pattern.shape[1]
    cells = jnp.concatenate([cells, diagonal[None]], axis=0)
    main = cells[:, :64].reshape(NBR + 1, 8, 8, cam_dev)
    side = cells[:, 72:80].reshape(NBR + 1, 8, 1, cam_dev)
    foot = jnp.concatenate([cells[:, 64:72], cells[:, 80:81]], axis=1)[:, None]
    blocks = jnp.concatenate([jnp.concatenate([main, side], axis=2), foot], axis=1)
    gradient = jnp.concatenate([cells[NBR, 88:96], cells[NBR, 81:82]], axis=0)
    lower = factor_blocks(blocks[NBR])

    def gathered(vector):
        return lax.all_gather(vector, BOTH, axis=1, tiled=True)

    def summed(values):
        return lax.psum(jnp.sum(values), BOTH)

    step = jnp.zeros_like(gradient)
    rest = gradient
    scaled = solve_blocks(lower, rest)
    direction = scaled
    energy_now = summed(rest * scaled)
    for _ in range(ITERS):
        taken = jnp.concatenate([gathered(direction)[:, pattern], direction[:, None, :]], axis=1)
        image = jnp.sum(blocks * jnp.swapaxes(taken, 0, 1)[:, None], axis=(0, 2))
        alpha = energy_now / summed(direction * image)
        step = step + alpha * direction
        rest = rest - alpha * image
        scaled = solve_blocks(lower, rest)
        energy_next = summed(rest * scaled)
        direction = scaled + energy_next / energy_now * direction
        energy_now = energy_next
    whole = gathered(step)
    npts = obs_camera.shape[1]
    rows = jacobian_cam.reshape(TRACK, 2, 9, npts)
    seen = jnp.swapaxes(whole[:, obs_camera], 0, 1)
    change = jnp.sum(rows * seen[:, None], axis=2) + residuals
    change = change * used.astype(F32)[:, None]
    reduced = -jnp.sum(jacobian_pt.reshape(TRACK, 2, 3, npts) * change[:, :, None], axis=(0, 1))
    point_step = jnp.sum(point_inverse.reshape(3, 3, npts) * reduced[None], axis=1)
    return step, rest, point_step


def shape(*dims, dtype=F32):
    return jax.ShapeDtypeStruct(dims, dtype)


def call(kernel, outs, name, scratch=(), flops=0):
    cost = pl.CostEstimate(flops=flops, bytes_accessed=1 << 20, transcendentals=0) if flops else None
    return pl.pallas_call(
        kernel, out_shape=outs, name=name, compiler_params=PARAMS, scratch_shapes=list(scratch),
        cost_estimate=cost,
    )


def exchange(message, devices):
    width = message.shape[0] // devices
    arrived = lax.all_to_all(
        message.reshape(devices, width, 1, 128), BOTH, split_axis=0, concat_axis=0, tiled=True
    )
    return arrived.reshape(devices * width, 128)


def per_device(
    jacobian_cam, jacobian_pt, residuals, point_inverse, obs_camera, pair_slot, observation_used, pattern,
):
    devices = lax.axis_size("cam") * lax.axis_size("pt")
    npts = obs_camera.shape[1]
    cam_dev = pattern.shape[1]
    shift = cam_dev.bit_length() - 1
    couplings = NBR * cam_dev

    cameras = flat(jacobian_cam)
    points = flat(jacobian_pt)

    packed, places, rank, back = call(
        functools.partial(pack_kernel, devices, shift),
        (
            shape(devices * 10, 128), shape(2 * TRACK, npts), shape(devices, cam_dev), shape(devices, cam_dev),
        ),
        "pack",
        [pltpu.VMEM((80, TRACK * npts), F32)],
    )(cameras, points, residuals, point_inverse, obs_camera, pair_slot, observation_used, pattern)
    got = exchange(packed, devices)
    sources, far_rank, far_back = call(
        functools.partial(place_kernel, devices, shift),
        (shape(1, couplings), shape(1, couplings), shape(1, couplings)),
        "place",
        flops=4 * 10**9,
    )(pattern)
    text, diagonal, lower, state, message = call(
        diagonal_kernel,
        (
            shape(OBS_CAP // 2, 80, 2 * devices),
            shape(CELL, cam_dev),
            shape(9, 16, cam_dev),
            shape(7, 16, cam_dev),
            shape(devices * ROWS, 128),
        ),
        "diagonal",
    )(got, rank, back)
    cells, wanted, inverse = call(
        coupling_kernel,
        (shape(NBR, CELL, cam_dev), shape(devices, 128), shape(CELL, cam_dev)),
        "coupling",
        [pltpu.VMEM((16, cam_dev), F32)],
        flops=8 * 10**9,
    )(text, lower)
    far = jnp.zeros((2, 16, couplings), F32)
    crowded = None
    for index in range(ITERS):
        last = index == ITERS - 1
        rows = PAIR_ROWS if last else ROWS
        arrived = exchange(message, devices)
        state, far, message = call(
            functools.partial(step_kernel, index),
            (shape(7, 16, cam_dev), shape(2, 16, couplings), shape(devices * rows, 128)),
            "step",
        )(
            arrived, sources, far_rank, far_back, wanted if last else rank, back, cells, diagonal, inverse,
            state, far,
        )
        if index == 0:
            crowded = state[6, 0, 0] > 0.0
    arrived = exchange(message, devices)
    found = call(
        finish_kernel, (shape(9, cam_dev), shape(9, cam_dev), shape(3, npts)), "finish"
    )(arrived, places, state, cameras, points, residuals, point_inverse, observation_used)

    def dense():
        return whole_exchange(
            cells, diagonal, pattern, jacobian_cam, jacobian_pt, residuals, point_inverse, obs_camera, observation_used
        )

    return lax.cond(crowded, dense, lambda: tuple(found))


def solution(mesh):
    return jax.shard_map(
        per_device,
        mesh=mesh,
        in_specs=(
            P(None, None, BOTH),
            P(None, None, BOTH),
            P(None, None, BOTH),
            P(None, BOTH),
            P(None, BOTH),
            P(None, None, BOTH),
            P(None, BOTH),
            P(None, BOTH),
        ),
        out_specs=(P(None, BOTH), P(None, BOTH), P(None, BOTH)),
        check_vma=False,
    )
```

```python
import functools

import jax
import jax.numpy as jnp
from jax import lax
from jax.experimental import pallas as pl
from jax.experimental.pallas import tpu as pltpu
from jax.sharding import PartitionSpec as P

TRACK = 4
NBR = 12
ITERS = 4
OBS_CAP = 16
DAMPING = 1.0
BOTH = ("cam", "pt")

GROUP = 14
PAIRS = 7
ROWS = 2
SLOTS = GROUP * ROWS
CARRIED = 32
PAIR_ROWS = 3
CELL = 96
F32 = jnp.float32
BF16 = jnp.bfloat16
PARAMS = pltpu.CompilerParams(vmem_limit_bytes=28 * 1024 * 1024)


def iota(shape, dim):
    return lax.broadcasted_iota(jnp.int32, shape, dim)


def quotient(values, divisor):
    return jnp.floor((values.astype(F32) + 0.5) * (1.0 / divisor))


def pieces(values):
    high = values.astype(BF16)
    rest = values - high.astype(F32)
    middle = rest.astype(BF16)
    low = (rest - middle.astype(F32)).astype(BF16)
    return high, middle, low


def dot_nn(left, right):
    return lax.dot_general(left, right, (((1,), (0,)), ((), ())), preferred_element_type=F32)


def dot_nt(left, right):
    return lax.dot_general(left, right, (((1,), (1,)), ((), ())), preferred_element_type=F32)


def one_hot(condition):
    return jnp.where(condition, 1.0, 0.0).astype(BF16)


def before(size):
    return one_hot(iota((size, size), 0) < iota((size, size), 1))


def flat(array):
    tracks, rows, npts = array.shape
    tiles = jnp.transpose(array, (1, 0, 2)).reshape(rows, tracks, npts // 128, 128)
    return jnp.transpose(tiles, (0, 2, 1, 3)).reshape(-1, 128)


def lines(ref, a, first, count, npts):
    tiles = npts // 128
    step = TRACK * tiles
    return jnp.concatenate(
        [ref[pl.ds(step * first + TRACK * t + a, count, stride=step), :] for t in range(tiles)], axis=1
    )


def pack_kernel(
    devices, shift, jc_ref, jp_ref, rs_ref, vi_ref, cam_ref, slot_ref, used_ref, pattern_ref,
    out_ref, place_ref, rank_ref, feat_ref,
):
    npts = cam_ref.shape[1]
    cam_dev = pattern_ref.shape[1]
    found = jnp.zeros((devices, cam_dev), F32)
    for k in range(NBR):
        target = lax.shift_right_logical(pattern_ref[k : k + 1, :], shift)
        found = jnp.where(iota((devices, cam_dev), 0) == target, 1.0, found)
    rank = dot_nn(found.astype(BF16), before(cam_dev))
    rank_ref[...] = jnp.where(found > 0, rank, -1.0e6)
    live = [used_ref[a : a + 1, :].astype(F32) for a in range(TRACK)]
    carry = jnp.zeros((devices, 1), F32)
    triangle = before(npts)
    hits = []
    withins = []
    for a in range(TRACK):
        owner = lax.shift_right_logical(cam_ref[a : a + 1, :], shift)
        hit = jnp.where(
            jnp.logical_and(iota((devices, npts), 0) == owner, live[a] > 0), 1.0, 0.0
        )
        hits.append(hit.astype(BF16))
        count = dot_nn(hits[a], triangle) + carry
        within = jnp.sum(hit * count, axis=0, keepdims=True)
        carry = carry + jnp.sum(hit, axis=1, keepdims=True)
        withins.append(within)
        place_ref[a : a + 1, :] = jnp.where(live[a] > 0, owner.astype(F32), -1.0)
        place_ref[TRACK + a : TRACK + a + 1, :] = within

    vi = [[vi_ref[3 * x + y : 3 * x + y + 1, :] for y in range(3)] for x in range(3)]
    jp = [
        [[gradient[3 * u + x : 3 * u + x + 1] for x in range(3)] for u in range(2)]
        for gradient in [lines(jp_ref, a, 0, 6, npts) for a in range(TRACK)]
    ]
    jc = [lines(jc_ref, a, 0, 18, npts) for a in range(TRACK)]
    res = [[rs_ref[a, u : u + 1, :] for u in range(2)] for a in range(TRACK)]
    grad = []
    for x in range(3):
        total = jnp.zeros((1, npts), F32)
        for a in range(TRACK):
            total = total - live[a] * (jp[a][0][x] * res[a][0] + jp[a][1][x] * res[a][1])
        grad.append(total)
    for a in range(TRACK):
        at = slice(a * npts, (a + 1) * npts)
        for u in range(2):
            feat_ref[8 * u : 8 * u + 8, at] = jc[a][9 * u : 9 * u + 8]
            feat_ref[64 + u : 65 + u, at] = jc[a][9 * u + 8 : 9 * u + 9]
        removed = [
            [live[a] * sum(jp[a][u][x] * vi[x][y] for x in range(3)) for y in range(3)]
            for u in range(2)
        ]

        def middle(b, u, v):
            return -live[b] * sum(removed[u][y] * jp[b][v][y] for y in range(3))

        partners = [b for b in range(TRACK) if b != a]
        for m, b in enumerate(partners):
            first = [jc[b][9 * v : 9 * v + 8] for v in range(2)]
            ninth = [jc[b][9 * v + 8 : 9 * v + 9] for v in range(2)]
            for u in range(2):
                row = 2 + 2 * m + u
                one, two = middle(b, u, 0), middle(b, u, 1)
                feat_ref[8 * row : 8 * row + 8, at] = one * first[0] + two * first[1]
                feat_ref[64 + row : 65 + row, at] = one * ninth[0] + two * ninth[1]
        feat_ref[72:73, at] = live[a] + middle(a, 0, 0)
        feat_ref[73:74, at] = middle(a, 0, 1)
        feat_ref[74:75, at] = live[a] + middle(a, 1, 1)
        for u in range(2):
            right = -(live[a] * res[a][u] + sum(removed[u][y] * grad[y] for y in range(3)))
            feat_ref[75 + u : 76 + u, at] = right
        own = cam_ref[a : a + 1, :] & (cam_dev - 1)
        for m, b in enumerate(partners):
            label = slot_ref[a, b : b + 1, :] * cam_dev + own
            feat_ref[77 + m : 78 + m, at] = label.astype(F32)

    owners = jnp.concatenate(hits, axis=1)
    place = jnp.concatenate(withins, axis=1)
    split = pieces(feat_ref[...])
    masks = [
        one_hot(jnp.broadcast_to(place, (16, TRACK * npts)) == float(s)) for s in range(OBS_CAP)
    ]
    for g in range(5):
        right = jnp.concatenate(
            [
                part[16 * g : 16 * g + 16] * masks[8 * h + c]
                for h in range(2) for part in split for c in range(8)
            ],
            axis=0,
        )
        sums = dot_nt(owners, right)
        for h in range(2):
            mine = sums[:, 384 * h : 384 * h + 384]
            out_ref[pl.ds(2 * g + h, devices, stride=10), :] = (
                mine[:, :128] + mine[:, 128:256] + mine[:, 256:]
            )


def place_kernel(devices, shift, pattern_ref, rank_ref, source_ref, far_ref, back_ref, choice_ref, count_ref):
    cam_dev = pattern_ref.shape[1]
    turned = rank_ref[...].T
    camera = iota(turned.shape, 0).astype(F32)
    for h in range(ROWS):
        for g in range(16):
            here = jnp.where(turned == float(GROUP * h + g), camera, 0.0)
            choice_ref[16 * h + g : 16 * h + g + 1, :] = jnp.sum(here, axis=0, keepdims=True).astype(jnp.int32)
    most = jnp.sum(jnp.where(turned >= 0, 1.0, 0.0), axis=0, keepdims=True)
    carried = total_of(jnp.maximum(2.0 * most - SLOTS, 0.0))
    full = jnp.max(most, axis=1, keepdims=True)
    crowded = jnp.where(jnp.logical_or(full > float(SLOTS), carried > float(CARRIED)), 1.0, 0.0)
    count_ref[0:1, :] = most
    count_ref[1:2, :] = jnp.zeros_like(most) + crowded
    count = jnp.zeros((devices, cam_dev), F32)
    sources = []
    withins = []
    for k in range(NBR):
        camera = pattern_ref[k : k + 1, :]
        source = lax.shift_right_logical(camera, shift)
        within = camera & (cam_dev - 1)
        sources.append(iota((devices, cam_dev), 0) == source)
        withins.append(iota((cam_dev, cam_dev), 0) == within)
        count = count + dot_nt(one_hot(sources[k]), one_hot(withins[k]))
        source_ref[:, k * cam_dev : (k + 1) * cam_dev] = source.astype(F32)
    found = one_hot(count > 0)
    rank = dot_nn(found, before(cam_dev))
    most = jnp.sum(found.astype(F32), axis=1, keepdims=True)
    turned = rank.T.astype(BF16)
    for k in range(NBR):
        column = dot_nn(turned, one_hot(sources[k]))
        mine = jnp.sum(jnp.where(withins[k], column, 0.0), axis=0, keepdims=True)
        far_ref[:, k * cam_dev : (k + 1) * cam_dev] = mine
        full = jnp.sum(jnp.where(sources[k], most, 0.0), axis=0, keepdims=True)
        back = SLOTS - 1.0 - mine
        back_ref[:, k * cam_dev : (k + 1) * cam_dev] = jnp.where(back >= full, back, -1.0)


def outer(left, right):
    blocks = []
    for r in range(8):
        blocks.append(left[0][0][r : r + 1] * right[0][0] + left[1][0][r : r + 1] * right[1][0])
    blocks.append(left[0][1] * right[0][0] + left[1][1] * right[1][0])
    blocks.append(left[0][0] * right[0][1] + left[1][0] * right[1][1])
    return blocks, left[0][1] * right[0][1] + left[1][1] * right[1][1]


def turn(got_ref, text_ref, parts):
    devices = got_ref.shape[0] // 10
    for h in range(2):
        for row, g in enumerate(parts):
            turned = got_ref[pl.ds(2 * g + h, devices, stride=10), :].T
            for c in range(8):
                at = slice((c % 2) * devices, (c % 2 + 1) * devices)
                text_ref[4 * h + c // 2, 16 * row : 16 * row + 16, at] = turned[16 * c : 16 * c + 16]


def observation(text, cam_dev):
    own = [(text[8 * u : 8 * u + 8], text[16 + u : 17 + u]) for u in range(2)]
    cells = [quotient(text[29 + m : 30 + m], cam_dev) for m in range(3)]
    within = text[29:30] - cells[0] * cam_dev
    hit = one_hot(iota((cam_dev, text.shape[1]), 0).astype(F32) == within)
    return own, cells, hit


def folded(sums):
    size = sums.shape[0] // 3
    return sums[:size] + sums[size : 2 * size] + sums[2 * size :]


def diagonal_kernel(
    got_ref, choice_ref, count_ref, text_ref, out_ref, lower_ref, state_ref, send_ref
):
    cam_dev = out_ref.shape[1]
    turn(got_ref, text_ref, (0, 4))
    unit = iota((CELL, cam_dev), 0)
    unit = jnp.logical_and(unit <= 63, unit == 9 * lax.shift_right_logical(unit, 3)) | (unit == 80)
    total = jnp.where(unit, DAMPING, 0.0)
    for index in range(OBS_CAP // 2):
        text = text_ref[index]
        own, _, hit = observation(text, cam_dev)
        corner = [[text[24:25], text[25:26]], [text[25:26], text[26:27]]]
        weighted = [
            tuple(corner[u][0] * own[0][i] + corner[u][1] * own[1][i] for i in range(2)) for u in range(2)
        ]
        blocks, edge = outer(own, weighted)
        extra = [text[27:28], text[28:29]]
        ninth = own[0][1] * extra[0] + own[1][1] * extra[1]
        blocks.append(jnp.concatenate([edge, ninth, jnp.zeros((6, text.shape[1]), F32)], axis=0))
        blocks.append(own[0][0] * extra[0] + own[1][0] * extra[1])
        term = jnp.concatenate(blocks, axis=0)
        total = total + folded(dot_nt(jnp.concatenate(pieces(term), axis=0), hit))
    out_ref[...] = total
    cholesky(out_ref, lower_ref)
    right = jnp.concatenate([total[88:96], total[81:82], jnp.zeros((7, cam_dev), F32)], axis=0)
    scaled = solve(lower_ref, right)
    zero = jnp.zeros_like(right)
    state_ref[0] = zero
    state_ref[1] = right
    state_ref[2] = scaled
    state_ref[3] = scaled
    for index in range(4, 7):
        state_ref[index] = zero
    send_rows(send_ref, coupled(scaled, None, choice_ref, count_ref), [count_ref[1:2, :1]])


def coupling_kernel(got_ref, text_ref, lower_ref, out_ref, wanted_ref, inverse_ref, edge_ref, more_ref):
    cam_dev = out_ref.shape[2]
    devices = wanted_ref.shape[1]
    out_ref[...] = jnp.zeros_like(out_ref)
    edge_ref[...] = jnp.zeros_like(edge_ref)
    turn(got_ref, more_ref, (1, 2, 3))

    def step(index, _):
        text, more = text_ref[index], more_ref[index]
        own, cells, hit = observation(text, cam_dev)
        partners = [(more[8 * v : 8 * v + 8], text[18 + v : 19 + v]) for v in range(6)]
        terms, edges = [], jnp.zeros((16, hit.shape[1]), F32)
        row = iota(edges.shape, 0).astype(F32)
        for m in range(3):
            blocks, edge = outer(own, partners[2 * m : 2 * m + 2])
            terms.append(jnp.concatenate(pieces(jnp.concatenate(blocks, axis=0)), axis=0))
            edges = jnp.where(row == cells[m], edge, edges)
        for k in range(NBR):
            part = None
            for m in range(3):
                piece = terms[m] * one_hot(cells[m] == float(k))
                part = piece if part is None else part + piece
            out_ref[k, :80] = out_ref[k, :80] + folded(dot_nt(part, hit))
        edge_ref[...] = edge_ref[...] + folded(dot_nt(jnp.concatenate(pieces(edges), axis=0), hit))
        return 0

    lax.fori_loop(0, OBS_CAP // 2, step, 0, unroll=True)
    for k in range(NBR):
        out_ref[k, 80:81] = edge_ref[k : k + 1]
    for s in range(OBS_CAP):
        label = text_ref[s // 2, 29:30, (s % 2) * devices : (s % 2 + 1) * devices]
        wanted_ref[s : s + 1, :] = (label - cam_dev * quotient(label, cam_dev)).astype(jnp.int32)
    row = iota((16, 9 * cam_dev), 0)
    unit = lax.shift_right_logical(iota((16, 9 * cam_dev), 1), cam_dev.bit_length() - 1) == row
    solved = solve(lower_ref, jnp.where(unit, 1.0, 0.0))
    columns = [solved[:, c * cam_dev : (c + 1) * cam_dev] for c in range(9)]
    inverse_ref[...] = jnp.concatenate(
        [column[:8] for column in columns] + [columns[8][:8], columns[8][8:], jnp.zeros((8, cam_dev), F32)],
        axis=0,
    )


def cholesky(cells_ref, lower_ref):
    cam_dev = cells_ref.shape[1]
    zero = jnp.zeros((7, cam_dev), F32)
    block = cells_ref[...]
    columns = [
        jnp.concatenate([block[8 * r : 8 * r + 8], block[64 + r : 65 + r], zero], axis=0) for r in range(8)
    ]
    columns.append(jnp.concatenate([block[64:72], block[80:81], zero], axis=0))
    row = iota((16, cam_dev), 0)
    for c in range(9):
        pivot = columns[c][c : c + 1]
        root = jnp.sqrt(pivot)
        inverse = 1.0 / root
        column = jnp.where(row > c, columns[c] * inverse, 0.0)
        for r in range(c + 1, 9):
            columns[r] = columns[r] - column * column[r : r + 1]
        lower_ref[c] = jnp.where(row == 9, inverse, jnp.where(row < 9, column, 0.0))


def solve(lower_ref, vector):
    row = iota(vector.shape, 0)
    rest = vector
    copies = vector.shape[1] // lower_ref.shape[2]
    columns = [jnp.concatenate([lower_ref[c]] * copies, axis=1) for c in range(9)]
    for c in range(9):
        column = columns[c]
        value = rest[c : c + 1] * column[9:10]
        rest = jnp.where(row == c, value, rest - jnp.where(row < 9, column, 0.0) * value)
    for c in reversed(range(9)):
        column = columns[c]
        if c < 8:
            dotted = jnp.sum(
                jnp.where(jnp.logical_and(row > c, row < 9), column * rest, 0.0), axis=0, keepdims=True
            )
        else:
            dotted = jnp.zeros((1, vector.shape[1]), F32)
        value = (rest[c : c + 1] - dotted) * column[9:10]
        rest = jnp.where(row == c, value, rest)
    return rest


def multiply(pairs):
    cam_dev = pairs[0][1].shape[1]
    sums = [jnp.zeros((8, cam_dev), F32) for _ in range(9)]
    side = jnp.zeros((8, cam_dev), F32)
    corner = jnp.zeros((1, cam_dev), F32)
    for cell_ref, vector in pairs:
        first, last = vector[0:8], vector[8:9]
        for r in range(9):
            sums[r] = sums[r] + cell_ref[8 * r : 8 * r + 8, :] * first
        side = side + cell_ref[72:80, :] * last
        corner = corner + cell_ref[80:81, :] * last
    sums = [jnp.sum(part, axis=0, keepdims=True) for part in sums]
    top = jnp.concatenate(sums[:8], axis=0) + side
    return jnp.concatenate([top, sums[8] + corner, jnp.zeros((7, cam_dev), F32)], axis=0)


def total_of(values):
    return jnp.sum(jnp.sum(values, axis=1, keepdims=True), axis=0, keepdims=True)


FIRST = 8


def chosen(values, cameras):
    width = values.shape[1]
    return jnp.concatenate(
        [
            jnp.take_along_axis(values, cameras[:, at : at + width], axis=1, mode="promise_in_bounds")
            for at in range(0, cameras.shape[1], width)
        ],
        axis=1,
    )


def spread(row):
    return jnp.broadcast_to(row, (8, row.shape[1]))


def message(firsts, ninths):
    return jnp.concatenate(firsts[:FIRST] + ninths[:1] + firsts[FIRST:] + ninths[1:], axis=0)


def camera_rows(vector, choice_ref, order):
    cameras = [choice_ref[at : at + 1, :] for at in order]
    firsts = [chosen(vector[:8], spread(row)) for row in cameras]
    last = spread(vector[8:9])
    blank = jnp.zeros_like(cameras[0])
    ninths = [
        chosen(last, jnp.concatenate(cameras[:FIRST], axis=0)),
        chosen(last, jnp.concatenate(cameras[FIRST:] + [blank, blank], axis=0)),
    ]
    return message(firsts, ninths)


def coupled(vector, second, choice_ref, count_ref):
    texts = [camera_rows(vector, choice_ref, range(16 * h, 16 * h + GROUP)) for h in range(ROWS)]
    if second is not None:
        others = camera_rows(second, choice_ref, range(GROUP - 1, -1, -1))
        lane = iota(others.shape, 0)
        low = jnp.where(lane < 64, lax.shift_right_logical(lane, 3), lane - 64)
        high = FIRST + jnp.where(lane < 120, lax.shift_right_logical(lane - 72, 3), lane - 120)
        place = GROUP * (ROWS - 1) + jnp.where(lane < 72, low, high)
        texts[-1] = jnp.where(place.astype(F32) >= count_ref[0:1, :], others, texts[-1])
    return texts


def observed(one, two, wanted_ref):
    even = iota((8, one.shape[1]), 0) & 1
    last = jnp.where(even == 0, spread(one[8:9]), spread(two[8:9]))
    blank = jnp.zeros((1, wanted_ref.shape[1]), jnp.int32)
    texts = []
    for h in range(PAIR_ROWS):
        slots = [PAIRS * h + g for g in range(PAIRS)]
        cameras = [wanted_ref[slot : slot + 1, :] if slot < OBS_CAP else blank for slot in slots]
        firsts = [chosen(vector[:8], spread(row)) for row in cameras for vector in (one, two)]
        double = [row for row in cameras for _ in range(2)] + [blank, blank]
        ninths = [chosen(last, jnp.concatenate(double[at : at + 8], axis=0)) for at in (0, 8)]
        texts.append(message(firsts, ninths))
    return texts


def send_rows(send_ref, texts, scalars):
    rows = len(texts)
    devices = send_ref.shape[0] // rows
    for h, text in enumerate(texts):
        lane = iota(text.shape, 0)
        for index, scalar in enumerate(scalars[2 * h : 2 * h + 2]):
            text = jnp.where(lane == 126 + index, scalar, text)
        send_ref[pl.ds(h, devices, stride=rows), :] = text.T


def read_rows(got_ref, rows, sources):
    devices = got_ref.shape[0] // rows
    turned = [got_ref[pl.ds(h, devices, stride=rows), :].T for h in range(rows)]
    mark = one_hot(iota((devices, sources.shape[1]), 0).astype(F32) == sources)
    split = jnp.concatenate([piece for plane in turned for piece in pieces(plane)], axis=0)
    taken = dot_nn(split, mark)
    taken = [
        taken[at : at + 128] + taken[at + 128 : at + 256] + taken[at + 256 : at + 384]
        for at in range(0, 384 * rows, 384)
    ]
    sums = [jnp.sum(plane[126 + i : 127 + i], axis=1, keepdims=True) for plane in turned for i in range(2)]
    return taken, sums


def pick(taken, groups):
    top = jnp.zeros((8, taken.shape[1]), F32)
    for g in range(GROUP):
        at = 8 * g if g < FIRST else 8 * g + 8
        top = jnp.where(groups == float(g), taken[at : at + 8], top)
    row = iota((8, taken.shape[1]), 0).astype(F32)
    ninth = jnp.where(row == groups, taken[64:72], jnp.where(row + FIRST == groups, taken[120:128], 0.0))
    ninth = jnp.sum(ninth, axis=0, keepdims=True)
    return jnp.concatenate([top, ninth, jnp.zeros((7, taken.shape[1]), F32)], axis=0)


def step_kernel(
    index, got_ref, source_ref, place_ref, second_ref, choice_ref, count_ref, cells_ref, diagonal_ref, inverse_ref,
    state_ref, far_ref, state_out, far_out, send_ref,
):
    (upper, lower), sums = read_rows(got_ref, ROWS, source_ref[...])
    place = place_ref[...]
    part = quotient(place, GROUP)
    arrived = pick(jnp.where(part == 0, upper, lower), place - part * GROUP)
    step, rest, scaled, direction = (state_ref[i] for i in range(4))
    if index:
        image, image_scaled = state_ref[4], state_ref[5]
        energy, cross, square, old = sums
        alpha = old / energy
        beta = (old - 2.0 * alpha * cross + alpha * alpha * square) / old
        step = step + alpha * direction
        rest = rest - alpha * image
        direction = (scaled - alpha * image_scaled) + beta * direction
        far_before = far_ref[1]
        if index >= 2:
            second = second_ref[...]
            far_before = jnp.where(second >= 0, pick(lower, second - GROUP), far_before)
        far_scaled = far_before - alpha * arrived
        far = far_scaled + beta * far_ref[0]
    else:
        far_scaled = arrived
        far = arrived
    cam_dev = cells_ref.shape[2]
    image = multiply(
        [(diagonal_ref, direction)]
        + [(cells_ref.at[k], far[:, k * cam_dev : (k + 1) * cam_dev]) for k in range(NBR)]
    )
    energy = total_of(direction * image)
    scaled = multiply([(inverse_ref, rest)]) if index else scaled
    old = total_of(rest * scaled)
    state_out[0] = step
    state_out[1] = rest
    state_out[2] = scaled
    state_out[3] = direction
    state_out[4] = image
    state_out[6] = state_ref[6] if index else jnp.zeros_like(step) + sums[0]
    far_out[0] = far
    far_out[1] = far_scaled
    if index == ITERS - 1:
        state_out[5] = jnp.zeros_like(image)
        send_rows(send_ref, observed(step, direction, choice_ref), [energy, old])
        return
    image_scaled = multiply([(inverse_ref, image)])
    state_out[5] = image_scaled
    scalars = [energy, total_of(scaled * image), total_of(image * image_scaled), old]
    second = scaled if index + 1 >= 2 else None
    send_rows(send_ref, coupled(image_scaled, second, choice_ref, count_ref), scalars)


def finish_kernel(
    got_ref, place_ref, state_ref, jc_ref, jp_ref, rs_ref, vi_ref, used_ref, step_ref, rest_ref, point_ref
):
    npts = used_ref.shape[1]
    places = jnp.concatenate([place_ref[a : a + 1, :] for a in range(TRACK)], axis=1)
    within = jnp.concatenate([place_ref[TRACK + a : TRACK + a + 1, :] for a in range(TRACK)], axis=1)
    taken, sums = read_rows(got_ref, PAIR_ROWS, places)
    energy, old = sums[:2]
    alpha = old / energy
    step_ref[...] = (state_ref[0] + alpha * state_ref[3])[:9]
    rest_ref[...] = (state_ref[1] - alpha * state_ref[4])[:9]
    part = quotient(within, PAIRS)
    taken = jnp.where(part == 0, taken[0], jnp.where(part == 1, taken[1], taken[2]))
    groups = 2.0 * (within - part * PAIRS)
    moved = pick(taken, groups) + alpha * pick(taken, groups + 1.0)
    reduced = [jnp.zeros((1, npts), F32) for _ in range(3)]
    for a in range(TRACK):
        live = used_ref[a : a + 1, :].astype(F32)
        there = moved[:9, a * npts : (a + 1) * npts]
        jacobian = lines(jc_ref, a, 0, 18, npts)
        gradient = lines(jp_ref, a, 0, 6, npts)
        for u in range(2):
            change = jnp.sum(jacobian[9 * u : 9 * u + 9] * there, axis=0, keepdims=True)
            change = live * (change + rs_ref[a, u : u + 1, :])
            for x in range(3):
                reduced[x] = reduced[x] - gradient[3 * u + x : 3 * u + x + 1] * change
    for x in range(3):
        point_ref[x : x + 1, :] = sum(
            vi_ref[3 * x + y : 3 * x + y + 1, :] * reduced[y] for y in range(3)
        )


def factor_blocks(matrix):
    lower = {}
    for row_idx in range(9):
        for col_idx in range(row_idx + 1):
            accum = matrix[row_idx, col_idx]
            for inner_idx in range(col_idx):
                accum = accum - lower[row_idx, inner_idx] * lower[col_idx, inner_idx]
            if row_idx == col_idx:
                lower[row_idx, row_idx] = jnp.sqrt(accum)
            else:
                lower[row_idx, col_idx] = accum / lower[col_idx, col_idx]
    return lower


def solve_blocks(lower, vector):
    forward = []
    for row_idx in range(9):
        accum = vector[row_idx]
        for inner_idx in range(row_idx):
            accum = accum - lower[row_idx, inner_idx] * forward[inner_idx]
        forward.append(accum / lower[row_idx, row_idx])
    backward = [None] * 9
    for row_idx in reversed(range(9)):
        accum = forward[row_idx]
        for inner_idx in range(row_idx + 1, 9):
            accum = accum - lower[inner_idx, row_idx] * backward[inner_idx]
        backward[row_idx] = accum / lower[row_idx, row_idx]
    return jnp.stack(backward)


def whole_exchange(cells, diagonal, pattern, jacobian_cam, jacobian_pt, residuals, point_inverse, obs_camera, used):
    cam_dev = pattern.shape[1]
    cells = jnp.concatenate([cells, diagonal[None]], axis=0)
    main = cells[:, :64].reshape(NBR + 1, 8, 8, cam_dev)
    side = cells[:, 72:80].reshape(NBR + 1, 8, 1, cam_dev)
    foot = jnp.concatenate([cells[:, 64:72], cells[:, 80:81]], axis=1)[:, None]
    blocks = jnp.concatenate([jnp.concatenate([main, side], axis=2), foot], axis=1)
    gradient = jnp.concatenate([cells[NBR, 88:96], cells[NBR, 81:82]], axis=0)
    lower = factor_blocks(blocks[NBR])

    def gathered(vector):
        return lax.all_gather(vector, BOTH, axis=1, tiled=True)

    def summed(values):
        return lax.psum(jnp.sum(values), BOTH)

    step = jnp.zeros_like(gradient)
    rest = gradient
    scaled = solve_blocks(lower, rest)
    direction = scaled
    energy_now = summed(rest * scaled)
    for _ in range(ITERS):
        taken = jnp.concatenate([gathered(direction)[:, pattern], direction[:, None, :]], axis=1)
        image = jnp.sum(blocks * jnp.swapaxes(taken, 0, 1)[:, None], axis=(0, 2))
        alpha = energy_now / summed(direction * image)
        step = step + alpha * direction
        rest = rest - alpha * image
        scaled = solve_blocks(lower, rest)
        energy_next = summed(rest * scaled)
        direction = scaled + energy_next / energy_now * direction
        energy_now = energy_next
    whole = gathered(step)
    npts = obs_camera.shape[1]
    rows = jacobian_cam.reshape(TRACK, 2, 9, npts)
    seen = jnp.swapaxes(whole[:, obs_camera], 0, 1)
    change = jnp.sum(rows * seen[:, None], axis=2) + residuals
    change = change * used.astype(F32)[:, None]
    reduced = -jnp.sum(jacobian_pt.reshape(TRACK, 2, 3, npts) * change[:, :, None], axis=(0, 1))
    point_step = jnp.sum(point_inverse.reshape(3, 3, npts) * reduced[None], axis=1)
    return step, rest, point_step


def shape(*dims, dtype=F32):
    return jax.ShapeDtypeStruct(dims, dtype)


def call(kernel, outs, name, scratch=(), flops=0):
    cost = pl.CostEstimate(flops=flops, bytes_accessed=1 << 20, transcendentals=0) if flops else None
    return pl.pallas_call(
        kernel, out_shape=outs, name=name, compiler_params=PARAMS, scratch_shapes=list(scratch),
        cost_estimate=cost,
    )


def exchange(message, devices):
    width = message.shape[0] // devices
    arrived = lax.all_to_all(
        message.reshape(devices, width, 1, 128), BOTH, split_axis=0, concat_axis=0, tiled=True
    )
    return arrived.reshape(devices * width, 128)


def per_device(
    jacobian_cam, jacobian_pt, residuals, point_inverse, obs_camera, pair_slot, observation_used, pattern,
):
    devices = lax.axis_size("cam") * lax.axis_size("pt")
    npts = obs_camera.shape[1]
    cam_dev = pattern.shape[1]
    shift = cam_dev.bit_length() - 1
    couplings = NBR * cam_dev

    cameras = flat(jacobian_cam)
    points = flat(jacobian_pt)

    packed, places, rank = call(
        functools.partial(pack_kernel, devices, shift),
        (
            shape(devices * 10, 128), shape(2 * TRACK, npts), shape(devices, cam_dev),
        ),
        "pack",
        [pltpu.VMEM((80, TRACK * npts), F32)],
    )(cameras, points, residuals, point_inverse, obs_camera, pair_slot, observation_used, pattern)
    got = exchange(packed, devices)
    sources, far_rank, far_back, choice, count = call(
        functools.partial(place_kernel, devices, shift),
        (
            shape(1, couplings),
            shape(1, couplings),
            shape(1, couplings),
            shape(16 * ROWS, devices, dtype=jnp.int32),
            shape(2, devices),
        ),
        "place",
        flops=4 * 10**9,
    )(pattern, rank)
    text, diagonal, lower, state, message = call(
        diagonal_kernel,
        (
            shape(OBS_CAP // 2, 32, 2 * devices),
            shape(CELL, cam_dev),
            shape(9, 16, cam_dev),
            shape(7, 16, cam_dev),
            shape(devices * ROWS, 128),
        ),
        "diagonal",
    )(got, choice, count)
    cells, wanted, inverse = call(
        coupling_kernel,
        (shape(NBR, CELL, cam_dev), shape(OBS_CAP, devices, dtype=jnp.int32), shape(CELL, cam_dev)),
        "coupling",
        [pltpu.VMEM((16, cam_dev), F32), pltpu.VMEM((OBS_CAP // 2, 48, 2 * devices), F32)],
        flops=8 * 10**9,
    )(got, text, lower)
    far = jnp.zeros((2, 16, couplings), F32)
    crowded = None
    for index in range(ITERS):
        last = index == ITERS - 1
        rows = PAIR_ROWS if last else ROWS
        arrived = exchange(message, devices)
        state, far, message = call(
            functools.partial(step_kernel, index),
            (shape(7, 16, cam_dev), shape(2, 16, couplings), shape(devices * rows, 128)),
            "step",
        )(
            arrived, sources, far_rank, far_back, wanted if last else choice, count, cells, diagonal, inverse,
            state, far,
        )
        if index == 0:
            crowded = state[6, 0, 0] > 0.0
    arrived = exchange(message, devices)
    found = call(
        finish_kernel, (shape(9, cam_dev), shape(9, cam_dev), shape(3, npts)), "finish"
    )(arrived, places, state, cameras, points, residuals, point_inverse, observation_used)

    def dense():
        return whole_exchange(
            cells, diagonal, pattern, jacobian_cam, jacobian_pt, residuals, point_inverse, obs_camera, observation_used
        )

    return lax.cond(crowded, dense, lambda: tuple(found))


def solution(mesh):
    return jax.shard_map(
        per_device,
        mesh=mesh,
        in_specs=(
            P(None, None, BOTH),
            P(None, None, BOTH),
            P(None, None, BOTH),
            P(None, BOTH),
            P(None, BOTH),
            P(None, None, BOTH),
            P(None, BOTH),
            P(None, BOTH),
        ),
        out_specs=(P(None, BOTH), P(None, BOTH), P(None, BOTH)),
        check_vma=False,
    )
```

```python
import functools

import jax
import jax.numpy as jnp
from jax import lax
from jax.experimental import pallas as pl
from jax.experimental.pallas import tpu as pltpu
from jax.sharding import PartitionSpec as P

TRACK = 4
NBR = 12
ITERS = 4
OBS_CAP = 16
DAMPING = 1.0
BOTH = ("cam", "pt")

GROUP = 14
PAIRS = 7
ROWS = 2
SLOTS = GROUP * ROWS
CARRIED = 32
PAIR_ROWS = 3
CELL = 96
F32 = jnp.float32
BF16 = jnp.bfloat16
PARAMS = pltpu.CompilerParams(vmem_limit_bytes=28 * 1024 * 1024)


def iota(shape, dim):
    return lax.broadcasted_iota(jnp.int32, shape, dim)


def quotient(values, divisor):
    return jnp.floor((values.astype(F32) + 0.5) * (1.0 / divisor))


def pieces(values):
    high = values.astype(BF16)
    rest = values - high.astype(F32)
    middle = rest.astype(BF16)
    low = (rest - middle.astype(F32)).astype(BF16)
    return high, middle, low


def dot_nn(left, right):
    return lax.dot_general(left, right, (((1,), (0,)), ((), ())), preferred_element_type=F32)


def dot_nt(left, right):
    return lax.dot_general(left, right, (((1,), (1,)), ((), ())), preferred_element_type=F32)


def one_hot(condition):
    return jnp.where(condition, 1.0, 0.0).astype(BF16)


def before(size):
    return one_hot(iota((size, size), 0) < iota((size, size), 1))


def flat(array):
    tracks, rows, npts = array.shape
    tiles = jnp.transpose(array, (1, 0, 2)).reshape(rows, tracks, npts // 128, 128)
    return jnp.transpose(tiles, (0, 2, 1, 3)).reshape(-1, 128)


def lines(ref, a, first, count, npts):
    tiles = npts // 128
    step = TRACK * tiles
    return jnp.concatenate(
        [ref[pl.ds(step * first + TRACK * t + a, count, stride=step), :] for t in range(tiles)], axis=1
    )


def pack_kernel(
    devices, shift, jc_ref, jp_ref, rs_ref, vi_ref, cam_ref, slot_ref, used_ref, pattern_ref,
    out_ref, place_ref, rank_ref, feat_ref,
):
    npts = cam_ref.shape[1]
    cam_dev = pattern_ref.shape[1]
    found = jnp.zeros((devices, cam_dev), F32)
    for k in range(NBR):
        target = lax.shift_right_logical(pattern_ref[k : k + 1, :], shift)
        found = jnp.where(iota((devices, cam_dev), 0) == target, 1.0, found)
    rank = dot_nn(found.astype(BF16), before(cam_dev))
    rank_ref[...] = jnp.where(found > 0, rank, -1.0e6)
    live = [used_ref[a : a + 1, :].astype(F32) for a in range(TRACK)]
    carry = jnp.zeros((devices, 1), F32)
    triangle = before(npts)
    hits = []
    withins = []
    for a in range(TRACK):
        owner = lax.shift_right_logical(cam_ref[a : a + 1, :], shift)
        hit = jnp.where(
            jnp.logical_and(iota((devices, npts), 0) == owner, live[a] > 0), 1.0, 0.0
        )
        hits.append(hit.astype(BF16))
        count = dot_nn(hits[a], triangle) + carry
        within = jnp.sum(hit * count, axis=0, keepdims=True)
        carry = carry + jnp.sum(hit, axis=1, keepdims=True)
        withins.append(within)
        place_ref[a : a + 1, :] = jnp.where(live[a] > 0, owner.astype(F32), -1.0)
        place_ref[TRACK + a : TRACK + a + 1, :] = within

    vi = [[vi_ref[3 * x + y : 3 * x + y + 1, :] for y in range(3)] for x in range(3)]
    jp = [
        [[gradient[3 * u + x : 3 * u + x + 1] for x in range(3)] for u in range(2)]
        for gradient in [lines(jp_ref, a, 0, 6, npts) for a in range(TRACK)]
    ]
    jc = [lines(jc_ref, a, 0, 18, npts) for a in range(TRACK)]
    res = [[rs_ref[a, u : u + 1, :] for u in range(2)] for a in range(TRACK)]
    grad = []
    for x in range(3):
        total = jnp.zeros((1, npts), F32)
        for a in range(TRACK):
            total = total - live[a] * (jp[a][0][x] * res[a][0] + jp[a][1][x] * res[a][1])
        grad.append(total)
    for a in range(TRACK):
        at = slice(a * npts, (a + 1) * npts)
        for u in range(2):
            feat_ref[8 * u : 8 * u + 8, at] = jc[a][9 * u : 9 * u + 8]
            feat_ref[64 + u : 65 + u, at] = jc[a][9 * u + 8 : 9 * u + 9]
        removed = [
            [live[a] * sum(jp[a][u][x] * vi[x][y] for x in range(3)) for y in range(3)]
            for u in range(2)
        ]

        def middle(b, u, v):
            return -live[b] * sum(removed[u][y] * jp[b][v][y] for y in range(3))

        partners = [b for b in range(TRACK) if b != a]
        for m, b in enumerate(partners):
            first = [jc[b][9 * v : 9 * v + 8] for v in range(2)]
            ninth = [jc[b][9 * v + 8 : 9 * v + 9] for v in range(2)]
            for u in range(2):
                row = 2 + 2 * m + u
                one, two = middle(b, u, 0), middle(b, u, 1)
                feat_ref[8 * row : 8 * row + 8, at] = one * first[0] + two * first[1]
                feat_ref[64 + row : 65 + row, at] = one * ninth[0] + two * ninth[1]
        feat_ref[72:73, at] = live[a] + middle(a, 0, 0)
        feat_ref[73:74, at] = middle(a, 0, 1)
        feat_ref[74:75, at] = live[a] + middle(a, 1, 1)
        for u in range(2):
            right = -(live[a] * res[a][u] + sum(removed[u][y] * grad[y] for y in range(3)))
            feat_ref[75 + u : 76 + u, at] = right
        own = cam_ref[a : a + 1, :] & (cam_dev - 1)
        for m, b in enumerate(partners):
            label = slot_ref[a, b : b + 1, :] * cam_dev + own
            feat_ref[77 + m : 78 + m, at] = label.astype(F32)

    owners = jnp.concatenate(hits, axis=1)
    place = jnp.concatenate(withins, axis=1)
    split = pieces(feat_ref[...])
    masks = [
        one_hot(jnp.broadcast_to(place, (16, TRACK * npts)) == float(s)) for s in range(OBS_CAP)
    ]
    for g in range(5):
        right = jnp.concatenate(
            [
                part[16 * g : 16 * g + 16] * masks[8 * h + c]
                for h in range(2) for part in split for c in range(8)
            ],
            axis=0,
        )
        sums = dot_nt(owners, right)
        for h in range(2):
            mine = sums[:, 384 * h : 384 * h + 384]
            out_ref[pl.ds(2 * g + h, devices, stride=10), :] = (
                mine[:, :128] + mine[:, 128:256] + mine[:, 256:]
            )


def place_kernel(devices, shift, pattern_ref, rank_ref, source_ref, far_ref, back_ref, choice_ref, count_ref):
    cam_dev = pattern_ref.shape[1]
    turned = rank_ref[...].T
    camera = iota(turned.shape, 0).astype(F32)
    for h in range(ROWS):
        for g in range(16):
            here = jnp.where(turned == float(GROUP * h + g), camera, 0.0)
            choice_ref[16 * h + g : 16 * h + g + 1, :] = jnp.sum(here, axis=0, keepdims=True).astype(jnp.int32)
    most = jnp.sum(jnp.where(turned >= 0, 1.0, 0.0), axis=0, keepdims=True)
    carried = total_of(jnp.maximum(2.0 * most - SLOTS, 0.0))
    full = jnp.max(most, axis=1, keepdims=True)
    crowded = jnp.where(jnp.logical_or(full > float(SLOTS), carried > float(CARRIED)), 1.0, 0.0)
    count_ref[0:1, :] = most
    count_ref[1:2, :] = jnp.zeros_like(most) + crowded
    count = jnp.zeros((devices, cam_dev), F32)
    sources = []
    withins = []
    for k in range(NBR):
        camera = pattern_ref[k : k + 1, :]
        source = lax.shift_right_logical(camera, shift)
        within = camera & (cam_dev - 1)
        sources.append(iota((devices, cam_dev), 0) == source)
        withins.append(iota((cam_dev, cam_dev), 0) == within)
        count = count + dot_nt(one_hot(sources[k]), one_hot(withins[k]))
        source_ref[:, k * cam_dev : (k + 1) * cam_dev] = source.astype(F32)
    found = one_hot(count > 0)
    rank = dot_nn(found, before(cam_dev))
    most = jnp.sum(found.astype(F32), axis=1, keepdims=True)
    turned = rank.T.astype(BF16)
    for k in range(NBR):
        column = dot_nn(turned, one_hot(sources[k]))
        mine = jnp.sum(jnp.where(withins[k], column, 0.0), axis=0, keepdims=True)
        far_ref[:, k * cam_dev : (k + 1) * cam_dev] = mine
        full = jnp.sum(jnp.where(sources[k], most, 0.0), axis=0, keepdims=True)
        back = SLOTS - 1.0 - mine
        back_ref[:, k * cam_dev : (k + 1) * cam_dev] = jnp.where(back >= full, back, -1.0)


def outer(left, right):
    blocks = []
    for r in range(8):
        blocks.append(left[0][0][r : r + 1] * right[0][0] + left[1][0][r : r + 1] * right[1][0])
    blocks.append(left[0][1] * right[0][0] + left[1][1] * right[1][0])
    blocks.append(left[0][0] * right[0][1] + left[1][0] * right[1][1])
    return blocks, left[0][1] * right[0][1] + left[1][1] * right[1][1]


def turn(got_ref, text_ref, parts):
    devices = got_ref.shape[0] // 10
    for h in range(2):
        for row, g in enumerate(parts):
            turned = got_ref[pl.ds(2 * g + h, devices, stride=10), :].T
            for c in range(8):
                at = slice((c % 2) * devices, (c % 2 + 1) * devices)
                text_ref[4 * h + c // 2, 16 * row : 16 * row + 16, at] = turned[16 * c : 16 * c + 16]


def observation(text, cam_dev):
    own = [(text[8 * u : 8 * u + 8], text[16 + u : 17 + u]) for u in range(2)]
    cells = [quotient(text[29 + m : 30 + m], cam_dev) for m in range(3)]
    within = text[29:30] - cells[0] * cam_dev
    hit = one_hot(iota((cam_dev, text.shape[1]), 0).astype(F32) == within)
    return own, cells, hit


def folded(sums):
    size = sums.shape[0] // 3
    return sums[:size] + sums[size : 2 * size] + sums[2 * size :]


def diagonal_kernel(
    got_ref, choice_ref, count_ref, text_ref, out_ref, lower_ref, state_ref, send_ref
):
    cam_dev = out_ref.shape[1]
    turn(got_ref, text_ref, (0, 4))
    unit = iota((CELL, cam_dev), 0)
    unit = jnp.logical_and(unit <= 63, unit == 9 * lax.shift_right_logical(unit, 3)) | (unit == 80)
    total = jnp.where(unit, DAMPING, 0.0)
    for index in range(OBS_CAP // 2):
        text = text_ref[index]
        own, _, hit = observation(text, cam_dev)
        corner = [[text[24:25], text[25:26]], [text[25:26], text[26:27]]]
        weighted = [
            tuple(corner[u][0] * own[0][i] + corner[u][1] * own[1][i] for i in range(2)) for u in range(2)
        ]
        blocks, edge = outer(own, weighted)
        extra = [text[27:28], text[28:29]]
        ninth = own[0][1] * extra[0] + own[1][1] * extra[1]
        blocks.append(jnp.concatenate([edge, ninth, jnp.zeros((6, text.shape[1]), F32)], axis=0))
        blocks.append(own[0][0] * extra[0] + own[1][0] * extra[1])
        term = jnp.concatenate(blocks, axis=0)
        total = total + folded(dot_nt(jnp.concatenate(pieces(term), axis=0), hit))
    out_ref[...] = total
    cholesky(out_ref, lower_ref)
    right = jnp.concatenate([total[88:96], total[81:82], jnp.zeros((7, cam_dev), F32)], axis=0)
    scaled = solve(lower_ref, right)
    zero = jnp.zeros_like(right)
    state_ref[0] = zero
    state_ref[1] = right
    state_ref[2] = scaled
    state_ref[3] = scaled
    for index in range(4, 7):
        state_ref[index] = zero
    send_rows(send_ref, coupled(scaled, None, choice_ref, count_ref), [count_ref[1:2, :1]])


def coupling_kernel(got_ref, text_ref, lower_ref, out_ref, wanted_ref, inverse_ref, edge_ref, more_ref):
    cam_dev = out_ref.shape[2]
    devices = wanted_ref.shape[1]
    out_ref[...] = jnp.zeros_like(out_ref)
    edge_ref[...] = jnp.zeros_like(edge_ref)
    turn(got_ref, more_ref, (1, 2, 3))

    def step(index, _):
        text, more = text_ref[index], more_ref[index]
        own, cells, hit = observation(text, cam_dev)
        partners = [(more[8 * v : 8 * v + 8], text[18 + v : 19 + v]) for v in range(6)]
        terms, edges = [], jnp.zeros((16, hit.shape[1]), F32)
        row = iota(edges.shape, 0).astype(F32)
        for m in range(3):
            blocks, edge = outer(own, partners[2 * m : 2 * m + 2])
            terms.append(jnp.concatenate(pieces(jnp.concatenate(blocks, axis=0)), axis=0))
            edges = jnp.where(row == cells[m], edge, edges)
        for k in range(NBR):
            part = None
            for m in range(3):
                piece = terms[m] * one_hot(cells[m] == float(k))
                part = piece if part is None else part + piece
            out_ref[k, :80] = out_ref[k, :80] + folded(dot_nt(part, hit))
        edge_ref[...] = edge_ref[...] + folded(dot_nt(jnp.concatenate(pieces(edges), axis=0), hit))
        return 0

    lax.fori_loop(0, OBS_CAP // 2, step, 0, unroll=True)
    for k in range(NBR):
        out_ref[k, 80:81] = edge_ref[k : k + 1]
    for s in range(OBS_CAP):
        label = text_ref[s // 2, 29:30, (s % 2) * devices : (s % 2 + 1) * devices]
        wanted_ref[s : s + 1, :] = (label - cam_dev * quotient(label, cam_dev)).astype(jnp.int32)
    row = iota((16, 9 * cam_dev), 0)
    unit = lax.shift_right_logical(iota((16, 9 * cam_dev), 1), cam_dev.bit_length() - 1) == row
    solved = solve(lower_ref, jnp.where(unit, 1.0, 0.0))
    columns = [solved[:, c * cam_dev : (c + 1) * cam_dev] for c in range(9)]
    inverse_ref[...] = jnp.concatenate(
        [column[:8] for column in columns] + [columns[8][:8], columns[8][8:], jnp.zeros((8, cam_dev), F32)],
        axis=0,
    )


def cholesky(cells_ref, lower_ref):
    cam_dev = cells_ref.shape[1]
    zero = jnp.zeros((7, cam_dev), F32)
    block = cells_ref[...]
    columns = [
        jnp.concatenate([block[8 * r : 8 * r + 8], block[64 + r : 65 + r], zero], axis=0) for r in range(8)
    ]
    columns.append(jnp.concatenate([block[64:72], block[80:81], zero], axis=0))
    row = iota((16, cam_dev), 0)
    for c in range(9):
        pivot = columns[c][c : c + 1]
        root = jnp.sqrt(pivot)
        inverse = 1.0 / root
        column = jnp.where(row > c, columns[c] * inverse, 0.0)
        for r in range(c + 1, 9):
            columns[r] = columns[r] - column * column[r : r + 1]
        lower_ref[c] = jnp.where(row == 9, inverse, jnp.where(row < 9, column, 0.0))


def solve(lower_ref, vector):
    row = iota(vector.shape, 0)
    rest = vector
    copies = vector.shape[1] // lower_ref.shape[2]
    columns = [jnp.concatenate([lower_ref[c]] * copies, axis=1) for c in range(9)]
    for c in range(9):
        column = columns[c]
        value = rest[c : c + 1] * column[9:10]
        rest = jnp.where(row == c, value, rest - jnp.where(row < 9, column, 0.0) * value)
    for c in reversed(range(9)):
        column = columns[c]
        if c < 8:
            dotted = jnp.sum(
                jnp.where(jnp.logical_and(row > c, row < 9), column * rest, 0.0), axis=0, keepdims=True
            )
        else:
            dotted = jnp.zeros((1, vector.shape[1]), F32)
        value = (rest[c : c + 1] - dotted) * column[9:10]
        rest = jnp.where(row == c, value, rest)
    return rest


def multiply(pairs):
    cam_dev = pairs[0][1].shape[1]
    sums = [jnp.zeros((8, cam_dev), F32) for _ in range(9)]
    side = jnp.zeros((8, cam_dev), F32)
    corner = jnp.zeros((1, cam_dev), F32)
    for cell_ref, vector in pairs:
        first, last = vector[0:8], vector[8:9]
        for r in range(9):
            sums[r] = sums[r] + cell_ref[8 * r : 8 * r + 8, :] * first
        side = side + cell_ref[72:80, :] * last
        corner = corner + cell_ref[80:81, :] * last
    sums = [jnp.sum(part, axis=0, keepdims=True) for part in sums]
    top = jnp.concatenate(sums[:8], axis=0) + side
    return jnp.concatenate([top, sums[8] + corner, jnp.zeros((7, cam_dev), F32)], axis=0)


def total_of(values):
    return jnp.sum(jnp.sum(values, axis=1, keepdims=True), axis=0, keepdims=True)


FIRST = 8


def chosen(values, cameras):
    width = values.shape[1]
    return jnp.concatenate(
        [
            jnp.take_along_axis(values, cameras[:, at : at + width], axis=1, mode="promise_in_bounds")
            for at in range(0, cameras.shape[1], width)
        ],
        axis=1,
    )


def spread(row):
    return jnp.broadcast_to(row, (8, row.shape[1]))


def message(firsts, ninths):
    return jnp.concatenate(firsts[:FIRST] + ninths[:1] + firsts[FIRST:] + ninths[1:], axis=0)


def camera_rows(vector, choice_ref, order):
    cameras = [choice_ref[at : at + 1, :] for at in order]
    firsts = [chosen(vector[:8], spread(row)) for row in cameras]
    last = spread(vector[8:9])
    blank = jnp.zeros_like(cameras[0])
    ninths = [
        chosen(last, jnp.concatenate(cameras[:FIRST], axis=0)),
        chosen(last, jnp.concatenate(cameras[FIRST:] + [blank, blank], axis=0)),
    ]
    return message(firsts, ninths)


def coupled(vector, second, choice_ref, count_ref):
    texts = [camera_rows(vector, choice_ref, range(16 * h, 16 * h + GROUP)) for h in range(ROWS)]
    if second is not None:
        others = camera_rows(second, choice_ref, range(GROUP - 1, -1, -1))
        lane = iota(others.shape, 0)
        low = jnp.where(lane < 64, lax.shift_right_logical(lane, 3), lane - 64)
        high = FIRST + jnp.where(lane < 120, lax.shift_right_logical(lane - 72, 3), lane - 120)
        place = GROUP * (ROWS - 1) + jnp.where(lane < 72, low, high)
        texts[-1] = jnp.where(place.astype(F32) >= count_ref[0:1, :], others, texts[-1])
    return texts


def observed(one, two, wanted_ref):
    even = iota((8, one.shape[1]), 0) & 1
    last = jnp.where(even == 0, spread(one[8:9]), spread(two[8:9]))
    blank = jnp.zeros((1, wanted_ref.shape[1]), jnp.int32)
    texts = []
    for h in range(PAIR_ROWS):
        slots = [PAIRS * h + g for g in range(PAIRS)]
        cameras = [wanted_ref[slot : slot + 1, :] if slot < OBS_CAP else blank for slot in slots]
        firsts = [chosen(vector[:8], spread(row)) for row in cameras for vector in (one, two)]
        double = [row for row in cameras for _ in range(2)] + [blank, blank]
        ninths = [chosen(last, jnp.concatenate(double[at : at + 8], axis=0)) for at in (0, 8)]
        texts.append(message(firsts, ninths))
    return texts


def send_rows(send_ref, texts, scalars):
    rows = len(texts)
    devices = send_ref.shape[0] // rows
    for h, text in enumerate(texts):
        lane = iota(text.shape, 0)
        for index, scalar in enumerate(scalars[2 * h : 2 * h + 2]):
            text = jnp.where(lane == 126 + index, scalar, text)
        send_ref[pl.ds(h, devices, stride=rows), :] = text.T


def read_rows(got_ref, rows, sources):
    devices = got_ref.shape[0] // rows
    turned = [got_ref[pl.ds(h, devices, stride=rows), :].T for h in range(rows)]
    mark = one_hot(iota((devices, sources.shape[1]), 0).astype(F32) == sources)
    parts = turned[:2] + [jnp.concatenate([plane[0:32], plane[64:80]], axis=0) for plane in turned[2:]]
    split = jnp.concatenate([piece for part in parts for piece in pieces(part)], axis=0)
    sums = dot_nn(split, mark)
    taken, at = [], 0
    for part in parts:
        taken.append(folded(sums[at : at + 3 * part.shape[0]]))
        at += 3 * part.shape[0]
    sums = [jnp.sum(plane[126 + i : 127 + i], axis=1, keepdims=True) for plane in turned for i in range(2)]
    return taken, sums


def pick(taken, groups):
    top = jnp.zeros((8, taken.shape[1]), F32)
    for g in range(GROUP):
        at = 8 * g if g < FIRST else 8 * g + 8
        top = jnp.where(groups == float(g), taken[at : at + 8], top)
    row = iota((8, taken.shape[1]), 0).astype(F32)
    ninth = jnp.where(row == groups, taken[64:72], jnp.where(row + FIRST == groups, taken[120:128], 0.0))
    ninth = jnp.sum(ninth, axis=0, keepdims=True)
    return jnp.concatenate([top, ninth, jnp.zeros((7, taken.shape[1]), F32)], axis=0)


def step_kernel(
    index, got_ref, source_ref, place_ref, second_ref, choice_ref, count_ref, cells_ref, diagonal_ref, inverse_ref,
    state_ref, far_ref, state_out, far_out, send_ref,
):
    (upper, lower), sums = read_rows(got_ref, ROWS, source_ref[...])
    place = place_ref[...]
    part = quotient(place, GROUP)
    arrived = pick(jnp.where(part == 0, upper, lower), place - part * GROUP)
    step, rest, scaled, direction = (state_ref[i] for i in range(4))
    if index:
        image, image_scaled = state_ref[4], state_ref[5]
        energy, cross, square, old = sums
        alpha = old / energy
        beta = (old - 2.0 * alpha * cross + alpha * alpha * square) / old
        step = step + alpha * direction
        rest = rest - alpha * image
        direction = (scaled - alpha * image_scaled) + beta * direction
        far_before = far_ref[1]
        if index >= 2:
            second = second_ref[...]
            far_before = jnp.where(second >= 0, pick(lower, second - GROUP), far_before)
        far_scaled = far_before - alpha * arrived
        far = far_scaled + beta * far_ref[0]
    else:
        far_scaled = arrived
        far = arrived
    cam_dev = cells_ref.shape[2]
    image = multiply(
        [(diagonal_ref, direction)]
        + [(cells_ref.at[k], far[:, k * cam_dev : (k + 1) * cam_dev]) for k in range(NBR)]
    )
    energy = total_of(direction * image)
    scaled = multiply([(inverse_ref, rest)]) if index else scaled
    old = total_of(rest * scaled)
    state_out[0] = step
    state_out[1] = rest
    state_out[2] = scaled
    state_out[3] = direction
    state_out[4] = image
    state_out[6] = state_ref[6] if index else jnp.zeros_like(step) + sums[0]
    far_out[0] = far
    far_out[1] = far_scaled
    if index == ITERS - 1:
        state_out[5] = jnp.zeros_like(image)
        send_rows(send_ref, observed(step, direction, choice_ref), [energy, old])
        return
    image_scaled = multiply([(inverse_ref, image)])
    state_out[5] = image_scaled
    scalars = [energy, total_of(scaled * image), total_of(image * image_scaled), old]
    second = scaled if index + 1 >= 2 else None
    send_rows(send_ref, coupled(image_scaled, second, choice_ref, count_ref), scalars)


def finish_kernel(
    got_ref, place_ref, state_ref, jc_ref, jp_ref, rs_ref, vi_ref, used_ref, step_ref, rest_ref, point_ref
):
    npts = used_ref.shape[1]
    places = jnp.concatenate([place_ref[a : a + 1, :] for a in range(TRACK)], axis=1)
    within = jnp.concatenate([place_ref[TRACK + a : TRACK + a + 1, :] for a in range(TRACK)], axis=1)
    taken, sums = read_rows(got_ref, PAIR_ROWS, places)
    energy, old = sums[:2]
    alpha = old / energy
    step_ref[...] = (state_ref[0] + alpha * state_ref[3])[:9]
    rest_ref[...] = (state_ref[1] - alpha * state_ref[4])[:9]
    part = quotient(within, PAIRS)
    first = jnp.where(part == 0, taken[0], taken[1])
    third = part == 2
    taken = jnp.concatenate(
        [
            jnp.where(third, taken[2][:32], first[:32]),
            first[32:64],
            jnp.where(third, taken[2][32:], first[64:80]),
            first[80:],
        ],
        axis=0,
    )
    groups = 2.0 * (within - part * PAIRS)
    moved = pick(taken, groups) + alpha * pick(taken, groups + 1.0)
    reduced = [jnp.zeros((1, npts), F32) for _ in range(3)]
    for a in range(TRACK):
        live = used_ref[a : a + 1, :].astype(F32)
        there = moved[:9, a * npts : (a + 1) * npts]
        jacobian = lines(jc_ref, a, 0, 18, npts)
        gradient = lines(jp_ref, a, 0, 6, npts)
        for u in range(2):
            change = jnp.sum(jacobian[9 * u : 9 * u + 9] * there, axis=0, keepdims=True)
            change = live * (change + rs_ref[a, u : u + 1, :])
            for x in range(3):
                reduced[x] = reduced[x] - gradient[3 * u + x : 3 * u + x + 1] * change
    for x in range(3):
        point_ref[x : x + 1, :] = sum(
            vi_ref[3 * x + y : 3 * x + y + 1, :] * reduced[y] for y in range(3)
        )


def factor_blocks(matrix):
    lower = {}
    for row_idx in range(9):
        for col_idx in range(row_idx + 1):
            accum = matrix[row_idx, col_idx]
            for inner_idx in range(col_idx):
                accum = accum - lower[row_idx, inner_idx] * lower[col_idx, inner_idx]
            if row_idx == col_idx:
                lower[row_idx, row_idx] = jnp.sqrt(accum)
            else:
                lower[row_idx, col_idx] = accum / lower[col_idx, col_idx]
    return lower


def solve_blocks(lower, vector):
    forward = []
    for row_idx in range(9):
        accum = vector[row_idx]
        for inner_idx in range(row_idx):
            accum = accum - lower[row_idx, inner_idx] * forward[inner_idx]
        forward.append(accum / lower[row_idx, row_idx])
    backward = [None] * 9
    for row_idx in reversed(range(9)):
        accum = forward[row_idx]
        for inner_idx in range(row_idx + 1, 9):
            accum = accum - lower[inner_idx, row_idx] * backward[inner_idx]
        backward[row_idx] = accum / lower[row_idx, row_idx]
    return jnp.stack(backward)


def whole_exchange(cells, diagonal, pattern, jacobian_cam, jacobian_pt, residuals, point_inverse, obs_camera, used):
    cam_dev = pattern.shape[1]
    cells = jnp.concatenate([cells, diagonal[None]], axis=0)
    main = cells[:, :64].reshape(NBR + 1, 8, 8, cam_dev)
    side = cells[:, 72:80].reshape(NBR + 1, 8, 1, cam_dev)
    foot = jnp.concatenate([cells[:, 64:72], cells[:, 80:81]], axis=1)[:, None]
    blocks = jnp.concatenate([jnp.concatenate([main, side], axis=2), foot], axis=1)
    gradient = jnp.concatenate([cells[NBR, 88:96], cells[NBR, 81:82]], axis=0)
    lower = factor_blocks(blocks[NBR])

    def gathered(vector):
        return lax.all_gather(vector, BOTH, axis=1, tiled=True)

    def summed(values):
        return lax.psum(jnp.sum(values), BOTH)

    step = jnp.zeros_like(gradient)
    rest = gradient
    scaled = solve_blocks(lower, rest)
    direction = scaled
    energy_now = summed(rest * scaled)
    for _ in range(ITERS):
        taken = jnp.concatenate([gathered(direction)[:, pattern], direction[:, None, :]], axis=1)
        image = jnp.sum(blocks * jnp.swapaxes(taken, 0, 1)[:, None], axis=(0, 2))
        alpha = energy_now / summed(direction * image)
        step = step + alpha * direction
        rest = rest - alpha * image
        scaled = solve_blocks(lower, rest)
        energy_next = summed(rest * scaled)
        direction = scaled + energy_next / energy_now * direction
        energy_now = energy_next
    whole = gathered(step)
    npts = obs_camera.shape[1]
    rows = jacobian_cam.reshape(TRACK, 2, 9, npts)
    seen = jnp.swapaxes(whole[:, obs_camera], 0, 1)
    change = jnp.sum(rows * seen[:, None], axis=2) + residuals
    change = change * used.astype(F32)[:, None]
    reduced = -jnp.sum(jacobian_pt.reshape(TRACK, 2, 3, npts) * change[:, :, None], axis=(0, 1))
    point_step = jnp.sum(point_inverse.reshape(3, 3, npts) * reduced[None], axis=1)
    return step, rest, point_step


def shape(*dims, dtype=F32):
    return jax.ShapeDtypeStruct(dims, dtype)


def call(kernel, outs, name, scratch=(), flops=0):
    cost = pl.CostEstimate(flops=flops, bytes_accessed=1 << 20, transcendentals=0) if flops else None
    return pl.pallas_call(
        kernel, out_shape=outs, name=name, compiler_params=PARAMS, scratch_shapes=list(scratch),
        cost_estimate=cost,
    )


def exchange(message, devices):
    width = message.shape[0] // devices
    arrived = lax.all_to_all(
        message.reshape(devices, width, 1, 128), BOTH, split_axis=0, concat_axis=0, tiled=True
    )
    return arrived.reshape(devices * width, 128)


def per_device(
    jacobian_cam, jacobian_pt, residuals, point_inverse, obs_camera, pair_slot, observation_used, pattern,
):
    devices = lax.axis_size("cam") * lax.axis_size("pt")
    npts = obs_camera.shape[1]
    cam_dev = pattern.shape[1]
    shift = cam_dev.bit_length() - 1
    couplings = NBR * cam_dev

    cameras = flat(jacobian_cam)
    points = flat(jacobian_pt)

    packed, places, rank = call(
        functools.partial(pack_kernel, devices, shift),
        (
            shape(devices * 10, 128), shape(2 * TRACK, npts), shape(devices, cam_dev),
        ),
        "pack",
        [pltpu.VMEM((80, TRACK * npts), F32)],
    )(cameras, points, residuals, point_inverse, obs_camera, pair_slot, observation_used, pattern)
    got = exchange(packed, devices)
    sources, far_rank, far_back, choice, count = call(
        functools.partial(place_kernel, devices, shift),
        (
            shape(1, couplings),
            shape(1, couplings),
            shape(1, couplings),
            shape(16 * ROWS, devices, dtype=jnp.int32),
            shape(2, devices),
        ),
        "place",
        flops=4 * 10**9,
    )(pattern, rank)
    text, diagonal, lower, state, message = call(
        diagonal_kernel,
        (
            shape(OBS_CAP // 2, 32, 2 * devices),
            shape(CELL, cam_dev),
            shape(9, 16, cam_dev),
            shape(7, 16, cam_dev),
            shape(devices * ROWS, 128),
        ),
        "diagonal",
    )(got, choice, count)
    cells, wanted, inverse = call(
        coupling_kernel,
        (shape(NBR, CELL, cam_dev), shape(OBS_CAP, devices, dtype=jnp.int32), shape(CELL, cam_dev)),
        "coupling",
        [pltpu.VMEM((16, cam_dev), F32), pltpu.VMEM((OBS_CAP // 2, 48, 2 * devices), F32)],
        flops=8 * 10**9,
    )(got, text, lower)
    far = jnp.zeros((2, 16, couplings), F32)
    crowded = None
    for index in range(ITERS):
        last = index == ITERS - 1
        rows = PAIR_ROWS if last else ROWS
        arrived = exchange(message, devices)
        state, far, message = call(
            functools.partial(step_kernel, index),
            (shape(7, 16, cam_dev), shape(2, 16, couplings), shape(devices * rows, 128)),
            "step",
        )(
            arrived, sources, far_rank, far_back, wanted if last else choice, count, cells, diagonal, inverse,
            state, far,
        )
        if index == 0:
            crowded = state[6, 0, 0] > 0.0
    arrived = exchange(message, devices)
    found = call(
        finish_kernel, (shape(9, cam_dev), shape(9, cam_dev), shape(3, npts)), "finish"
    )(arrived, places, state, cameras, points, residuals, point_inverse, observation_used)

    def dense():
        return whole_exchange(
            cells, diagonal, pattern, jacobian_cam, jacobian_pt, residuals, point_inverse, obs_camera, observation_used
        )

    return lax.cond(crowded, dense, lambda: tuple(found))


def solution(mesh):
    return jax.shard_map(
        per_device,
        mesh=mesh,
        in_specs=(
            P(None, None, BOTH),
            P(None, None, BOTH),
            P(None, None, BOTH),
            P(None, BOTH),
            P(None, BOTH),
            P(None, None, BOTH),
            P(None, BOTH),
            P(None, BOTH),
        ),
        out_specs=(P(None, BOTH), P(None, BOTH), P(None, BOTH)),
        check_vma=False,
    )
```
